32 devices in a mesh: rows: 8 (over z, x), seq: 4 (over y, core).
Axes of the slice: x: 2, y: 2, z: 4, core: 2. Of those that a mesh axis runs over, the one named last changes fastest.
Arguments:
- target: bfloat16 [16, 1024, 512], P('rows', 'seq'), may hold values from -6 to 6
- memory: bfloat16 [16, 1024, 512], P('rows', 'seq'), may hold values from -6 to 6
- target_segments: int32 [16, 1024], P('rows'), may hold values from 0 to 7, as said below
- memory_segments: int32 [16, 1024], P('rows'), may hold values from 0 to 7, as said below
- self_query: bfloat16 [512, 512], replicated, may hold values from -0.25 to 0.25
- self_key: bfloat16 [512, 512], replicated, may hold values from -0.25 to 0.25
- self_value: bfloat16 [512, 512], replicated, may hold values from -0.25 to 0.25
- self_output: bfloat16 [512, 512], replicated, may hold values from -1.5 to 1.5
- cross_query: bfloat16 [512, 512], replicated, may hold values from -0.25 to 0.25
- cross_key: bfloat16 [512, 512], replicated, may hold values from -0.25 to 0.25
- cross_value: bfloat16 [512, 512], replicated, may hold values from -0.25 to 0.25
- cross_output: bfloat16 [512, 512], replicated, may hold values from -1.5 to 1.5
- ffn_in: bfloat16 [512, 2048], replicated, may hold values from -0.25 to 0.25
- ffn_out: bfloat16 [2048, 512], replicated, may hold values from -0.125 to 0.125
- omega_self: float32 [512], replicated, may hold values from 0.5 to 2
- omega_cross: float32 [512], replicated, may hold values from 0.5 to 2
- omega_ffn: float32 [512], replicated, may hold values from 0.5 to 2
- gain_self: float32 [512], replicated, may hold values from 0.5 to 1.5
- bias_self: float32 [512], replicated, may hold values from -2.5 to 2.5
- gain_cross: float32 [512], replicated, may hold values from 0.5 to 1.5
- bias_cross: float32 [512], replicated, may hold values from -2.5 to 2.5
- gain_ffn: float32 [512], replicated, may hold values from 0.5 to 1.5
- bias_ffn: float32 [512], replicated, may hold values from -2.5 to 2.5
- cotangent: bfloat16 [16, 1024, 512], P('rows', 'seq'), may hold values from -6 to 6
Outputs:
- output: bfloat16 [16, 1024, 512], P('rows', 'seq')
- target_grad: float32 [16, 1024, 512], P('rows', 'seq')
- memory_grad: float32 [16, 1024, 512], P('rows', 'seq')
- self_query_grad: float32 [512, 512], replicated
- self_key_grad: float32 [512, 512], replicated
- self_value_grad: float32 [512, 512], replicated
- self_output_grad: float32 [512, 512], replicated
- cross_query_grad: float32 [512, 512], replicated
- cross_key_grad: float32 [512, 512], replicated
- cross_value_grad: float32 [512, 512], replicated
- cross_output_grad: float32 [512, 512], replicated
- ffn_in_grad: float32 [512, 2048], replicated
- ffn_out_grad: float32 [2048, 512], replicated
- omega_self_grad: float32 [512], replicated
- omega_cross_grad: float32 [512], replicated
- omega_ffn_grad: float32 [512], replicated
- gain_self_grad: float32 [512], replicated
- bias_self_grad: float32 [512], replicated
- gain_cross_grad: float32 [512], replicated
- bias_cross_grad: float32 [512], replicated
- gain_ffn_grad: float32 [512], replicated
- bias_ffn_grad: float32 [512], replicated
The draws below stay inside these ranges and needn't reach their ends.
Inputs may be any that keep to these rules, and one draw needn't show every extreme that they name: `target_segments`: along each row the ids start at 0 and never fall. In each aligned block of 2 rows one row, drawn from the seed, is a single document; every other row holds exactly 8 documents of one or more positions. `memory_segments`: along each row the ids start at 0 and never fall, and a row holds exactly the document ids of the same row of target_segments, each at one or more positions.
All inputs are finite; a program needn't handle non-finite values.
Results may differ from the reference program's by a relative error of at most 0.034.
Values may be sent and summed in bfloat16 or wider, within the bound.
A program may use at most 256 MiB of HBM per device.

```python
import math
import jax
import jax.numpy as jnp
from jax import lax

D = 512
HEADS = 8
FF = 2048
ROWS_DEV = 2
SEGMENTS = 8
BATCH = 16
LENGTH = 1024
MEMORY = 1024


def single_rows(key):
    chosen = jax.random.randint(jax.random.fold_in(key, 5), (BATCH // ROWS_DEV,), 0, ROWS_DEV)
    row_index = jnp.arange(BATCH)
    return row_index % ROWS_DEV == chosen[row_index // ROWS_DEV]


def packed_labels(key, single, length):
    row_keys = jax.random.split(key, BATCH)
    starts = jax.vmap(lambda row_key: jax.random.permutation(row_key, length - 1)[:SEGMENTS - 1])(row_keys) + 1
    places = jnp.arange(length)
    labels = jnp.sum((places[None, None, :] >= starts[:, :, None]).astype(jnp.int32), axis=1)
    return jnp.where(single[:, None], 0, labels).astype(jnp.int32)


def draw_target_segments(key, part):
    single = single_rows(key)
    key = jax.random.fold_in(key, 17)
    return packed_labels(key, single, LENGTH)


def draw_memory_segments(key, part):
    single = single_rows(key)
    key = jax.random.fold_in(key, 29)
    return packed_labels(key, single, MEMORY)


def level_of(own_key, dims, cuts, least, high):
    def one(position, blocks):
        draws = jax.random.uniform(jax.random.fold_in(jax.random.fold_in(own_key, 6), position), (blocks,), jnp.float32, least / len(cuts), high / len(cuts))
        return jnp.repeat(jnp.exp(draws), dims[position] // blocks).reshape((-1,) + (1,) * (len(dims) - position - 1))

    factor_of = one(*cuts[0])
    for cut in cuts[1:]:
        factor_of = factor_of * one(*cut)
    return factor_of


def gaussian(key, dims, scale, limit, pieces=(), kind=jnp.bfloat16):
    entries = scale * jax.random.normal(key, dims, jnp.float32)
    if pieces:
        entries = entries * level_of(key, dims, pieces, -0.22, 0.18)
    return jnp.clip(entries, -limit, limit).astype(kind)


def setup_inputs(seed: int = 0) -> dict:
    key_of = jax.random.split(jax.random.key(seed), 25)
    return {
        "target": gaussian(key_of[0], (BATCH, LENGTH, D), 1.0, 6.0, ((0, 8), (1, 4))),
        "memory": gaussian(key_of[1], (BATCH, MEMORY, D), 1.0, 6.0, ((0, 8), (1, 4))),
        "target_segments": draw_target_segments(jax.random.fold_in(key_of[24], 71), 0),
        "memory_segments": draw_memory_segments(jax.random.fold_in(key_of[24], 71), 0),
        "self_query": gaussian(key_of[4], (D, D), D ** -0.5, 0.25),
        "self_key": gaussian(key_of[5], (D, D), D ** -0.5, 0.25),
        "self_value": gaussian(key_of[6], (D, D), D ** -0.5, 0.25),
        "self_output": gaussian(key_of[7], (D, D), (D // 32) ** -0.5, 1.5),
        "cross_query": gaussian(key_of[8], (D, D), D ** -0.5, 0.25),
        "cross_key": gaussian(key_of[9], (D, D), D ** -0.5, 0.25),
        "cross_value": gaussian(key_of[10], (D, D), D ** -0.5, 0.25),
        "cross_output": gaussian(key_of[11], (D, D), (D // 32) ** -0.5, 1.5),
        "ffn_in": gaussian(key_of[12], (D, FF), D ** -0.5, 0.25),
        "ffn_out": gaussian(key_of[13], (FF, D), FF ** -0.5, 0.125),
        "omega_self": jnp.clip(jnp.exp(jax.random.uniform(key_of[14], (D,), jnp.float32, math.log(0.5), math.log(2.0))), 0.5, 2.0),
        "omega_cross": jnp.clip(jnp.exp(jax.random.uniform(key_of[15], (D,), jnp.float32, math.log(0.5), math.log(2.0))), 0.5, 2.0),
        "omega_ffn": jnp.clip(jnp.exp(jax.random.uniform(key_of[16], (D,), jnp.float32, math.log(0.5), math.log(2.0))), 0.5, 2.0),
        "gain_self": jnp.clip(1.0 + 0.1 * jax.random.normal(key_of[17], (D,), jnp.float32), 0.5, 1.5),
        "bias_self": gaussian(key_of[18], (D,), 0.3, 2.5, (), jnp.float32),
        "gain_cross": jnp.clip(1.0 + 0.1 * jax.random.normal(key_of[19], (D,), jnp.float32), 0.5, 1.5),
        "bias_cross": gaussian(key_of[20], (D,), 0.3, 2.5, (), jnp.float32),
        "gain_ffn": jnp.clip(1.0 + 0.1 * jax.random.normal(key_of[21], (D,), jnp.float32), 0.5, 1.5),
        "bias_ffn": gaussian(key_of[22], (D,), 0.3, 2.5, (), jnp.float32),
        "cotangent": gaussian(key_of[23], (BATCH, LENGTH, D), 1.0, 6.0, ((0, 8), (1, 4))),
    }


@jax.custom_vjp
def low(v):
    return lax.optimization_barrier(v.astype(jnp.bfloat16)).astype(jnp.float32)

@jax.custom_vjp
def low_back(v):
    return v

def low_keep(v):
    return (low(v), None)

def low_pass(kept, grad):
    return (grad,)

def back_keep(v):
    return (v, None)

def back_low(kept, grad):
    return (low(grad),)
low.defvjp(low_keep, low_pass)
low_back.defvjp(back_keep, back_low)

def round_both(value):
    return low_back(low(value))

def layer_norm(pre_norm, gain, bias):
    centred = pre_norm - lax.optimization_barrier(jnp.mean(pre_norm, axis=-1, keepdims=True))
    spread = lax.optimization_barrier(jnp.mean(centred * centred, axis=-1, keepdims=True))
    return centred * lax.rsqrt(spread + 1e-05) * gain + bias

def project(inputs, weight):
    return jnp.einsum('rsd,df->rsf', inputs, weight, precision=lax.Precision.HIGHEST)

def split_heads(values):
    return values.reshape(values.shape[0], values.shape[1], HEADS, -1)

def attend_rows(queries, keys, values, query_ids, key_ids, causal):
    length = queries.shape[0]
    block_rows = 512 if length % 512 == 0 else length
    block_count = length // block_rows
    key_place = jnp.arange(keys.shape[0])
    score_scale = 1.0 / math.sqrt(queries.shape[-1])

    @jax.checkpoint
    def one_block(inputs):
        query_block, id_block, offset = inputs
        raw = jnp.einsum('qhe,khe->hqk', query_block, keys, precision=lax.Precision.HIGHEST) * score_scale
        scores = low_back(raw)
        allowed = id_block[:, None] == key_ids[None, :]
        if causal:
            query_place = offset + jnp.arange(block_rows)
            allowed = allowed & (key_place[None, :] <= query_place[:, None])
        scores = jnp.where(allowed[None], scores, -1e+30)
        weights = jax.nn.softmax(scores, axis=-1)
        return jnp.einsum('hqk,khe->qhe', low(weights), values, precision=lax.Precision.HIGHEST)
    blocks = (queries.reshape(block_count, block_rows, queries.shape[1], queries.shape[2]), query_ids.reshape(block_count, block_rows), jnp.arange(block_count) * block_rows)
    result = lax.map(one_block, blocks)
    return result.reshape(queries.shape)

def attend_all(queries, keys, values, query_ids, key_ids, causal):

    def one_row(items):
        return attend_rows(items[0], items[1], items[2], items[3], items[4], causal)
    return lax.map(one_row, (queries, keys, values, query_ids, key_ids))

def forward(target_wide, memory_wide, target_segments, memory_segments, params):
    self_query, self_key, self_value, self_output, cross_query, cross_key, cross_value, cross_output, ffn_in, ffn_out, omega_self, omega_cross, omega_ffn, gain_self, bias_self, gain_cross, bias_cross, gain_ffn, bias_ffn = params
    queries = round_both(project(target_wide, self_query))
    keys_self = round_both(project(target_wide, self_key))
    values_self = round_both(project(target_wide, self_value))
    self_heads = attend_all(split_heads(queries), split_heads(keys_self), split_heads(values_self), target_segments, target_segments, True)
    self_out = round_both(self_heads.reshape(target_wide.shape))
    self_branch = low_back(project(self_out, self_output))
    hidden_one = layer_norm(target_wide * omega_self + self_branch, gain_self, bias_self)
    cross_queries = round_both(project(low(hidden_one), cross_query))
    cross_keys = round_both(project(memory_wide, cross_key))
    cross_values = round_both(project(memory_wide, cross_value))
    cross_heads = attend_all(split_heads(cross_queries), split_heads(cross_keys), split_heads(cross_values), target_segments, memory_segments, False)
    cross_out = round_both(cross_heads.reshape(target_wide.shape))
    cross_branch = low_back(project(cross_out, cross_output))
    hidden_two = layer_norm(hidden_one * omega_cross + cross_branch, gain_cross, bias_cross)
    upward = low_back(project(low(hidden_two), ffn_in))
    active = low(jax.nn.gelu(upward))
    ffn_branch = low_back(project(active, ffn_out))
    return layer_norm(hidden_two * omega_ffn + ffn_branch, gain_ffn, bias_ffn)

def reference(target, memory, target_segments, memory_segments, self_query, self_key, self_value, self_output, cross_query, cross_key, cross_value, cross_output, ffn_in, ffn_out, omega_self, omega_cross, omega_ffn, gain_self, bias_self, gain_cross, bias_cross, gain_ffn, bias_ffn, cotangent):
    matrices = (self_query, self_key, self_value, self_output, cross_query, cross_key, cross_value, cross_output, ffn_in, ffn_out)
    vectors = (omega_self, omega_cross, omega_ffn, gain_self, bias_self, gain_cross, bias_cross, gain_ffn, bias_ffn)
    params = tuple((matrix_item.astype(jnp.float32) for matrix_item in matrices)) + tuple((vector_item.astype(jnp.float32) for vector_item in vectors))

    def run(target_wide, memory_wide, weights):
        return forward(target_wide, memory_wide, target_segments, memory_segments, weights)
    result, pullback = jax.vjp(run, target.astype(jnp.float32), memory.astype(jnp.float32), params)
    target_grad, memory_grad, grads = pullback(cotangent.astype(jnp.float32))
    return (result.astype(jnp.bfloat16), target_grad, memory_grad, grads[0], grads[1], grads[2], grads[3], grads[4], grads[5], grads[6], grads[7], grads[8], grads[9], grads[10], grads[11], grads[12], grads[13], grads[14], grads[15], grads[16], grads[17], grads[18])
```

```python
import functools
import math
from types import SimpleNamespace
from typing import NamedTuple

import jax
import jax.numpy as jnp
from jax import lax
from jax.experimental import pallas as pl
from jax.experimental.pallas import tpu as pltpu
from jax.sharding import PartitionSpec as P

HEADS = 8


masked_score = -1e30


def from_behind(block, axis, distance):
    devices = range(lax.axis_size(axis))
    route = [(i - distance, i) for i in devices if i - distance in devices]
    return lax.ppermute(block, axis, route)


def shifted(block, axis, distance):
    devices = range(lax.axis_size(axis))
    route = [((i - distance) % len(devices), i) for i in devices]
    return lax.ppermute(block, axis, route)


def layer_norm(pre_norm, gain, bias):
    centred = pre_norm - jnp.mean(pre_norm, axis=-1, keepdims=True)
    spread = jnp.mean(centred * centred, axis=-1, keepdims=True)
    return centred * lax.rsqrt(spread + 1e-05) * gain + bias


def residual_norm(previous, branch, omega, gain, bias):
    return layer_norm(previous * omega + branch, gain, bias)


def forward_product(inputs, weight):
    return jnp.dot(inputs, weight, preferred_element_type=jnp.float32)


def weight_product(inputs, grads):
    return jnp.einsum("rsd,rsf->df", inputs, grads, preferred_element_type=jnp.float32)


def input_product(grads, weight):
    return jnp.einsum("rsf,df->rsd", grads, weight, preferred_element_type=jnp.float32)


def split_heads(values, head_count):
    return values.reshape(values.shape[0], values.shape[1], head_count, -1)


def attend_update(running, query_low, key_low, value_low, allowed, score_scale, head_count):
    best, total, accum = running
    raw = (
        jnp.einsum(
            "rqhe,rkhe->rqhk",
            split_heads(query_low, head_count),
            split_heads(key_low, head_count),
            preferred_element_type=jnp.float32,
        )
        * score_scale
    )
    scores = jnp.where(allowed[:, :, None, :], raw, masked_score)
    new_best = jnp.maximum(best, jnp.max(scores, axis=-1))
    weights = jnp.where(allowed[:, :, None, :], jnp.exp(scores - new_best[..., None]), 0.0)
    factor = jnp.exp(best - new_best)
    total = total * factor + jnp.sum(weights, axis=-1)
    accum = accum * factor[..., None] + jnp.einsum(
        "rqhk,rkhe->rqhe",
        weights.astype(jnp.bfloat16),
        split_heads(value_low, head_count),
        preferred_element_type=jnp.float32,
    )
    return (new_best, total, accum)


def attend_grads(
    query_low, key_low, value_low, grad_low, logsum, row_delta, allowed, score_scale, head_count
):
    query_heads = split_heads(query_low, head_count)
    key_heads = split_heads(key_low, head_count)
    value_heads = split_heads(value_low, head_count)
    grad_heads = split_heads(grad_low, head_count)
    raw = (
        jnp.einsum("rqhe,rkhe->rqhk", query_heads, key_heads, preferred_element_type=jnp.float32)
        * score_scale
    )
    scores = jnp.where(allowed[:, :, None, :], raw, masked_score)
    attention_weights = jnp.exp(scores - logsum[..., None])
    value_grad = jnp.einsum(
        "rqhk,rqhe->rkhe",
        attention_weights.astype(jnp.bfloat16),
        grad_heads,
        preferred_element_type=jnp.float32,
    )
    weight_grad = jnp.einsum(
        "rqhe,rkhe->rqhk", grad_heads, value_heads, preferred_element_type=jnp.float32
    )
    score_grad = (attention_weights * (weight_grad - row_delta[..., None])).astype(jnp.bfloat16)
    query_grad = (
        jnp.einsum("rqhk,rkhe->rqhe", score_grad, key_heads, preferred_element_type=jnp.float32)
        * score_scale
    )
    key_grad = (
        jnp.einsum("rqhk,rqhe->rkhe", score_grad, query_heads, preferred_element_type=jnp.float32)
        * score_scale
    )
    query_shape = (query_low.shape[0], query_low.shape[1], query_low.shape[2])
    key_shape = (key_low.shape[0], key_low.shape[1], key_low.shape[2])
    return (
        query_grad.reshape(query_shape),
        key_grad.reshape(key_shape),
        value_grad.reshape(key_shape),
    )


def ring_device(
    target,
    memory,
    target_segments,
    memory_segments,
    self_query,
    self_key,
    self_value,
    self_output,
    cross_query,
    cross_key,
    cross_value,
    cross_output,
    ffn_in,
    ffn_out,
    omega_self,
    omega_cross,
    omega_ffn,
    gain_self,
    bias_self,
    gain_cross,
    bias_cross,
    gain_ffn,
    bias_ffn,
    cotangent,
):
    batch_rows, local_span, model_width = target.shape
    head_count = HEADS
    head_width = model_width // head_count
    score_scale = 1.0 / math.sqrt(head_width)
    self_index = lax.axis_index("seq")
    axis_size = lax.axis_size("seq")
    offsets = jnp.arange(local_span, dtype=jnp.int32)
    local_ids = lax.dynamic_slice_in_dim(target_segments, self_index * local_span, local_span, 1)

    def block_mask(query_source, key_source):
        query_ids = lax.dynamic_slice_in_dim(
            target_segments, query_source * local_span, local_span, 1
        )
        key_ids = lax.dynamic_slice_in_dim(target_segments, key_source * local_span, local_span, 1)
        query_place = query_source * local_span + offsets
        key_place = key_source * local_span + offsets
        matching = query_ids[:, :, None] == key_ids[:, None, :]
        return matching & (key_place[None, None, :] <= query_place[None, :, None])

    empty_state = (
        jnp.full((batch_rows, local_span, head_count), masked_score, jnp.float32),
        jnp.zeros((batch_rows, local_span, head_count), jnp.float32),
        jnp.zeros((batch_rows, local_span, head_count, head_width), jnp.float32),
    )
    self_triple = jnp.concatenate((self_query, self_key, self_value), axis=1)
    triple_low = forward_product(target, self_triple).astype(jnp.bfloat16)
    query_low = triple_low[..., :model_width]
    key_low = triple_low[..., model_width : 2 * model_width]
    value_low = triple_low[..., 2 * model_width :]
    running = attend_update(
        empty_state,
        query_low,
        key_low,
        value_low,
        block_mask(self_index, self_index),
        score_scale,
        head_count,
    )

    def forward_turn(step_index, carry):
        key_pair, running = carry
        key_pair = from_behind((key_pair[0], key_pair[1]), "seq", 1)
        source = (self_index - step_index + axis_size) % axis_size

        def forward_visit(inner):
            return attend_update(
                inner,
                query_low,
                key_pair[0],
                key_pair[1],
                block_mask(self_index, source),
                score_scale,
                head_count,
            )

        running = lax.cond(source <= self_index, forward_visit, lambda inner: inner, running)
        return (key_pair, running)

    key_pair, running = lax.fori_loop(1, axis_size, forward_turn, ((key_low, value_low), running))
    best, total, accum = running
    self_logsum = best + jnp.log(total)
    self_heads = accum / total[..., None]
    self_low = self_heads.reshape(batch_rows, local_span, model_width).astype(jnp.bfloat16)
    self_branch = forward_product(self_low, self_output)
    target_wide = target.astype(jnp.float32)
    hidden_one, pull_one = jax.vjp(
        residual_norm, target_wide, self_branch, omega_self, gain_self, bias_self
    )
    hidden_one_low = hidden_one.astype(jnp.bfloat16)
    cross_query_low = forward_product(hidden_one_low, cross_query).astype(jnp.bfloat16)
    cross_pair = jnp.concatenate((cross_key, cross_value), axis=1)
    memory_pairs = forward_product(
        lax.all_gather(memory, "seq", axis=1, tiled=True), cross_pair
    ).astype(jnp.bfloat16)
    memory_total = memory_pairs.shape[1]
    key_block = 1024
    block_count = memory_total // key_block

    def cross_mask(block_index):
        key_ids = lax.dynamic_slice_in_dim(memory_segments, block_index * key_block, key_block, 1)
        return local_ids[:, :, None] == key_ids[:, None, :]

    def block_pairs(block_index):
        return lax.dynamic_slice_in_dim(memory_pairs, block_index * key_block, key_block, 1)

    def cross_turn(block_index, running):
        pairs = block_pairs(block_index)
        return attend_update(
            running,
            cross_query_low,
            pairs[..., :model_width],
            pairs[..., model_width:],
            cross_mask(block_index),
            score_scale,
            head_count,
        )

    best, total, accum = lax.fori_loop(0, block_count, cross_turn, empty_state)
    cross_logsum = best + jnp.log(total)
    cross_heads = accum / total[..., None]
    cross_low = cross_heads.reshape(batch_rows, local_span, model_width).astype(jnp.bfloat16)
    cross_branch = forward_product(cross_low, cross_output)
    hidden_two, pull_two = jax.vjp(
        residual_norm, hidden_one, cross_branch, omega_cross, gain_cross, bias_cross
    )
    hidden_two_low = hidden_two.astype(jnp.bfloat16)
    upward = forward_product(hidden_two_low, ffn_in)
    activated, pull_gelu = jax.vjp(jax.nn.gelu, upward)
    active_low = activated.astype(jnp.bfloat16)
    ffn_branch = forward_product(active_low, ffn_out)
    result, pull_three = jax.vjp(
        residual_norm, hidden_two, ffn_branch, omega_ffn, gain_ffn, bias_ffn
    )
    two_grad, ffn_branch_grad, omega_ffn_grad, gain_ffn_grad, bias_ffn_grad = pull_three(
        cotangent.astype(jnp.float32)
    )
    ffn_branch_low = ffn_branch_grad.astype(jnp.bfloat16)
    ffn_out_grad = weight_product(active_low, ffn_branch_low)
    upward_grad = pull_gelu(input_product(ffn_branch_low, ffn_out))[0]
    upward_low = upward_grad.astype(jnp.bfloat16)
    ffn_in_grad = weight_product(hidden_two_low, upward_low)
    two_grad = two_grad + input_product(upward_low, ffn_in)
    one_grad, cross_branch_grad, omega_cross_grad, gain_cross_grad, bias_cross_grad = pull_two(
        two_grad
    )
    cross_branch_low = cross_branch_grad.astype(jnp.bfloat16)
    cross_output_grad = weight_product(cross_low, cross_branch_low)
    cross_heads_grad = input_product(cross_branch_low, cross_output).astype(jnp.bfloat16)
    cross_delta = jnp.sum(
        split_heads(cross_heads_grad, head_count).astype(jnp.float32) * cross_heads, axis=-1
    )

    def cross_back(block_index, carry):
        query_grad, pair_grads = carry
        pairs = block_pairs(block_index)
        grads = attend_grads(
            cross_query_low,
            pairs[..., :model_width],
            pairs[..., model_width:],
            cross_heads_grad,
            cross_logsum,
            cross_delta,
            cross_mask(block_index),
            score_scale,
            head_count,
        )
        block_grads = jnp.concatenate((grads[1], grads[2]), axis=2)
        pair_grads = lax.dynamic_update_slice_in_dim(
            pair_grads, block_grads, block_index * key_block, 1
        )
        return (query_grad + grads[0], pair_grads)

    zero_grid = jnp.zeros((batch_rows, local_span, model_width), jnp.float32)
    cross_query_sum, pair_grads = lax.fori_loop(
        0,
        block_count,
        cross_back,
        (zero_grid, jnp.zeros((batch_rows, memory_total, 2 * model_width), jnp.float32)),
    )
    local_pair_grads = lax.psum_scatter(
        pair_grads.astype(jnp.bfloat16), "seq", scatter_dimension=1, tiled=True
    )
    memory_grad = input_product(local_pair_grads, cross_pair)
    pair_weight_grad = weight_product(memory, local_pair_grads)
    cross_query_low_grad = cross_query_sum.astype(jnp.bfloat16)
    cross_query_grad = weight_product(hidden_one_low, cross_query_low_grad)
    one_grad = one_grad + input_product(cross_query_low_grad, cross_query)
    target_residual_grad, self_branch_grad, omega_self_grad, gain_self_grad, bias_self_grad = (
        pull_one(one_grad)
    )
    self_branch_low = self_branch_grad.astype(jnp.bfloat16)
    self_output_grad = weight_product(self_low, self_branch_low)
    self_heads_grad = input_product(self_branch_low, self_output).astype(jnp.bfloat16)
    self_delta = jnp.sum(
        split_heads(self_heads_grad, head_count).astype(jnp.float32) * self_heads, axis=-1
    )

    def key_turn(step_index, carry):
        key_pair, grad_pair, query_grad = carry
        source = (self_index - step_index + axis_size) % axis_size

        def key_visit(inner):
            grads = attend_grads(
                query_low,
                key_pair[0],
                key_pair[1],
                self_heads_grad,
                self_logsum,
                self_delta,
                block_mask(self_index, source),
                score_scale,
                head_count,
            )
            return (inner[0] + grads[0], inner[1] + grads[1], inner[2] + grads[2])

        query_grad, key_grad, value_grad = lax.cond(
            source <= self_index,
            key_visit,
            lambda inner: inner,
            (query_grad, grad_pair[0], grad_pair[1]),
        )
        grad_pair = (
            shifted(key_grad.astype(jnp.bfloat16), "seq", 1).astype(key_grad.dtype),
            shifted(value_grad.astype(jnp.bfloat16), "seq", 1).astype(value_grad.dtype),
        )
        key_pair = from_behind((key_pair[0], key_pair[1]), "seq", 1)
        return (key_pair, grad_pair, query_grad)

    key_pair, grad_pair, query_grad = lax.fori_loop(
        0, axis_size, key_turn, ((key_low, value_low), (zero_grid, zero_grid), zero_grid)
    )
    key_grad, value_grad = grad_pair
    triple_grad_low = jnp.concatenate((query_grad, key_grad, value_grad), axis=2).astype(
        jnp.bfloat16
    )
    target_grad = target_residual_grad + input_product(triple_grad_low, self_triple)
    triple_weight_grad = weight_product(target, triple_grad_low)
    sums = lax.psum(
        (
            triple_weight_grad[:, :model_width],
            triple_weight_grad[:, model_width : 2 * model_width],
            triple_weight_grad[:, 2 * model_width :],
            self_output_grad,
            cross_query_grad,
            pair_weight_grad[:, :model_width],
            pair_weight_grad[:, model_width:],
            cross_output_grad,
            ffn_in_grad,
            ffn_out_grad,
            omega_self_grad,
            omega_cross_grad,
            omega_ffn_grad,
            gain_self_grad,
            bias_self_grad,
            gain_cross_grad,
            bias_cross_grad,
            gain_ffn_grad,
            bias_ffn_grad,
        ),
        ("rows", "seq"),
    )
    return (result.astype(jnp.bfloat16), target_grad, memory_grad) + tuple(sums)


MESH = pl.DeviceIdType.MESH
f32, bf16 = jnp.float32, jnp.bfloat16

def dot(a, b):
    return jnp.dot(a, b, preferred_element_type=f32)

def dot_t(a, b):
    return lax.dot_general(a, b, (((1,), (1,)), ((), ())), preferred_element_type=f32)

def t_dot(a, b):
    return lax.dot_general(a, b, (((0,), (0,)), ((), ())), preferred_element_type=f32)

def mult(i, m):
    return i if isinstance(i, int) else pl.multiple_of(i, m)

def head_place(i, heads):
    row, head = i // heads, i % heads
    return row, head, pl.ds(mult(head * 64, 64), 64), pl.ds(mult(head // 2 * 128, 128), 128)

def attend_forward(key, value_t, query_z, bias, scores, kept, kept_out, kept_sem, out_t, inverse, heads):
    rows, keys, queries = bias.shape
    count, piece, slots = rows * heads, 256, kept.shape[0]

    def first(i, slot):
        row, head, _, pair = head_place(i, heads)
        best = None
        for c in range(keys // piece):
            ks = pl.ds(c * piece, piece)
            s = dot(key[row, ks, pair], query_z[row, head]) + bias[row, ks]
            scores[slot, ks] = s
            top = jnp.max(s.reshape(piece // 8, 8, queries), axis=0)
            best = top if best is None else jnp.maximum(best, top)
        return best

    def out_copy(i):
        row, head, _, _ = head_place(i, heads)
        return pltpu.make_async_copy(kept.at[i % slots], kept_out.at[row, head], kept_sem.at[i % slots])

    def second(i, slot, best):
        row, head, here, _ = head_place(i, heads)
        best = jnp.max(best, axis=0, keepdims=True)
        total = out = None
        for c in range(keys // piece):
            ks = pl.ds(c * piece, piece)
            p = jnp.exp(scores[slot, ks] - best)
            part = jnp.sum(p.reshape(piece // 8, 8, queries), axis=0)
            total = part if total is None else total + part
            p = p.astype(bf16)
            kept[i % slots, ks] = p
            part = dot(value_t[row, here, ks], p)
            out = part if out is None else out + part
        scale = 1.0 / jnp.sum(total, axis=0, keepdims=True)
        out_t[row, here, :] = (out * scale).astype(bf16)
        inverse[row, head] = jnp.broadcast_to(scale, (8, queries))

    def free(i):
        @pl.when(i >= slots)
        def _():
            out_copy(i - slots).wait()

    def body(j, best):
        i = 2 * j
        free(i)
        free(i + 1)
        later = first(i + 1, 1)
        second(i, 0, best)
        best = first(jnp.minimum(i + 2, count - 1), 0)
        second(i + 1, 1, later)
        out_copy(i).start()
        out_copy(i + 1).start()
        return best

    lax.fori_loop(0, count // 2, body, first(0, 0))
    return [out_copy(i) for i in range(count - slots, count)]

def norm_parts(pre):
    centred = pre - jnp.mean(pre, axis=-1, keepdims=True)
    rstd = lax.rsqrt(jnp.mean(centred * centred, axis=-1, keepdims=True) + 1e-05)
    return centred * rstd, rstd

def pad_pairs(query, query_z, row, heads):
    turned = query.T
    half = lax.broadcasted_iota(jnp.int32, (128, query.shape[0]), 0) // 64
    for head in range(heads):
        pair = turned[head // 2 * 128 : head // 2 * 128 + 128]
        query_z[row, head] = jnp.where(half == head % 2, pair, jnp.zeros_like(pair))

class ForwardIn(NamedTuple):
    target: object
    memory: object
    target_segments: object
    memory_segments: object
    self_query: object
    self_key: object
    self_value: object
    self_output: object
    cross_query: object
    cross_key: object
    cross_value: object
    cross_output: object
    ffn_in: object
    ffn_out: object
    omega_self: object
    omega_cross: object
    omega_ffn: object
    gain_self: object
    bias_self: object
    gain_cross: object
    bias_cross: object
    gain_ffn: object
    bias_ffn: object
    cotangent: object

class ForwardOut(NamedTuple):
    output: object
    target_all: object
    memory_all: object
    self_kept: object
    cross_kept: object
    self_inverse: object
    cross_inverse: object
    self_out: object
    cross_out: object
    self_q: object
    cross_q: object
    one_low: object
    one_hat: object
    one_rstd: object
    two_low: object
    two_hat: object
    two_rstd: object
    active: object
    upward_grad: object
    branch_grad: object
    two_grad: object
    sums: object

class ForwardScratch(NamedTuple):
    key: object
    value_t: object
    query_z: object
    seen_self: object
    seen_cross: object
    scores: object
    kept: object
    mem_key: object
    mem_value_t: object
    wide: object
    slope: object
    one: object
    two: object
    value_turned: object
    mem_value_turned: object

FORWARD_NAMES = ForwardIn._fields + ForwardOut._fields + ForwardScratch._fields
MATRICES = ForwardIn._fields[4:14]
VECTORS = ForwardIn._fields[14:23]

def forward_kernel(heads, *refs):
    r = SimpleNamespace(**dict(zip(FORWARD_NAMES, refs)))
    send, recv, local, kept_sem, kept_sem2 = refs[-5:]
    me_r, me_s = lax.axis_index("rows"), lax.axis_index("seq")
    core, side = me_s % 2, me_s // 2
    span, width = r.target.shape[1], r.target.shape[2]
    rows = r.target.shape[0]
    tokens = rows * span
    length = r.target_all.shape[1]
    other_core, other_side = me_s + 1 - 2 * core, me_s + 2 - 4 * side

    def place(i):
        return pl.ds(mult(i * span, span), span)

    def remote(src, dst, k, to):
        return pltpu.make_async_remote_copy(src_ref=src, dst_ref=dst, send_sem=send.at[k], recv_sem=recv.at[k],
            device_id=(me_r, to), device_id_type=MESH)

    full_x, full_m = r.target_all, r.memory_all
    x_core = remote(r.target, full_x.at[:, place(me_s)], 0, other_core)
    x_side = remote(r.target, full_x.at[:, place(me_s)], 1, other_side)
    x_pass = remote(full_x.at[:, place(other_side)], full_x.at[:, place(other_side)], 2, other_core)
    m_core = remote(r.memory, full_m.at[:, place(me_s)], 3, other_core)
    m_side = remote(r.memory, full_m.at[:, place(me_s)], 4, other_side)
    m_pass = remote(full_m.at[:, place(other_side)], full_m.at[:, place(other_side)], 5, other_core)
    x_own = pltpu.make_async_copy(r.target, full_x.at[:, place(me_s)], local.at[0])
    m_own = pltpu.make_async_copy(r.memory, full_m.at[:, place(me_s)], local.at[1])
    x_own.start()
    m_own.start()
    barrier = pltpu.get_barrier_semaphore()
    for to in (other_core, other_side):
        pl.semaphore_signal(barrier, inc=1, device_id=(me_r, to), device_id_type=MESH)
    pl.semaphore_wait(barrier, 2)

    @pl.when(side == 0)
    def _():
        x_side.start()
    m_side.start()
    x_core.start()
    m_core.start()

    @pl.when(side == 0)
    def _():
        full_x[:, pl.ds(length // 2, length // 2), :] = jnp.zeros((rows, length // 2, width), bf16)

    def mask(ids, bias, causal):
        for row in range(rows):
            mine = r.target_segments[pl.ds(row, 1), pl.ds(mult(me_s * span, span), span)].astype(f32)
            for c in range(length // 128):
                line = ids[pl.ds(row, 1), pl.ds(c * 128, 128)].astype(f32)
                column = jnp.broadcast_to(line, (128, 128)).T
                column = jnp.concatenate([column] * (span // 128), axis=1)
                seen = column == mine
                if causal:
                    key_place = c * 128 + lax.broadcasted_iota(jnp.int32, (128, span), 0)
                    query_place = me_s * span + lax.broadcasted_iota(jnp.int32, (128, span), 1)
                    seen = seen & (key_place <= query_place)
                bias[row, pl.ds(c * 128, 128)] = jnp.where(seen, 0.0, -1e30)

    mask(r.target_segments, r.seen_self, True)
    mask(r.memory_segments, r.seen_cross, False)
    r.value_turned[...] = r.self_value[...].T
    r.mem_value_turned[...] = r.cross_value[...].T
    x_own.wait()
    m_own.wait()

    def project_pair(full, key_weight, turned, key, value_t, block):
        at = place(block)
        for row in range(rows):
            here = full[row, at]
            key[row, at] = dot(here, key_weight[...]).astype(bf16)
            value_t[row, :, at] = dot_t(turned[...], here).astype(bf16)

    def project_self(block):
        project_pair(full_x, r.self_key, r.value_turned, r.key, r.value_t, block)

    def project_cross(block):
        project_pair(full_m, r.cross_key, r.mem_value_turned, r.mem_key, r.mem_value_t, block)

    for row in range(rows):
        query = (dot(full_x[row, place(me_s)], r.self_query[...]).astype(bf16) * 0.125).astype(bf16)
        r.self_q[row] = query
        pad_pairs(query, r.query_z, row, heads)
    project_self(me_s)
    project_cross(me_s)
    x_core.wait()
    project_self(other_core)
    m_core.wait()
    project_cross(other_core)

    @pl.when(side == 1)
    def _():
        x_side.wait_recv()
        x_pass.start()
    project_self(other_side)

    @pl.when(side == 1)
    def _():
        x_pass.wait()

    @pl.when(side == 0)
    def _():
        x_side.wait_send()
    project_self(other_side + 1 - 2 * core)

    last = attend_forward(r.key, r.value_t, r.query_z, r.seen_self, r.scores, r.kept, r.self_kept,
        kept_sem, r.self_out, r.self_inverse, heads)
    m_side.wait()
    m_pass.start()
    vec = [getattr(r, k)[...].reshape(1, width) for k in VECTORS]
    part = 128
    for row in range(rows):
        r.wide[pl.ds(row * span, span)] = t_dot(r.self_out[row], r.self_output[...])

    @pl.loop(0, tokens // part)
    def _(i):
        at = pl.ds(mult(i * part, part), part)
        row, inner = i // (span // part), i % (span // part)
        x = full_x[row, pl.ds(mult(me_s * span + inner * part, part), part)].astype(f32)
        hat, rstd = norm_parts(x * vec[0] + r.wide[at])
        one = hat * vec[3] + vec[4]
        r.one_hat[at] = hat
        r.one_rstd[at] = jnp.broadcast_to(rstd, (part, 128))
        r.one[at] = one
        r.one_low[at] = one.astype(bf16)

    for row in range(rows):
        query = (dot(r.one_low[pl.ds(row * span, span)], r.cross_query[...]).astype(bf16) * 0.125).astype(bf16)
        r.cross_q[row] = query
        pad_pairs(query, r.query_z, row, heads)
    project_cross(other_side)
    m_pass.wait()
    project_cross(other_side + 1 - 2 * core)
    for copy in last:
        copy.wait()
    last = attend_forward(r.mem_key, r.mem_value_t, r.query_z, r.seen_cross, r.scores, r.kept, r.cross_kept,
        kept_sem2, r.cross_out, r.cross_inverse, heads)
    for row in range(rows):
        r.wide[pl.ds(row * span, span)] = t_dot(r.cross_out[row], r.cross_output[...])

    @pl.loop(0, tokens // part)
    def _(i):
        at = pl.ds(mult(i * part, part), part)
        hat, rstd = norm_parts(r.one[at] * vec[1] + r.wide[at])
        two = hat * vec[5] + vec[6]
        r.two_hat[at] = hat
        r.two_rstd[at] = jnp.broadcast_to(rstd, (part, 128))
        r.two[at] = two
        r.two_low[at] = two.astype(bf16)

    c0 = math.sqrt(2.0 / math.pi)
    blocks = r.ffn_in.shape[1] // 512
    r.wide[...] = jnp.zeros_like(r.wide)

    @pl.loop(0, blocks)
    def _(j):
        cols = pl.ds(mult(j * 512, 512), 512)
        for half in range(2):
            at = pl.ds(half * (tokens // 2), tokens // 2)
            u = dot(r.two_low[at], r.ffn_in[:, cols])
            square = u * u
            t = jnp.tanh(c0 * u * (1.0 + 0.044715 * square))
            active = (0.5 * u * (1.0 + t)).astype(bf16)
            r.active[at, cols] = active
            r.slope[at, cols] = (0.5 * (1.0 + t) + (0.5 * c0) * u * (1.0 - t * t) * (1.0 + (3 * 0.044715) * square)).astype(bf16)
            r.wide[at] += dot(active, r.ffn_out[cols, :])

    r.sums[...] = jnp.zeros_like(r.sums)

    @pl.loop(0, tokens // part)
    def _(i):
        at = pl.ds(mult(i * part, part), part)
        row, inner = i // (span // part), i % (span // part)
        near = pl.ds(mult(inner * part, part), part)
        two = r.two[at]
        hat, rstd = norm_parts(two * vec[2] + r.wide[at])
        r.output[row, near] = (hat * vec[7] + vec[8]).astype(bf16)
        grad = r.cotangent[row, near].astype(f32)
        scaled = grad * vec[7]
        back = rstd * (scaled - jnp.mean(scaled, axis=-1, keepdims=True) - hat * jnp.mean(scaled * hat, axis=-1, keepdims=True))
        r.branch_grad[at] = back.astype(bf16)
        r.two_grad[at] = back * vec[2]
        r.sums[0] += jnp.sum((back * two).reshape(part // 8, 8, width), axis=0)
        r.sums[1] += jnp.sum((grad * hat).reshape(part // 8, 8, width), axis=0)
        r.sums[2] += jnp.sum(grad.reshape(part // 8, 8, width), axis=0)

    @pl.loop(0, blocks)
    def _(j):
        cols = pl.ds(mult(j * 512, 512), 512)
        for half in range(2):
            at = pl.ds(half * (tokens // 2), tokens // 2)
            grad = dot_t(r.branch_grad[at], r.ffn_out[cols, :])
            r.upward_grad[at, cols] = (grad * r.slope[at, cols].astype(f32)).astype(bf16)

    for copy in last:
        copy.wait()

def forward_call(target, memory, target_segments, memory_segments, matrices, vectors, cotangent, heads=8):
    rows, span, width = target.shape
    length = target_segments.shape[1]
    tokens = rows * span
    hidden = matrices[8].shape[1]
    any_, vm = pl.BlockSpec(memory_space=pl.ANY), pl.BlockSpec(memory_space=pltpu.VMEM)
    s = jax.ShapeDtypeStruct
    outs = ForwardOut(output=s((rows, span, width), bf16), target_all=s((rows, length, width), bf16), memory_all=s((rows, length, width), bf16),
        self_kept=s((rows, heads, length, span), bf16), cross_kept=s((rows, heads, length, span), bf16),
        self_inverse=s((rows, heads, 8, span), f32), cross_inverse=s((rows, heads, 8, span), f32),
        self_out=s((rows, width, span), bf16), cross_out=s((rows, width, span), bf16),
        self_q=s((rows, span, width), bf16), cross_q=s((rows, span, width), bf16),
        one_low=s((tokens, width), bf16), one_hat=s((tokens, width), f32), one_rstd=s((tokens, 128), f32),
        two_low=s((tokens, width), bf16), two_hat=s((tokens, width), f32), two_rstd=s((tokens, 128), f32),
        active=s((tokens, hidden), bf16), upward_grad=s((tokens, hidden), bf16), branch_grad=s((tokens, width), bf16),
        two_grad=s((tokens, width), f32), sums=s((3, 8, width), f32))
    scratch = ForwardScratch(key=((rows, length, width), bf16), value_t=((rows, width, length), bf16), query_z=((rows, heads, 128, span), bf16),
        seen_self=((rows, length, span), f32), seen_cross=((rows, length, span), f32), scores=((2, length, span), f32),
        kept=((4, length, span), bf16), mem_key=((rows, length, width), bf16), mem_value_t=((rows, width, length), bf16),
        wide=((tokens, width), f32), slope=((tokens, hidden), bf16), one=((tokens, width), f32), two=((tokens, width), f32),
        value_turned=((width, width), bf16), mem_value_turned=((width, width), bf16))
    return ForwardOut(*pl.pallas_call(
        functools.partial(forward_kernel, heads),
        out_shape=list(outs),
        in_specs=[any_, any_] + [vm] * (len(ForwardIn._fields) - 2),
        out_specs=list(ForwardOut(*[vm] * len(outs))._replace(self_kept=any_, cross_kept=any_)),
        scratch_shapes=[pltpu.VMEM(*k) for k in scratch] + [pltpu.SemaphoreType.DMA((6,)), pltpu.SemaphoreType.DMA((6,)),
            pltpu.SemaphoreType.DMA((2,)), pltpu.SemaphoreType.DMA((4,)), pltpu.SemaphoreType.DMA((4,))],
        compiler_params=pltpu.CompilerParams(collective_id=0, has_side_effects=True, vmem_limit_bytes=62 << 20),
        name="forward",
    )(target, memory, target_segments, memory_segments, *matrices, *vectors, cotangent))

class Reduction:
    def __init__(self, block, near, landed, reduced, send, recv, own, lags, hole, gap):
        self.block, self.near, self.landed, self.reduced = block, near, landed, reduced
        self.send, self.recv, self.own = send, recv, own
        self.r, self.s = lax.axis_index("rows"), lax.axis_index("seq")
        self.core, self.y = self.s % 2, self.s // 2
        self.x, self.z0, self.z1 = self.r % 2, (self.r // 2) % 2, self.r // 4
        self.count, self.size = block.shape[0], block.shape[1]
        self.lags, self.hole, self.gap = lags, hole, gap
        self.waves = self.count + gap + lags[-1]

    def partners(self):
        r, s = self.r, self.s
        return ((r, s + 1 - 2 * self.core), (r, s + 2 - 4 * self.y), (r + 1 - 2 * self.x, s),
                (r + 2 - 4 * self.z0, s), (r + 4 - 8 * self.z1, s))

    def hops(self, c):
        k = c % 4
        iz = k // 3
        iy = (k % 2) * (1 - iz)
        ix = 1 - iy - iz
        y, x, z0, z1 = self.y, self.x, self.z0, self.z1
        dx, dy, d0, d1 = 1 - 2 * x, 2 - 4 * y, 2 - 4 * z0, 4 - 8 * z1
        return (
            (0, 1 - 2 * self.core, self.core),
            (ix * dx + iz * d0, iy * dy, ix * x + iy * y + iz * z0),
            (iy * dx + iz * d1, ix * dy, iy * x + ix * y + iz * z1),
            (iz * dx + (1 - iz) * d0, 0, iz * x + (1 - iz) * z0),
            ((1 - iz) * d1, iz * dy, iz * y + (1 - iz) * z1),
        )

    def start_of(self, j, hops):
        off = 0
        for i in range(j):
            off = off + hops[i][2] * (self.size >> (i + 1))
        return off

    def landing(self, c, j):
        half = self.size >> (j + 1)
        if j == 0:
            return self.near.at[c % self.near.shape[0]]
        return self.landed.at[c, pl.ds(self.size // 2 - (self.size >> j), half)]

    def copy(self, c, j, hops, gather):
        off, half = self.start_of(j, hops), self.size >> (j + 1)
        dr, ds, bit = hops[j]
        if gather:
            mine = pl.ds(pl.multiple_of(off + bit * half, 16), half)
            src, dst = (self.block if j == 4 else self.reduced).at[c, mine], self.reduced.at[c, mine]
        else:
            src, dst = self.block.at[c, pl.ds(pl.multiple_of(off + (1 - bit) * half, 16), half)], self.landing(c, j)
        sem = j + 5 * gather
        return pltpu.make_async_remote_copy(src_ref=src, dst_ref=dst, send_sem=self.send.at[c, sem],
            recv_sem=self.recv.at[c, sem], device_id=(self.r + dr, self.s + ds), device_id_type=MESH)

    def own_copy(self, c, hops):
        mine = pl.ds(pl.multiple_of(self.start_of(5, hops), 16), self.size >> 5)
        return pltpu.make_async_copy(self.block.at[c, mine], self.reduced.at[c, mine], self.own.at[c])

    def add(self, c, j, hops):
        keep = pl.ds(pl.multiple_of(self.start_of(j + 1, hops), 16), self.size >> (j + 1))
        self.block[c, keep] = (self.block[c, keep].astype(f32) + self.landing(c, j)[...].astype(f32)).astype(bf16)

    def step(self, c, s):
        hops = self.hops(c)
        if 1 <= s <= 5:
            self.copy(c, s - 1, hops, 0).wait()
            self.add(c, s - 1, hops)
        elif s > 5:
            self.copy(c, 10 - s, hops, 1).wait()
        if s == 5:
            self.own_copy(c, hops).start()
        elif s == 6:
            self.own_copy(c, hops).wait()
        if s <= 4:
            self.copy(c, s, hops, 0).start()
        elif s <= 9:
            self.copy(c, 9 - s, hops, 1).start()

    def wave(self, t):
        for s in reversed(range(11)):
            v = t - self.lags[s]
            late = (v + 64) // (self.hole + self.gap + 64)
            c = v - self.gap * late
            @pl.when((v >= 0) & (c < self.count) & ((v < self.hole) | (late > 0)))
            def _():
                self.step(c, s)

class Loads(NamedTuple):
    active: object
    branch_grad: object
    two_low: object
    upward_grad: object
    ffn_in: object
    two_grad: object
    two_hat: object
    two_rstd: object
    cross_output: object
    cross_out: object
    cross_inverse: object
    memory_all: object
    cross_key: object
    cross_value: object
    cross_q: object
    one_low: object
    cross_query: object
    one_hat: object
    one_rstd: object
    self_output: object
    self_out: object
    self_inverse: object
    self_key: object
    self_value: object
    self_q: object
    self_query: object

class BackOut(NamedTuple):
    reduced: object
    target_grad: object
    memory_grad: object
    vector_grads: object

class BackScratch(NamedTuple):
    block: object
    near: object
    landed: object
    key_t: object
    value: object
    key_grad: object
    value_grad: object
    score_grad: object
    kept: object
    part: object
    part_core: object
    part_side: object
    query_grad_t: object
    query_grad: object
    branch_low: object
    out_grad_t: object
    out_grad: object
    delta: object
    vec: object
    vec_landed: object
    acc: object

LOADS = Loads._fields
UNLOADED = ForwardOut._fields[3:5] + ForwardOut._fields[1:2] + ForwardOut._fields[-1:] + VECTORS

def backward_kernel(heads, lags, hole, gap, *refs):
    n = len(LOADS + UNLOADED)
    hbm = SimpleNamespace(**dict(zip(LOADS + UNLOADED, refs)))
    r = SimpleNamespace(**dict(zip(BackOut._fields + LOADS + BackScratch._fields, refs[n:])))
    load_sem, kept_sem, send, recv, own_sem, part_send, part_recv, vec_send, vec_recv, out_sem = refs[-10:]
    r.sums = hbm.sums
    rows, length, width = r.memory_all.shape
    tokens = r.two_low.shape[0]
    span = tokens // rows
    sides = length // span // 2
    red = Reduction(r.block, r.near, r.landed, r.reduced, send, recv, own_sem, lags, hole, gap)
    me_r, me_s, core, side = red.r, red.s, red.core, red.y

    loads = Loads(*[pltpu.make_async_copy(getattr(hbm, k), getattr(r, k), load_sem.at[i]) for i, k in enumerate(LOADS)])
    for copy in loads:
        copy.start()

    def need(*copies):
        for copy in copies:
            copy.wait()

    barrier = pltpu.get_barrier_semaphore()
    for to in red.partners():
        pl.semaphore_signal(barrier, inc=1, device_id=to, device_id_type=MESH)
    pl.semaphore_wait(barrier, 5)

    def row_at(row):
        return pl.ds(row * span, span)

    def place(i):
        return pl.ds(mult(i * span, span), span)

    def ffn_block(c):
        @pl.when(c < 4)
        def _():
            r.block[c] = t_dot(r.active[:, pl.ds(mult(c * 512, 512), 512)], r.branch_grad[...]).astype(bf16)
        @pl.when((c >= 4) & (c < 8))
        def _():
            r.block[c] = t_dot(r.two_low[...], r.upward_grad[:, pl.ds(mult((c - 4) * 512, 512), 512)]).astype(bf16)

    vec = [getattr(hbm, k)[...].reshape(1, width) for k in VECTORS]
    part = 128

    def norm_back(grad_ref, hat_ref, rstd_ref, gain, bias, omega, previous, slot):
        for i in range(3):
            r.acc[slot + i] = jnp.zeros_like(r.acc[slot + i])

        @pl.loop(0, tokens // part)
        def _(i):
            at = pl.ds(mult(i * part, part), part)
            hat, grad = hat_ref[at], grad_ref[at]
            scaled = grad * gain
            back = rstd_ref[at][:, 0:1] * (scaled - jnp.mean(scaled, axis=-1, keepdims=True)
                - hat * jnp.mean(scaled * hat, axis=-1, keepdims=True))
            r.branch_low[at] = back.astype(bf16)
            grad_ref[at] = back * omega
            for k, term in enumerate((back * previous(i), grad * hat, grad)):
                r.acc[slot + k] += jnp.sum(term.reshape(part // 8, 8, width), axis=0)

    def attention_start(weight, out_t, inverse):
        for row in range(rows):
            grad_t = dot_t(weight[...], r.branch_low[row_at(row)])
            for head in range(heads):
                here = pl.ds(head * 64, 64)
                scaled = grad_t[head * 64 : head * 64 + 64] * inverse[row, head][0:1]
                r.out_grad_t[row, here] = scaled.astype(bf16)
                delta = jnp.sum(scaled * out_t[row, here].astype(f32), axis=0, keepdims=True)
                r.delta[row, head] = jnp.broadcast_to(delta, (8, span))
            r.out_grad[row] = r.out_grad_t[row].T

    def keys_again(full, key_weight, value_weight):
        key_turned = key_weight[...].T
        for row in range(rows):
            for c in range(length // 512):
                at = pl.ds(c * 512, 512)
                here = full[row, at]
                r.key_t[row, :, at] = dot_t(key_turned, here).astype(bf16)
                r.value[row, at] = dot(here, value_weight[...]).astype(bf16)

    def attention_back(kept_hbm, query, beside):
        count, piece, slots = rows * heads, 256, r.kept.shape[0]
        top = lax.broadcasted_iota(jnp.int32, (128, span), 0) // 64
        left = lax.broadcasted_iota(jnp.int32, (span, 128), 1) // 64

        def fetch(i):
            row, head, _, _ = head_place(i, heads)
            return pltpu.make_async_copy(kept_hbm.at[row, head], r.kept.at[i % slots], kept_sem.at[i % slots])

        def first(i, slot):
            row, head, _, pair = head_place(i, heads)
            fetch(i).wait()
            grad = jnp.where(top == head % 2, r.out_grad_t[row, pair, :], jnp.zeros((128, span), bf16))
            for c in range(length // piece):
                ks = pl.ds(c * piece, piece)
                p_grad = dot(r.value[row, ks, pair], grad)
                r.score_grad[slot, ks] = (r.kept[i % slots, ks].astype(f32) * (p_grad - r.delta[row, head][0:1])).astype(bf16)

        def second(j, slot):
            i = 2 * j
            row, head, _, pair = head_place(i, heads)
            none = jnp.zeros((span, 128), bf16)
            q, g = query[row, :, pair], r.out_grad[row, :, pair]
            qs = [jnp.where(left == e, q, none) for e in range(2)]
            gs = [jnp.where(left == e, g, none) for e in range(2)]
            out = [None, None]
            for c in range(length // piece):
                ks = pl.ds(c * piece, piece)
                ds = [r.score_grad[slot + e, ks] for e in range(2)]
                r.value_grad[row, ks, pair] = (dot(r.kept[i % slots, ks], gs[0]) + dot(r.kept[(i + 1) % slots, ks], gs[1])).astype(bf16)
                r.key_grad[row, ks, pair] = (dot(ds[0], qs[0]) + dot(ds[1], qs[1])).astype(bf16)
                for e in range(2):
                    a = dot(r.key_t[row, pl.ds(mult((head + e) * 64, 64), 64), ks], ds[e])
                    out[e] = a if out[e] is None else out[e] + a
            for e in range(2):
                r.query_grad_t[row, pl.ds(mult((head + e) * 64, 64), 64), :] = (out[e] * 0.125).astype(bf16)

        for i in range(slots // 2):
            fetch(i).start()
        first(0, 0)
        first(1, 1)

        @pl.loop(0, count // 4)
        def _(g):
            j = 2 * g
            @pl.when(j + 2 < count // 2)
            def _():
                for e in range(4):
                    fetch(2 * j + 4 + e).start()
            first(2 * j + 2, 2)
            first(2 * j + 3, 3)
            second(j, 0)
            @pl.when(j + 2 < count // 2)
            def _():
                first(2 * j + 4, 0)
                first(2 * j + 5, 1)
            second(j + 1, 2)
            beside(g)
        for row in range(rows):
            r.query_grad[row] = r.query_grad_t[row].T

    def pair_product(key_weight, value_weight):
        for row in range(rows):
            for i in range(2 * sides):
                at = pl.ds(i * span, span)
                r.part[i, row] = (dot_t(r.key_grad[row, at], key_weight[...]) + dot_t(r.value_grad[row, at], value_weight[...])).astype(bf16)

    def part_copy(k, src, dst, to):
        return pltpu.make_async_remote_copy(src_ref=src, dst_ref=dst, send_sem=part_send.at[k], recv_sem=part_recv.at[k],
            device_id=(me_r, to), device_id_type=MESH)

    def part_copies(turn):
        base = 3 * turn
        to_core, to_side = me_s + 1 - 2 * core, me_s + 2 - 4 * side
        far, near = 2 * (1 - side), 2 * side
        return (part_copy(base, r.part.at[far + 1 - core], r.part_core.at[turn, 0], to_core),
            part_copy(base + 1, r.part.at[near + 1 - core], r.part_core.at[turn, 1], to_core),
            part_copy(base + 2, r.part.at[far + core], r.part_side.at[turn], to_side))

    def part_start(copies):
        copies[0].start()
        copies[1].start()

    def part_cross(copies, turn):
        far = 2 * (1 - side) + core
        copies[0].wait()
        r.part[far] = (r.part[far].astype(f32) + r.part_core[turn, 0].astype(f32)).astype(bf16)

    def part_own(copies, turn):
        copies[1].wait()
        return r.part[2 * side + core].astype(f32) + r.part_core[turn, 1].astype(f32)

    need(loads.active, loads.branch_grad)
    ffn_block(0)
    red.wave(0)
    need(loads.two_low, loads.upward_grad, loads.ffn_in, loads.two_grad)
    ffn_block(1)
    red.wave(1)

    @pl.loop(0, tokens // 128)
    def _(i):
        at = pl.ds(mult(i * 128, 128), 128)
        r.two_grad[at] += dot_t(r.upward_grad[at], r.ffn_in[...])
    ffn_block(2)
    red.wave(2)
    need(loads.two_hat, loads.two_rstd, loads.one_hat, loads.one_rstd, loads.cross_output, loads.cross_out, loads.cross_inverse)
    norm_back(r.two_grad, r.two_hat, r.two_rstd, vec[5], vec[6], vec[1],
        lambda i: r.one_hat[pl.ds(mult(i * part, part), part)] * vec[3] + vec[4], 0)
    ffn_block(3)
    red.wave(3)
    r.block[8] = sum(dot(r.cross_out[row], r.branch_low[row_at(row)]) for row in range(rows)).astype(bf16)
    attention_start(r.cross_output, r.cross_out, r.cross_inverse)
    need(loads.memory_all, loads.cross_key, loads.cross_value, loads.cross_q)
    keys_again(r.memory_all, r.cross_key, r.cross_value)

    def beside_cross(g):
        ffn_block(4 + g)
        red.wave(4 + g)
    attention_back(hbm.cross_kept, r.cross_q, beside_cross)
    red.wave(8)
    r.block[9] = sum(t_dot(r.memory_all[row], r.key_grad[row]) for row in range(rows)).astype(bf16)
    red.wave(9)
    r.block[10] = sum(t_dot(r.memory_all[row], r.value_grad[row]) for row in range(rows)).astype(bf16)
    red.wave(10)
    target_load = pltpu.make_async_copy(hbm.target_all, r.memory_all, out_sem.at[0])
    target_load.start()
    need(loads.one_low, loads.cross_query)
    r.block[11] = sum(t_dot(r.one_low[row_at(row)], r.query_grad[row]) for row in range(rows)).astype(bf16)
    red.wave(11)
    for row in range(rows):
        r.two_grad[row_at(row)] += dot_t(r.query_grad[row], r.cross_query[...])
    pair_product(r.cross_key, r.cross_value)
    copies = part_copies(0)
    part_start(copies)
    need(loads.self_output, loads.self_out, loads.self_inverse, loads.self_key, loads.self_value, loads.self_q, loads.self_query)
    target_load.wait()
    full = r.memory_all

    def own_target(i):
        row, inner = i // (span // part), i % (span // part)
        return full[row, pl.ds(mult(me_s * span + inner * part, part), part)].astype(f32)
    norm_back(r.two_grad, r.one_hat, r.one_rstd, vec[3], vec[4], vec[0], own_target, 3)
    part_cross(copies, 0)
    copies[2].start()
    r.block[12] = sum(dot(r.self_out[row], r.branch_low[row_at(row)]) for row in range(rows)).astype(bf16)
    red.wave(12)
    for i in range(3):
        r.vec[pl.ds(i, 1)] = jnp.sum(r.acc[3 + i], axis=0, keepdims=True)
        r.vec[pl.ds(3 + i, 1)] = jnp.sum(r.acc[i], axis=0, keepdims=True)
        r.vec[pl.ds(6 + i, 1)] = jnp.sum(r.sums[i], axis=0, keepdims=True)
    r.vec[pl.ds(9, 7)] = jnp.zeros((7, width), f32)
    attention_start(r.self_output, r.self_out, r.self_inverse)
    keys_again(full, r.self_key, r.self_value)
    red.wave(13)

    def vec_copy(k):
        return pltpu.make_async_remote_copy(src_ref=r.vec, dst_ref=r.vec_landed.at[k], send_sem=vec_send.at[k],
            recv_sem=vec_recv.at[k], device_id=red.partners()[k], device_id_type=MESH)

    def beside_self(g):
        red.wave(14 + g)
    attention_back(hbm.self_kept, r.self_q, beside_self)
    own = part_own(copies, 0)
    copies[2].wait()
    r.memory_grad[...] = own + r.part_side[0].astype(f32)
    r.block[13] = sum(t_dot(full[row], r.key_grad[row]) for row in range(rows)).astype(bf16)
    red.wave(18)
    r.block[14] = sum(t_dot(full[row], r.value_grad[row]) for row in range(rows)).astype(bf16)
    red.wave(19)
    r.block[15] = sum(t_dot(full[row, place(me_s)], r.query_grad[row]) for row in range(rows)).astype(bf16)
    red.wave(20)
    pair_product(r.self_key, r.self_value)
    copies = part_copies(1)
    part_start(copies)
    for row in range(rows):
        r.two_grad[row_at(row)] += dot_t(r.query_grad[row], r.self_query[...])
    for k in range(5):
        vec_copy(k).start()
        if k == 2:
            part_cross(copies, 1)
            @pl.when(side == 1)
            def _():
                copies[2].start()
        red.wave(21 + k)
        vec_copy(k).wait()
        r.vec[...] += r.vec_landed[k]
    r.vector_grads[...] = r.vec[...]
    r.target_grad[...] = part_own(copies, 1) + r.two_grad[...].reshape(rows, span, width)

    @pl.loop(26, red.waves)
    def _(t):
        red.wave(t)

    @pl.when(side == 1)
    def _():
        copies[2].wait_send()

    @pl.when(side == 0)
    def _():
        copies[2].wait_recv()
        r.target_grad[...] += r.part_side[1].astype(f32)

def backward_call(o, matrices, vectors, heads=8, lags=tuple(3 * i for i in range(11)), hole=13, gap=5):
    rows, length, width = o.target_all.shape
    tokens, hidden = o.active.shape
    span = tokens // rows
    any_, vm = pl.BlockSpec(memory_space=pl.ANY), pl.BlockSpec(memory_space=pltpu.VMEM)
    s = jax.ShapeDtypeStruct
    operands = dict(o._asdict(), **dict(zip(MATRICES + VECTORS, matrices + vectors)))
    blocks = 8 + 2 * hidden // 512
    outs = BackOut(reduced=s((blocks, 512, width), bf16), target_grad=s((rows, span, width), f32), memory_grad=s((rows, span, width), f32),
        vector_grads=s((16, width), f32))
    big = (rows, length, width)
    scratch = BackScratch(block=((blocks, 512, width), bf16), near=((8, 256, width), bf16), landed=((blocks, 256, width), bf16),
        key_t=((rows, width, length), bf16), value=(big, bf16), key_grad=(big, bf16), value_grad=(big, bf16),
        score_grad=((4, length, span), bf16), kept=((8, length, span), bf16), part=((length // span, rows, span, width), bf16),
        part_core=((2, 2, rows, span, width), bf16), part_side=((2, rows, span, width), bf16),
        query_grad_t=((rows, width, span), bf16), query_grad=((rows, span, width), bf16), branch_low=((tokens, width), bf16),
        out_grad_t=((rows, width, span), bf16), out_grad=((rows, span, width), bf16), delta=((rows, heads, 8, span), f32),
        vec=((16, width), f32), vec_landed=((5, 16, width), f32), acc=((6, 8, width), f32))
    dma = pltpu.SemaphoreType.DMA
    return BackOut(*pl.pallas_call(
        functools.partial(backward_kernel, heads, lags, hole, gap),
        out_shape=list(outs),
        in_specs=[vm if k in UNLOADED[3:] else any_ for k in LOADS + UNLOADED],
        out_specs=[any_, vm, vm, vm],
        scratch_shapes=[pltpu.VMEM(operands[k].shape, operands[k].dtype) for k in LOADS] + [pltpu.VMEM(*k) for k in scratch]
            + [dma((len(LOADS),)), dma((8,)), dma((blocks, 10)), dma((blocks, 10)), dma((blocks,)), dma((6,)), dma((6,)), dma((5,)), dma((5,)), dma((2,))],
        compiler_params=pltpu.CompilerParams(collective_id=1, has_side_effects=True, vmem_limit_bytes=63 << 20),
        name="backward",
    )(*(operands[k] for k in LOADS + UNLOADED)))

FINISH_BLOCK = (15, 13, 14, 12, 11, 9, 10, 8)
VECTOR_PLACE = (0, 3, 6, 1, 2, 4, 5, 7, 8)

def finish_kernel(reduced, vector_grads, *refs):
    outs, small = refs[:10], refs[10:19]
    stage, sem = refs[19:]
    slots = stage.shape[0]
    wide = outs[8].shape[1] // 512
    places = [outs[9].at[pl.ds(512 * i, 512)] for i in range(wide)] + [outs[8].at[:, pl.ds(512 * i, 512)] for i in range(wide)]
    places += [None] * 8
    for out, block in zip(outs, FINISH_BLOCK):
        places[block] = out
    for ref, row in zip(small, VECTOR_PLACE):
        ref[...] = vector_grads[row]
    copies = [pltpu.make_async_copy(stage.at[i % slots], place, sem.at[i % slots]) for i, place in enumerate(places)]
    for i, copy in enumerate(copies):
        if i >= slots:
            copies[i - slots].wait()
        stage[i % slots] = reduced[i].astype(f32)
        copy.start()
    for copy in copies[-slots:]:
        copy.wait()

def finish_call(reduced, vector_grads, hidden):
    width = reduced.shape[2]
    any_, vm = pl.BlockSpec(memory_space=pl.ANY), pl.BlockSpec(memory_space=pltpu.VMEM)
    s = jax.ShapeDtypeStruct
    shapes = [s((width, width), f32)] * 8 + [s((width, hidden), f32), s((hidden, width), f32)] + [s((width,), f32)] * 9
    return pl.pallas_call(
        finish_kernel,
        out_shape=shapes,
        in_specs=[vm, vm],
        out_specs=[any_] * 10 + [vm] * 9,
        scratch_shapes=[pltpu.VMEM((6, 512, width), f32), pltpu.SemaphoreType.DMA((6,))],
        compiler_params=pltpu.CompilerParams(vmem_limit_bytes=32 << 20),
        name="finish",
    )(reduced, vector_grads)


def per_device(*args):
    rows, span, width = args[0].shape
    hidden = args[12].shape[1]
    fits = lax.axis_size("rows") == 8 and lax.axis_size("seq") == 4
    if not fits or (rows, span, width, hidden) != (2, 256, 512, 2048) or args[1].shape != args[0].shape:
        return ring_device(*args)
    matrices, vectors = args[4:14], args[14:23]
    kept = forward_call(args[0], args[1], args[2], args[3], matrices, vectors, args[23], HEADS)
    back = backward_call(kept, matrices, vectors, HEADS)
    sums = finish_call(back.reduced, back.vector_grads, hidden)
    return (kept.output, back.target_grad, back.memory_grad) + tuple(sums)


def solution(mesh):
    placed = (
        P("rows", "seq", None),
        P("rows", "seq", None),
        P("rows", None),
        P("rows", None),
        P(),
        P(),
        P(),
        P(),
        P(),
        P(),
        P(),
        P(),
        P(),
        P(),
        P(),
        P(),
        P(),
        P(),
        P(),
        P(),
        P(),
        P(),
        P(),
        P("rows", "seq", None),
    )
    return jax.shard_map(
        per_device,
        mesh=mesh,
        in_specs=placed,
        out_specs=(
            P("rows", "seq", None),
            P("rows", "seq", None),
            P("rows", "seq", None),
            P(),
            P(),
            P(),
            P(),
            P(),
            P(),
            P(),
            P(),
            P(),
            P(),
            P(),
            P(),
            P(),
            P(),
            P(),
            P(),
            P(),
            P(),
            P(),
        ),
        check_vma=False,
    )
```

```python
import functools
import math
from types import SimpleNamespace
from typing import NamedTuple

import jax
import jax.numpy as jnp
from jax import lax
from jax.experimental import pallas as pl
from jax.experimental.pallas import tpu as pltpu
from jax.sharding import PartitionSpec as P

HEADS = 8


masked_score = -1e30


def from_behind(block, axis, distance):
    devices = range(lax.axis_size(axis))
    route = [(i - distance, i) for i in devices if i - distance in devices]
    return lax.ppermute(block, axis, route)


def shifted(block, axis, distance):
    devices = range(lax.axis_size(axis))
    route = [((i - distance) % len(devices), i) for i in devices]
    return lax.ppermute(block, axis, route)


def layer_norm(pre_norm, gain, bias):
    centred = pre_norm - jnp.mean(pre_norm, axis=-1, keepdims=True)
    spread = jnp.mean(centred * centred, axis=-1, keepdims=True)
    return centred * lax.rsqrt(spread + 1e-05) * gain + bias


def residual_norm(previous, branch, omega, gain, bias):
    return layer_norm(previous * omega + branch, gain, bias)


def forward_product(inputs, weight):
    return jnp.dot(inputs, weight, preferred_element_type=jnp.float32)


def weight_product(inputs, grads):
    return jnp.einsum("rsd,rsf->df", inputs, grads, preferred_element_type=jnp.float32)


def input_product(grads, weight):
    return jnp.einsum("rsf,df->rsd", grads, weight, preferred_element_type=jnp.float32)


def split_heads(values, head_count):
    return values.reshape(values.shape[0], values.shape[1], head_count, -1)


def attend_update(running, query_low, key_low, value_low, allowed, score_scale, head_count):
    best, total, accum = running
    raw = (
        jnp.einsum(
            "rqhe,rkhe->rqhk",
            split_heads(query_low, head_count),
            split_heads(key_low, head_count),
            preferred_element_type=jnp.float32,
        )
        * score_scale
    )
    scores = jnp.where(allowed[:, :, None, :], raw, masked_score)
    new_best = jnp.maximum(best, jnp.max(scores, axis=-1))
    weights = jnp.where(allowed[:, :, None, :], jnp.exp(scores - new_best[..., None]), 0.0)
    factor = jnp.exp(best - new_best)
    total = total * factor + jnp.sum(weights, axis=-1)
    accum = accum * factor[..., None] + jnp.einsum(
        "rqhk,rkhe->rqhe",
        weights.astype(jnp.bfloat16),
        split_heads(value_low, head_count),
        preferred_element_type=jnp.float32,
    )
    return (new_best, total, accum)


def attend_grads(
    query_low, key_low, value_low, grad_low, logsum, row_delta, allowed, score_scale, head_count
):
    query_heads = split_heads(query_low, head_count)
    key_heads = split_heads(key_low, head_count)
    value_heads = split_heads(value_low, head_count)
    grad_heads = split_heads(grad_low, head_count)
    raw = (
        jnp.einsum("rqhe,rkhe->rqhk", query_heads, key_heads, preferred_element_type=jnp.float32)
        * score_scale
    )
    scores = jnp.where(allowed[:, :, None, :], raw, masked_score)
    attention_weights = jnp.exp(scores - logsum[..., None])
    value_grad = jnp.einsum(
        "rqhk,rqhe->rkhe",
        attention_weights.astype(jnp.bfloat16),
        grad_heads,
        preferred_element_type=jnp.float32,
    )
    weight_grad = jnp.einsum(
        "rqhe,rkhe->rqhk", grad_heads, value_heads, preferred_element_type=jnp.float32
    )
    score_grad = (attention_weights * (weight_grad - row_delta[..., None])).astype(jnp.bfloat16)
    query_grad = (
        jnp.einsum("rqhk,rkhe->rqhe", score_grad, key_heads, preferred_element_type=jnp.float32)
        * score_scale
    )
    key_grad = (
        jnp.einsum("rqhk,rqhe->rkhe", score_grad, query_heads, preferred_element_type=jnp.float32)
        * score_scale
    )
    query_shape = (query_low.shape[0], query_low.shape[1], query_low.shape[2])
    key_shape = (key_low.shape[0], key_low.shape[1], key_low.shape[2])
    return (
        query_grad.reshape(query_shape),
        key_grad.reshape(key_shape),
        value_grad.reshape(key_shape),
    )


def ring_device(
    target,
    memory,
    target_segments,
    memory_segments,
    self_query,
    self_key,
    self_value,
    self_output,
    cross_query,
    cross_key,
    cross_value,
    cross_output,
    ffn_in,
    ffn_out,
    omega_self,
    omega_cross,
    omega_ffn,
    gain_self,
    bias_self,
    gain_cross,
    bias_cross,
    gain_ffn,
    bias_ffn,
    cotangent,
):
    batch_rows, local_span, model_width = target.shape
    head_count = HEADS
    head_width = model_width // head_count
    score_scale = 1.0 / math.sqrt(head_width)
    self_index = lax.axis_index("seq")
    axis_size = lax.axis_size("seq")
    offsets = jnp.arange(local_span, dtype=jnp.int32)
    local_ids = lax.dynamic_slice_in_dim(target_segments, self_index * local_span, local_span, 1)

    def block_mask(query_source, key_source):
        query_ids = lax.dynamic_slice_in_dim(
            target_segments, query_source * local_span, local_span, 1
        )
        key_ids = lax.dynamic_slice_in_dim(target_segments, key_source * local_span, local_span, 1)
        query_place = query_source * local_span + offsets
        key_place = key_source * local_span + offsets
        matching = query_ids[:, :, None] == key_ids[:, None, :]
        return matching & (key_place[None, None, :] <= query_place[None, :, None])

    empty_state = (
        jnp.full((batch_rows, local_span, head_count), masked_score, jnp.float32),
        jnp.zeros((batch_rows, local_span, head_count), jnp.float32),
        jnp.zeros((batch_rows, local_span, head_count, head_width), jnp.float32),
    )
    self_triple = jnp.concatenate((self_query, self_key, self_value), axis=1)
    triple_low = forward_product(target, self_triple).astype(jnp.bfloat16)
    query_low = triple_low[..., :model_width]
    key_low = triple_low[..., model_width : 2 * model_width]
    value_low = triple_low[..., 2 * model_width :]
    running = attend_update(
        empty_state,
        query_low,
        key_low,
        value_low,
        block_mask(self_index, self_index),
        score_scale,
        head_count,
    )

    def forward_turn(step_index, carry):
        key_pair, running = carry
        key_pair = from_behind((key_pair[0], key_pair[1]), "seq", 1)
        source = (self_index - step_index + axis_size) % axis_size

        def forward_visit(inner):
            return attend_update(
                inner,
                query_low,
                key_pair[0],
                key_pair[1],
                block_mask(self_index, source),
                score_scale,
                head_count,
            )

        running = lax.cond(source <= self_index, forward_visit, lambda inner: inner, running)
        return (key_pair, running)

    key_pair, running = lax.fori_loop(1, axis_size, forward_turn, ((key_low, value_low), running))
    best, total, accum = running
    self_logsum = best + jnp.log(total)
    self_heads = accum / total[..., None]
    self_low = self_heads.reshape(batch_rows, local_span, model_width).astype(jnp.bfloat16)
    self_branch = forward_product(self_low, self_output)
    target_wide = target.astype(jnp.float32)
    hidden_one, pull_one = jax.vjp(
        residual_norm, target_wide, self_branch, omega_self, gain_self, bias_self
    )
    hidden_one_low = hidden_one.astype(jnp.bfloat16)
    cross_query_low = forward_product(hidden_one_low, cross_query).astype(jnp.bfloat16)
    cross_pair = jnp.concatenate((cross_key, cross_value), axis=1)
    memory_pairs = forward_product(
        lax.all_gather(memory, "seq", axis=1, tiled=True), cross_pair
    ).astype(jnp.bfloat16)
    memory_total = memory_pairs.shape[1]
    key_block = 1024
    block_count = memory_total // key_block

    def cross_mask(block_index):
        key_ids = lax.dynamic_slice_in_dim(memory_segments, block_index * key_block, key_block, 1)
        return local_ids[:, :, None] == key_ids[:, None, :]

    def block_pairs(block_index):
        return lax.dynamic_slice_in_dim(memory_pairs, block_index * key_block, key_block, 1)

    def cross_turn(block_index, running):
        pairs = block_pairs(block_index)
        return attend_update(
            running,
            cross_query_low,
            pairs[..., :model_width],
            pairs[..., model_width:],
            cross_mask(block_index),
            score_scale,
            head_count,
        )

    best, total, accum = lax.fori_loop(0, block_count, cross_turn, empty_state)
    cross_logsum = best + jnp.log(total)
    cross_heads = accum / total[..., None]
    cross_low = cross_heads.reshape(batch_rows, local_span, model_width).astype(jnp.bfloat16)
    cross_branch = forward_product(cross_low, cross_output)
    hidden_two, pull_two = jax.vjp(
        residual_norm, hidden_one, cross_branch, omega_cross, gain_cross, bias_cross
    )
    hidden_two_low = hidden_two.astype(jnp.bfloat16)
    upward = forward_product(hidden_two_low, ffn_in)
    activated, pull_gelu = jax.vjp(jax.nn.gelu, upward)
    active_low = activated.astype(jnp.bfloat16)
    ffn_branch = forward_product(active_low, ffn_out)
    result, pull_three = jax.vjp(
        residual_norm, hidden_two, ffn_branch, omega_ffn, gain_ffn, bias_ffn
    )
    two_grad, ffn_branch_grad, omega_ffn_grad, gain_ffn_grad, bias_ffn_grad = pull_three(
        cotangent.astype(jnp.float32)
    )
    ffn_branch_low = ffn_branch_grad.astype(jnp.bfloat16)
    ffn_out_grad = weight_product(active_low, ffn_branch_low)
    upward_grad = pull_gelu(input_product(ffn_branch_low, ffn_out))[0]
    upward_low = upward_grad.astype(jnp.bfloat16)
    ffn_in_grad = weight_product(hidden_two_low, upward_low)
    two_grad = two_grad + input_product(upward_low, ffn_in)
    one_grad, cross_branch_grad, omega_cross_grad, gain_cross_grad, bias_cross_grad = pull_two(
        two_grad
    )
    cross_branch_low = cross_branch_grad.astype(jnp.bfloat16)
    cross_output_grad = weight_product(cross_low, cross_branch_low)
    cross_heads_grad = input_product(cross_branch_low, cross_output).astype(jnp.bfloat16)
    cross_delta = jnp.sum(
        split_heads(cross_heads_grad, head_count).astype(jnp.float32) * cross_heads, axis=-1
    )

    def cross_back(block_index, carry):
        query_grad, pair_grads = carry
        pairs = block_pairs(block_index)
        grads = attend_grads(
            cross_query_low,
            pairs[..., :model_width],
            pairs[..., model_width:],
            cross_heads_grad,
            cross_logsum,
            cross_delta,
            cross_mask(block_index),
            score_scale,
            head_count,
        )
        block_grads = jnp.concatenate((grads[1], grads[2]), axis=2)
        pair_grads = lax.dynamic_update_slice_in_dim(
            pair_grads, block_grads, block_index * key_block, 1
        )
        return (query_grad + grads[0], pair_grads)

    zero_grid = jnp.zeros((batch_rows, local_span, model_width), jnp.float32)
    cross_query_sum, pair_grads = lax.fori_loop(
        0,
        block_count,
        cross_back,
        (zero_grid, jnp.zeros((batch_rows, memory_total, 2 * model_width), jnp.float32)),
    )
    local_pair_grads = lax.psum_scatter(
        pair_grads.astype(jnp.bfloat16), "seq", scatter_dimension=1, tiled=True
    )
    memory_grad = input_product(local_pair_grads, cross_pair)
    pair_weight_grad = weight_product(memory, local_pair_grads)
    cross_query_low_grad = cross_query_sum.astype(jnp.bfloat16)
    cross_query_grad = weight_product(hidden_one_low, cross_query_low_grad)
    one_grad = one_grad + input_product(cross_query_low_grad, cross_query)
    target_residual_grad, self_branch_grad, omega_self_grad, gain_self_grad, bias_self_grad = (
        pull_one(one_grad)
    )
    self_branch_low = self_branch_grad.astype(jnp.bfloat16)
    self_output_grad = weight_product(self_low, self_branch_low)
    self_heads_grad = input_product(self_branch_low, self_output).astype(jnp.bfloat16)
    self_delta = jnp.sum(
        split_heads(self_heads_grad, head_count).astype(jnp.float32) * self_heads, axis=-1
    )

    def key_turn(step_index, carry):
        key_pair, grad_pair, query_grad = carry
        source = (self_index - step_index + axis_size) % axis_size

        def key_visit(inner):
            grads = attend_grads(
                query_low,
                key_pair[0],
                key_pair[1],
                self_heads_grad,
                self_logsum,
                self_delta,
                block_mask(self_index, source),
                score_scale,
                head_count,
            )
            return (inner[0] + grads[0], inner[1] + grads[1], inner[2] + grads[2])

        query_grad, key_grad, value_grad = lax.cond(
            source <= self_index,
            key_visit,
            lambda inner: inner,
            (query_grad, grad_pair[0], grad_pair[1]),
        )
        grad_pair = (
            shifted(key_grad.astype(jnp.bfloat16), "seq", 1).astype(key_grad.dtype),
            shifted(value_grad.astype(jnp.bfloat16), "seq", 1).astype(value_grad.dtype),
        )
        key_pair = from_behind((key_pair[0], key_pair[1]), "seq", 1)
        return (key_pair, grad_pair, query_grad)

    key_pair, grad_pair, query_grad = lax.fori_loop(
        0, axis_size, key_turn, ((key_low, value_low), (zero_grid, zero_grid), zero_grid)
    )
    key_grad, value_grad = grad_pair
    triple_grad_low = jnp.concatenate((query_grad, key_grad, value_grad), axis=2).astype(
        jnp.bfloat16
    )
    target_grad = target_residual_grad + input_product(triple_grad_low, self_triple)
    triple_weight_grad = weight_product(target, triple_grad_low)
    sums = lax.psum(
        (
            triple_weight_grad[:, :model_width],
            triple_weight_grad[:, model_width : 2 * model_width],
            triple_weight_grad[:, 2 * model_width :],
            self_output_grad,
            cross_query_grad,
            pair_weight_grad[:, :model_width],
            pair_weight_grad[:, model_width:],
            cross_output_grad,
            ffn_in_grad,
            ffn_out_grad,
            omega_self_grad,
            omega_cross_grad,
            omega_ffn_grad,
            gain_self_grad,
            bias_self_grad,
            gain_cross_grad,
            bias_cross_grad,
            gain_ffn_grad,
            bias_ffn_grad,
        ),
        ("rows", "seq"),
    )
    return (result.astype(jnp.bfloat16), target_grad, memory_grad) + tuple(sums)


MESH = pl.DeviceIdType.MESH
f32, bf16 = jnp.float32, jnp.bfloat16

def dot(a, b):
    return jnp.dot(a, b, preferred_element_type=f32)

def dot_t(a, b):
    return lax.dot_general(a, b, (((1,), (1,)), ((), ())), preferred_element_type=f32)

def t_dot(a, b):
    return lax.dot_general(a, b, (((0,), (0,)), ((), ())), preferred_element_type=f32)

def mult(i, m):
    return i if isinstance(i, int) else pl.multiple_of(i, m)

def head_place(i, heads):
    row, head = i // heads, i % heads
    return row, head, pl.ds(mult(head * 64, 64), 64), pl.ds(mult(head // 2 * 128, 128), 128)

def attend_forward(key, value_t, query_z, bias, scores, kept, kept_out, kept_sem, out_t, inverse, heads):
    rows, keys, queries = bias.shape
    count, piece, slots = rows * heads, 256, kept.shape[0]

    def first(i, slot):
        row, head, _, pair = head_place(i, heads)
        best = None
        for c in range(keys // piece):
            ks = pl.ds(c * piece, piece)
            s = dot(key[row, ks, pair], query_z[row, head]) + bias[row, ks]
            scores[slot, ks] = s
            top = jnp.max(s.reshape(piece // 8, 8, queries), axis=0)
            best = top if best is None else jnp.maximum(best, top)
        return best

    def out_copy(i):
        row, head, _, _ = head_place(i, heads)
        return pltpu.make_async_copy(kept.at[i % slots], kept_out.at[row, head], kept_sem.at[i % slots])

    def second(i, slot, best):
        row, head, here, _ = head_place(i, heads)
        best = jnp.max(best, axis=0, keepdims=True)
        total = out = None
        for c in range(keys // piece):
            ks = pl.ds(c * piece, piece)
            p = jnp.exp(scores[slot, ks] - best)
            part = jnp.sum(p.reshape(piece // 8, 8, queries), axis=0)
            total = part if total is None else total + part
            p = p.astype(bf16)
            kept[i % slots, ks] = p
            part = dot(value_t[row, here, ks], p)
            out = part if out is None else out + part
        scale = 1.0 / jnp.sum(total, axis=0, keepdims=True)
        out_t[row, here, :] = (out * scale).astype(bf16)
        inverse[row, head] = jnp.broadcast_to(scale, (8, queries))

    def free(i):
        @pl.when(i >= slots)
        def _():
            out_copy(i - slots).wait()

    def body(j, best):
        i = 2 * j
        free(i)
        free(i + 1)
        later = first(i + 1, 1)
        second(i, 0, best)
        best = first(jnp.minimum(i + 2, count - 1), 0)
        second(i + 1, 1, later)
        out_copy(i).start()
        out_copy(i + 1).start()
        return best

    lax.fori_loop(0, count // 2, body, first(0, 0))
    return [out_copy(i) for i in range(count - slots, count)]

def norm_parts(pre):
    centred = pre - jnp.mean(pre, axis=-1, keepdims=True)
    rstd = lax.rsqrt(jnp.mean(centred * centred, axis=-1, keepdims=True) + 1e-05)
    return centred * rstd, rstd

def pad_pairs(query, query_z, row, heads):
    turned = query.T
    half = lax.broadcasted_iota(jnp.int32, (128, query.shape[0]), 0) // 64
    for head in range(heads):
        pair = turned[head // 2 * 128 : head // 2 * 128 + 128]
        query_z[row, head] = jnp.where(half == head % 2, pair, jnp.zeros_like(pair))

class ForwardIn(NamedTuple):
    target: object
    memory: object
    target_segments: object
    memory_segments: object
    self_query: object
    self_key: object
    self_value: object
    self_output: object
    cross_query: object
    cross_key: object
    cross_value: object
    cross_output: object
    ffn_in: object
    ffn_out: object
    omega_self: object
    omega_cross: object
    omega_ffn: object
    gain_self: object
    bias_self: object
    gain_cross: object
    bias_cross: object
    gain_ffn: object
    bias_ffn: object
    cotangent: object

class ForwardOut(NamedTuple):
    output: object
    target_all: object
    memory_all: object
    self_kept: object
    cross_kept: object
    self_inverse: object
    cross_inverse: object
    self_out: object
    cross_out: object
    self_q: object
    cross_q: object
    one_low: object
    one_hat: object
    one_rstd: object
    two_low: object
    two_hat: object
    two_rstd: object
    active: object
    upward_grad: object
    branch_grad: object
    two_grad: object
    sums: object

class ForwardScratch(NamedTuple):
    key: object
    value_t: object
    query_z: object
    seen_self: object
    seen_cross: object
    scores: object
    kept: object
    mem_key: object
    mem_value_t: object
    wide: object
    slope: object
    one: object
    two: object
    value_turned: object
    mem_value_turned: object

FORWARD_NAMES = ForwardIn._fields + ForwardOut._fields + ForwardScratch._fields
MATRICES = ForwardIn._fields[4:14]
VECTORS = ForwardIn._fields[14:23]

def forward_kernel(heads, *refs):
    r = SimpleNamespace(**dict(zip(FORWARD_NAMES, refs)))
    send, recv, local, kept_sem, kept_sem2 = refs[-5:]
    me_r, me_s = lax.axis_index("rows"), lax.axis_index("seq")
    core, side = me_s % 2, me_s // 2
    span, width = r.target.shape[1], r.target.shape[2]
    rows = r.target.shape[0]
    tokens = rows * span
    length = r.target_all.shape[1]
    other_core, other_side = me_s + 1 - 2 * core, me_s + 2 - 4 * side

    def place(i):
        return pl.ds(mult(i * span, span), span)

    def remote(src, dst, k, to):
        return pltpu.make_async_remote_copy(src_ref=src, dst_ref=dst, send_sem=send.at[k], recv_sem=recv.at[k],
            device_id=(me_r, to), device_id_type=MESH)

    full_x, full_m = r.target_all, r.memory_all
    x_core = remote(r.target, full_x.at[:, place(me_s)], 0, other_core)
    x_side = remote(r.target, full_x.at[:, place(me_s)], 1, other_side)
    x_pass = remote(full_x.at[:, place(other_side)], full_x.at[:, place(other_side)], 2, other_core)
    m_core = remote(r.memory, full_m.at[:, place(me_s)], 3, other_core)
    m_side = remote(r.memory, full_m.at[:, place(me_s)], 4, other_side)
    m_pass = remote(full_m.at[:, place(other_side)], full_m.at[:, place(other_side)], 5, other_core)
    x_own = pltpu.make_async_copy(r.target, full_x.at[:, place(me_s)], local.at[0])
    m_own = pltpu.make_async_copy(r.memory, full_m.at[:, place(me_s)], local.at[1])
    x_own.start()
    m_own.start()
    barrier = pltpu.get_barrier_semaphore()
    for to in (other_core, other_side):
        pl.semaphore_signal(barrier, inc=1, device_id=(me_r, to), device_id_type=MESH)
    pl.semaphore_wait(barrier, 2)

    @pl.when(side == 0)
    def _():
        x_side.start()
    m_side.start()
    x_core.start()
    m_core.start()

    @pl.when(side == 0)
    def _():
        full_x[:, pl.ds(length // 2, length // 2), :] = jnp.zeros((rows, length // 2, width), bf16)

    def mask(ids, bias, causal):
        for row in range(rows):
            mine = r.target_segments[pl.ds(row, 1), pl.ds(mult(me_s * span, span), span)].astype(f32)
            for c in range(length // 128):
                line = ids[pl.ds(row, 1), pl.ds(c * 128, 128)].astype(f32)
                column = jnp.broadcast_to(line, (128, 128)).T
                column = jnp.concatenate([column] * (span // 128), axis=1)
                seen = column == mine
                if causal:
                    key_place = c * 128 + lax.broadcasted_iota(jnp.int32, (128, span), 0)
                    query_place = me_s * span + lax.broadcasted_iota(jnp.int32, (128, span), 1)
                    seen = seen & (key_place <= query_place)
                bias[row, pl.ds(c * 128, 128)] = jnp.where(seen, 0.0, -1e30)

    mask(r.target_segments, r.seen_self, True)
    mask(r.memory_segments, r.seen_cross, False)
    r.value_turned[...] = r.self_value[...].T
    r.mem_value_turned[...] = r.cross_value[...].T
    x_own.wait()
    m_own.wait()

    def project_pair(full, key_weight, turned, key, value_t, block):
        at = place(block)
        for row in range(rows):
            here = full[row, at]
            key[row, at] = dot(here, key_weight[...]).astype(bf16)
            value_t[row, :, at] = dot_t(turned[...], here).astype(bf16)

    def project_self(block):
        project_pair(full_x, r.self_key, r.value_turned, r.key, r.value_t, block)

    def project_cross(block):
        project_pair(full_m, r.cross_key, r.mem_value_turned, r.mem_key, r.mem_value_t, block)

    for row in range(rows):
        query = (dot(full_x[row, place(me_s)], r.self_query[...]).astype(bf16) * 0.125).astype(bf16)
        r.self_q[row] = query
        pad_pairs(query, r.query_z, row, heads)
    project_self(me_s)
    project_cross(me_s)
    x_core.wait()
    project_self(other_core)
    m_core.wait()
    project_cross(other_core)

    @pl.when(side == 1)
    def _():
        x_side.wait_recv()
        x_pass.start()
    project_self(other_side)

    @pl.when(side == 1)
    def _():
        x_pass.wait()

    @pl.when(side == 0)
    def _():
        x_side.wait_send()
    project_self(other_side + 1 - 2 * core)

    last = attend_forward(r.key, r.value_t, r.query_z, r.seen_self, r.scores, r.kept, r.self_kept,
        kept_sem, r.self_out, r.self_inverse, heads)
    m_side.wait()
    m_pass.start()
    vec = [getattr(r, k)[...].reshape(1, width) for k in VECTORS]
    part = 128
    for row in range(rows):
        r.wide[pl.ds(row * span, span)] = t_dot(r.self_out[row], r.self_output[...])

    @pl.loop(0, tokens // part)
    def _(i):
        at = pl.ds(mult(i * part, part), part)
        row, inner = i // (span // part), i % (span // part)
        x = full_x[row, pl.ds(mult(me_s * span + inner * part, part), part)].astype(f32)
        hat, rstd = norm_parts(x * vec[0] + r.wide[at])
        one = hat * vec[3] + vec[4]
        r.one_hat[at] = hat
        r.one_rstd[at] = jnp.broadcast_to(rstd, (part, 128))
        r.one[at] = one
        r.one_low[at] = one.astype(bf16)

    for row in range(rows):
        query = (dot(r.one_low[pl.ds(row * span, span)], r.cross_query[...]).astype(bf16) * 0.125).astype(bf16)
        r.cross_q[row] = query
        pad_pairs(query, r.query_z, row, heads)
    project_cross(other_side)
    m_pass.wait()
    project_cross(other_side + 1 - 2 * core)
    for copy in last:
        copy.wait()
    last = attend_forward(r.mem_key, r.mem_value_t, r.query_z, r.seen_cross, r.scores, r.kept, r.cross_kept,
        kept_sem2, r.cross_out, r.cross_inverse, heads)
    for row in range(rows):
        r.wide[pl.ds(row * span, span)] = t_dot(r.cross_out[row], r.cross_output[...])

    @pl.loop(0, tokens // part)
    def _(i):
        at = pl.ds(mult(i * part, part), part)
        hat, rstd = norm_parts(r.one[at] * vec[1] + r.wide[at])
        two = hat * vec[5] + vec[6]
        r.two_hat[at] = hat
        r.two_rstd[at] = jnp.broadcast_to(rstd, (part, 128))
        r.two[at] = two
        r.two_low[at] = two.astype(bf16)

    c0 = math.sqrt(2.0 / math.pi)
    blocks = r.ffn_in.shape[1] // 512
    r.wide[...] = jnp.zeros_like(r.wide)

    @pl.loop(0, blocks)
    def _(j):
        cols = pl.ds(mult(j * 512, 512), 512)
        for half in range(2):
            at = pl.ds(half * (tokens // 2), tokens // 2)
            u = dot(r.two_low[at], r.ffn_in[:, cols])
            square = u * u
            t = jnp.tanh(c0 * u * (1.0 + 0.044715 * square))
            active = (0.5 * u * (1.0 + t)).astype(bf16)
            r.active[at, cols] = active
            r.slope[at, cols] = (0.5 * (1.0 + t) + (0.5 * c0) * u * (1.0 - t * t) * (1.0 + (3 * 0.044715) * square)).astype(bf16)
            r.wide[at] += dot(active, r.ffn_out[cols, :])

    r.sums[...] = jnp.zeros_like(r.sums)

    @pl.loop(0, tokens // part)
    def _(i):
        at = pl.ds(mult(i * part, part), part)
        row, inner = i // (span // part), i % (span // part)
        near = pl.ds(mult(inner * part, part), part)
        two = r.two[at]
        hat, rstd = norm_parts(two * vec[2] + r.wide[at])
        r.output[row, near] = (hat * vec[7] + vec[8]).astype(bf16)
        grad = r.cotangent[row, near].astype(f32)
        scaled = grad * vec[7]
        back = rstd * (scaled - jnp.mean(scaled, axis=-1, keepdims=True) - hat * jnp.mean(scaled * hat, axis=-1, keepdims=True))
        r.branch_grad[at] = back.astype(bf16)
        r.two_grad[at] = back * vec[2]
        r.sums[0] += jnp.sum((back * two).reshape(part // 8, 8, width), axis=0)
        r.sums[1] += jnp.sum((grad * hat).reshape(part // 8, 8, width), axis=0)
        r.sums[2] += jnp.sum(grad.reshape(part // 8, 8, width), axis=0)

    @pl.loop(0, blocks)
    def _(j):
        cols = pl.ds(mult(j * 512, 512), 512)
        for half in range(2):
            at = pl.ds(half * (tokens // 2), tokens // 2)
            grad = dot_t(r.branch_grad[at], r.ffn_out[cols, :])
            r.upward_grad[at, cols] = (grad * r.slope[at, cols].astype(f32)).astype(bf16)

    for copy in last:
        copy.wait()

def forward_call(target, memory, target_segments, memory_segments, matrices, vectors, cotangent, heads=8):
    rows, span, width = target.shape
    length = target_segments.shape[1]
    tokens = rows * span
    hidden = matrices[8].shape[1]
    any_, vm = pl.BlockSpec(memory_space=pl.ANY), pl.BlockSpec(memory_space=pltpu.VMEM)
    s = jax.ShapeDtypeStruct
    outs = ForwardOut(output=s((rows, span, width), bf16), target_all=s((rows, length, width), bf16), memory_all=s((rows, length, width), bf16),
        self_kept=s((rows, heads, length, span), bf16), cross_kept=s((rows, heads, length, span), bf16),
        self_inverse=s((rows, heads, 8, span), f32), cross_inverse=s((rows, heads, 8, span), f32),
        self_out=s((rows, width, span), bf16), cross_out=s((rows, width, span), bf16),
        self_q=s((rows, span, width), bf16), cross_q=s((rows, span, width), bf16),
        one_low=s((tokens, width), bf16), one_hat=s((tokens, width), f32), one_rstd=s((tokens, 128), f32),
        two_low=s((tokens, width), bf16), two_hat=s((tokens, width), f32), two_rstd=s((tokens, 128), f32),
        active=s((tokens, hidden), bf16), upward_grad=s((tokens, hidden), bf16), branch_grad=s((tokens, width), bf16),
        two_grad=s((tokens, width), f32), sums=s((3, 8, width), f32))
    scratch = ForwardScratch(key=((rows, length, width), bf16), value_t=((rows, width, length), bf16), query_z=((rows, heads, 128, span), bf16),
        seen_self=((rows, length, span), f32), seen_cross=((rows, length, span), f32), scores=((2, length, span), f32),
        kept=((4, length, span), bf16), mem_key=((rows, length, width), bf16), mem_value_t=((rows, width, length), bf16),
        wide=((tokens, width), f32), slope=((tokens, hidden), bf16), one=((tokens, width), f32), two=((tokens, width), f32),
        value_turned=((width, width), bf16), mem_value_turned=((width, width), bf16))
    return ForwardOut(*pl.pallas_call(
        functools.partial(forward_kernel, heads),
        out_shape=list(outs),
        in_specs=[any_, any_] + [vm] * (len(ForwardIn._fields) - 2),
        out_specs=list(ForwardOut(*[vm] * len(outs))._replace(self_kept=any_, cross_kept=any_)),
        scratch_shapes=[pltpu.VMEM(*k) for k in scratch] + [pltpu.SemaphoreType.DMA((6,)), pltpu.SemaphoreType.DMA((6,)),
            pltpu.SemaphoreType.DMA((2,)), pltpu.SemaphoreType.DMA((4,)), pltpu.SemaphoreType.DMA((4,))],
        compiler_params=pltpu.CompilerParams(collective_id=0, has_side_effects=True, vmem_limit_bytes=62 << 20),
        name="forward",
    )(target, memory, target_segments, memory_segments, *matrices, *vectors, cotangent))

CLASSES = (3, 0, 3, 0, 3, 0, 0, 0, 1, 1, 0, 3, 3, 0, 0, 0)
PLAN = (
    (0,),
    (1,),
    (2,),
    (3,),
    (4,),
    (0, 5),
    (1, 6),
    (2, 3, 7),
    (4, 5, 6, 7, 0),
    (1,),
    (8,),
    (),
    (),
    (2, 3),
    (1, 8),
    (),
    (5, 4),
    (3,),
    (0,),
    (6, 2),
    (1, 8),
    (5, 4, 7, 9),
    (1, 0, 3, 2, 6, 10),
    (11,),
    (1, 0, 2, 3, 5, 4, 6, 8, 7, 9, 10, 11, 16),
    (),
    (1, 0, 2, 18),
    (3, 4, 12),
    (5,),
    (6, 8),
    (7,),
    (9, 10, 0, 16, 18, 12, 1, 2),
    (4,),
    (11,),
    (3, 5, 6, 9, 10),
    (8, 7),
    (),
    (1, 0),
    (4, 13),
    (14, 1),
    (15, 12),
    (2, 13, 14, 15, 11, 17),
    (),
    (5, 6, 16, 9, 18, 10, 8, 7, 13, 17, 3, 5, 14, 0, 6, 4, 13, 0, 15, 12, 11, 18, 2, 9, 3, 10, 8, 2, 7, 3, 5, 4, 5, 6, 13, 17, 12, 18, 9, 4, 10, 14, 8, 6, 13, 15, 11, 18, 9, 7, 10, 12, 14, 13, 15, 9, 8, 14, 11, 13, 15, 10, 7, 12, 8, 14, 11, 15, 7, 9, 14, 10, 13, 12, 9, 15, 11, 14, 10, 15, 13, 12, 13, 11, 14, 11, 14, 15, 12, 15, 12),
)

class Reduction:
    def __init__(self, block, near, landed, reduced, send, recv, own):
        self.block, self.near, self.landed, self.reduced = block, near, landed, reduced
        self.send, self.recv, self.own = send, recv, own
        self.r, self.s = lax.axis_index("rows"), lax.axis_index("seq")
        self.core, self.y = self.s % 2, self.s // 2
        self.x, self.z0, self.z1 = self.r % 2, (self.r // 2) % 2, self.r // 4
        self.count, self.size = block.shape[0], block.shape[1]
        x, y, z0, z1 = self.x, self.y, self.z0, self.z1
        core, ax, ay = (0, 1 - 2 * self.core, self.core), (1 - 2 * x, 0, x), (0, 2 - 4 * y, y)
        an, af = (2 - 4 * z0, 0, z0), (4 - 8 * z1, 0, z1)
        self.orders = {0: (core, ax, ay, an, af), 1: (core, ay, ax, an, af), 3: (core, an, af, ax, ay)}
        self.flows, self.turn, done = {}, 0, {}
        self.polls = []
        for entry in PLAN:
            self.polls.append([(c, done.setdefault(c, []).append(0) or len(done[c]) - 1) for c in entry])

    def partners(self):
        r, s = self.r, self.s
        return ((r, s + 1 - 2 * self.core), (r, s + 2 - 4 * self.y), (r + 1 - 2 * self.x, s),
                (r + 2 - 4 * self.z0, s), (r + 4 - 8 * self.z1, s))

    def start_of(self, j, hops):
        off = 0
        for i in range(j):
            off = off + hops[i][2] * (self.size >> (i + 1))
        return off

    def landing(self, c, j):
        half = self.size >> (j + 1)
        if j == 0:
            return self.near.at[c]
        return self.landed.at[c, pl.ds(self.size // 2 - (self.size >> j), half)]

    def copy(self, c, j, gather):
        hops = self.orders[CLASSES[c]]
        off, half = self.start_of(j, hops), self.size >> (j + 1)
        dr, ds, bit = hops[j]
        if gather:
            mine = pl.ds(pl.multiple_of(off + bit * half, 16), half)
            src, dst = (self.block if j == 4 else self.reduced).at[c, mine], self.reduced.at[c, mine]
        else:
            src, dst = self.block.at[c, pl.ds(pl.multiple_of(off + (1 - bit) * half, 16), half)], self.landing(c, j)
        return pltpu.make_async_remote_copy(src_ref=src, dst_ref=dst, send_sem=self.send.at[c],
            recv_sem=self.recv.at[c, j + 5 * gather], device_id=(self.r + dr, self.s + ds), device_id_type=MESH)

    def own_copy(self, c):
        mine = pl.ds(pl.multiple_of(self.start_of(5, self.orders[CLASSES[c]]), 16), self.size >> 5)
        return pltpu.make_async_copy(self.block.at[c, mine], self.reduced.at[c, mine], self.own.at[c])

    def add(self, c, j):
        keep = pl.ds(pl.multiple_of(self.start_of(j + 1, self.orders[CLASSES[c]]), 16), self.size >> (j + 1))
        self.block[c, keep] = (self.block[c, keep].astype(f32) + self.landing(c, j)[...].astype(f32)).astype(bf16)

    def step(self, c, s):
        if c >= self.count:
            return self.flows[c](s)
        if 1 <= s <= 5:
            self.copy(c, s - 1, 0).wait()
            self.add(c, s - 1)
        elif s > 5:
            self.copy(c, 10 - s, 1).wait()
        if s == 5:
            self.own_copy(c).start()
        elif s == 6:
            self.own_copy(c).wait()
        if s <= 4:
            self.copy(c, s, 0).start()
        elif s <= 9:
            self.copy(c, 9 - s, 1).start()

    def poll(self, index=None):
        if index is None:
            index = self.turn
            self.turn += 1
        for c, s in self.polls[index]:
            self.step(c, s)

    def poll_loop(self, base, count, i, half):
        for k in range(count):
            if self.polls[base + 2 * k + half]:
                @pl.when(i == k)
                def _():
                    self.poll(base + 2 * k + half)

class Loads(NamedTuple):
    active: object
    branch_grad: object
    two_low: object
    upward_grad: object
    ffn_in: object
    two_grad: object
    two_hat: object
    two_rstd: object
    cross_output: object
    cross_out: object
    cross_inverse: object
    memory_all: object
    cross_key: object
    cross_value: object
    cross_q: object
    one_low: object
    cross_query: object
    one_hat: object
    one_rstd: object
    self_output: object
    self_out: object
    self_inverse: object
    self_key: object
    self_value: object
    self_q: object
    self_query: object

class BackOut(NamedTuple):
    reduced: object
    target_grad: object
    memory_grad: object
    vector_grads: object

class BackScratch(NamedTuple):
    block: object
    near: object
    landed: object
    key_t: object
    value: object
    key_grad: object
    value_grad: object
    score_grad: object
    kept: object
    part: object
    part_core: object
    part_side: object
    query_grad_t: object
    query_grad: object
    branch_low: object
    out_grad_t: object
    out_grad: object
    delta: object
    vec: object
    vec_landed: object
    acc: object

LOADS = Loads._fields
UNLOADED = ForwardOut._fields[3:5] + ForwardOut._fields[1:2] + ForwardOut._fields[-1:] + VECTORS

def backward_kernel(heads, *refs):
    n = len(LOADS + UNLOADED)
    hbm = SimpleNamespace(**dict(zip(LOADS + UNLOADED, refs)))
    r = SimpleNamespace(**dict(zip(BackOut._fields + LOADS + BackScratch._fields, refs[n:])))
    load_sem, kept_sem, send, recv, own_sem, part_send, part_recv, vec_send, vec_recv, out_sem = refs[-10:]
    r.sums = hbm.sums
    rows, length, width = r.memory_all.shape
    tokens = r.two_low.shape[0]
    span = tokens // rows
    sides = length // span // 2
    red = Reduction(r.block, r.near, r.landed, r.reduced, send, recv, own_sem)
    me_r, me_s, core, side = red.r, red.s, red.core, red.y

    loads = Loads(*[pltpu.make_async_copy(getattr(hbm, k), getattr(r, k), load_sem.at[i]) for i, k in enumerate(LOADS)])
    for copy in loads:
        copy.start()

    def need(*copies):
        for copy in copies:
            copy.wait()

    barrier = pltpu.get_barrier_semaphore()
    for to in red.partners():
        pl.semaphore_signal(barrier, inc=1, device_id=to, device_id_type=MESH)
    pl.semaphore_wait(barrier, 5)

    def row_at(row):
        return pl.ds(row * span, span)

    def place(i):
        return pl.ds(mult(i * span, span), span)

    def ffn_block(c):
        if c < 4:
            r.block[c] = t_dot(r.active[:, pl.ds(c * 512, 512)], r.branch_grad[...]).astype(bf16)
        else:
            r.block[c] = t_dot(r.two_low[...], r.upward_grad[:, pl.ds((c - 4) * 512, 512)]).astype(bf16)

    vec = [getattr(hbm, k)[...].reshape(1, width) for k in VECTORS]
    part = 128

    def norm_back(grad_ref, hat_ref, rstd_ref, gain, omega, previous, slot):
        for i in range(3):
            r.acc[slot + i] = jnp.zeros_like(r.acc[slot + i])

        @pl.loop(0, tokens // part)
        def _(i):
            at = pl.ds(mult(i * part, part), part)
            hat, grad = hat_ref[at], grad_ref[at]
            scaled = grad * gain
            back = rstd_ref[at][:, 0:1] * (scaled - jnp.mean(scaled, axis=-1, keepdims=True)
                - hat * jnp.mean(scaled * hat, axis=-1, keepdims=True))
            r.branch_low[at] = back.astype(bf16)
            grad_ref[at] = back * omega
            for k, term in enumerate((back * previous(i), grad * hat, grad)):
                r.acc[slot + k] += jnp.sum(term.reshape(part // 8, 8, width), axis=0)

    def attention_start(weight, out_t, inverse):
        for row in range(rows):
            grad_t = dot_t(weight[...], r.branch_low[row_at(row)])
            for head in range(heads):
                here = pl.ds(head * 64, 64)
                scaled = grad_t[head * 64 : head * 64 + 64] * inverse[row, head][0:1]
                r.out_grad_t[row, here] = scaled.astype(bf16)
                delta = jnp.sum(scaled * out_t[row, here].astype(f32), axis=0, keepdims=True)
                r.delta[row, head] = jnp.broadcast_to(delta, (8, span))
            r.out_grad[row] = r.out_grad_t[row].T

    def keys_again(full, key_weight, value_weight):
        key_turned = key_weight[...].T
        for row in range(rows):
            for c in range(length // 512):
                at = pl.ds(c * 512, 512)
                here = full[row, at]
                r.key_t[row, :, at] = dot_t(key_turned, here).astype(bf16)
                r.value[row, at] = dot(here, value_weight[...]).astype(bf16)

    def attention_back(kept_hbm, query):
        base = red.turn
        red.turn += rows * heads // 2
        count, piece, slots = rows * heads, 256, r.kept.shape[0]
        top = lax.broadcasted_iota(jnp.int32, (128, span), 0) // 64
        left = lax.broadcasted_iota(jnp.int32, (span, 128), 1) // 64

        def fetch(i):
            row, head, _, _ = head_place(i, heads)
            return pltpu.make_async_copy(kept_hbm.at[row, head], r.kept.at[i % slots], kept_sem.at[i % slots])

        def first(i, slot):
            row, head, _, pair = head_place(i, heads)
            fetch(i).wait()
            grad = jnp.where(top == head % 2, r.out_grad_t[row, pair, :], jnp.zeros((128, span), bf16))
            for c in range(length // piece):
                ks = pl.ds(c * piece, piece)
                p_grad = dot(r.value[row, ks, pair], grad)
                r.score_grad[slot, ks] = (r.kept[i % slots, ks].astype(f32) * (p_grad - r.delta[row, head][0:1])).astype(bf16)

        def second(j, slot):
            i = 2 * j
            row, head, _, pair = head_place(i, heads)
            none = jnp.zeros((span, 128), bf16)
            q, g = query[row, :, pair], r.out_grad[row, :, pair]
            qs = [jnp.where(left == e, q, none) for e in range(2)]
            gs = [jnp.where(left == e, g, none) for e in range(2)]
            out = [None, None]
            for c in range(length // piece):
                ks = pl.ds(c * piece, piece)
                ds = [r.score_grad[slot + e, ks] for e in range(2)]
                r.value_grad[row, ks, pair] = (dot(r.kept[i % slots, ks], gs[0]) + dot(r.kept[(i + 1) % slots, ks], gs[1])).astype(bf16)
                r.key_grad[row, ks, pair] = (dot(ds[0], qs[0]) + dot(ds[1], qs[1])).astype(bf16)
                for e in range(2):
                    a = dot(r.key_t[row, pl.ds(mult((head + e) * 64, 64), 64), ks], ds[e])
                    out[e] = a if out[e] is None else out[e] + a
            for e in range(2):
                r.query_grad_t[row, pl.ds(mult((head + e) * 64, 64), 64), :] = (out[e] * 0.125).astype(bf16)

        for i in range(slots // 2):
            fetch(i).start()
        first(0, 0)
        first(1, 1)

        @pl.loop(0, count // 4)
        def _(g):
            j = 2 * g
            @pl.when(j + 2 < count // 2)
            def _():
                for e in range(4):
                    fetch(2 * j + 4 + e).start()
            first(2 * j + 2, 2)
            first(2 * j + 3, 3)
            second(j, 0)
            red.poll_loop(base, count // 4, g, 0)
            @pl.when(j + 2 < count // 2)
            def _():
                first(2 * j + 4, 0)
                first(2 * j + 5, 1)
            second(j + 1, 2)
            red.poll_loop(base, count // 4, g, 1)
        for row in range(rows):
            r.query_grad[row] = r.query_grad_t[row].T

    def pair_product(key_weight, value_weight):
        for row in range(rows):
            for i in range(2 * sides):
                at = pl.ds(i * span, span)
                r.part[i, row] = (dot_t(r.key_grad[row, at], key_weight[...]) + dot_t(r.value_grad[row, at], value_weight[...])).astype(bf16)

    def part_copy(k, src, dst, to):
        return pltpu.make_async_remote_copy(src_ref=src, dst_ref=dst, send_sem=part_send.at[k], recv_sem=part_recv.at[k],
            device_id=(me_r, to), device_id_type=MESH)

    def part_flow(turn, out):
        to_core, to_side = me_s + 1 - 2 * core, me_s + 2 - 4 * side
        far, near = 2 * (1 - side), 2 * side
        copies = (part_copy(3 * turn, r.part.at[far + 1 - core], r.part_core.at[turn, 0], to_core),
            part_copy(3 * turn + 1, r.part.at[near + 1 - core], r.part_core.at[turn, 1], to_core),
            part_copy(3 * turn + 2, r.part_core.at[turn, 0], r.part_side.at[turn], to_side))

        def across():
            copies[2].start()

        def arrived():
            copies[2].wait_recv()
            out[...] += r.part_side[turn].astype(f32)

        def step(s):
            if s == 0:
                copies[0].start()
                copies[1].start()
            elif s == 1:
                copies[0].wait()
                r.part_core[turn, 0] = (r.part[far + core].astype(f32) + r.part_core[turn, 0].astype(f32)).astype(bf16)
                pl.when(side >= turn)(across)
                copies[1].wait()
                out[...] = out[...] + r.part[near + core].astype(f32) + r.part_core[turn, 1].astype(f32)
            else:
                pl.when(side >= turn)(copies[2].wait_send)
                pl.when(side + turn <= 1)(arrived)
        return step

    def vec_copy(k):
        return pltpu.make_async_remote_copy(src_ref=r.vec, dst_ref=r.vec_landed.at[k], send_sem=vec_send.at[k],
            recv_sem=vec_recv.at[k], device_id=red.partners()[k], device_id_type=MESH)

    def vec_flow(s):
        if s >= 1:
            vec_copy(s - 1).wait()
            r.vec[...] += r.vec_landed[s - 1]
        if s <= 4:
            vec_copy(s).start()
        else:
            r.vector_grads[...] = r.vec[...]

    red.flows = {16: part_flow(0, r.memory_grad), 17: part_flow(1, r.target_grad), 18: vec_flow}

    need(loads.active, loads.branch_grad)
    for c in range(8):
        if c == 4:
            need(loads.two_low, loads.upward_grad)
        ffn_block(c)
        red.poll()
    need(loads.ffn_in, loads.two_grad)

    @pl.loop(0, tokens // 128)
    def _(i):
        at = pl.ds(mult(i * 128, 128), 128)
        r.two_grad[at] += dot_t(r.upward_grad[at], r.ffn_in[...])
    red.poll()
    need(loads.two_hat, loads.two_rstd, loads.one_hat, loads.one_rstd, loads.cross_output, loads.cross_out, loads.cross_inverse)
    norm_back(r.two_grad, r.two_hat, r.two_rstd, vec[5], vec[1], lambda i: r.one_hat[pl.ds(mult(i * part, part), part)] * vec[3] + vec[4], 0)
    red.poll()
    r.block[8] = sum(dot(r.cross_out[row], r.branch_low[row_at(row)]) for row in range(rows)).astype(bf16)
    red.poll()
    attention_start(r.cross_output, r.cross_out, r.cross_inverse)
    red.poll()
    need(loads.memory_all, loads.cross_key, loads.cross_value, loads.cross_q)
    keys_again(r.memory_all, r.cross_key, r.cross_value)
    red.poll()
    attention_back(hbm.cross_kept, r.cross_q)
    r.block[9] = sum(t_dot(r.memory_all[row], r.key_grad[row]) for row in range(rows)).astype(bf16)
    red.poll()
    r.block[10] = sum(t_dot(r.memory_all[row], r.value_grad[row]) for row in range(rows)).astype(bf16)
    red.poll()
    target_load = pltpu.make_async_copy(hbm.target_all, r.memory_all, out_sem)
    target_load.start()
    need(loads.one_low, loads.cross_query)
    r.block[11] = sum(t_dot(r.one_low[row_at(row)], r.query_grad[row]) for row in range(rows)).astype(bf16)
    red.poll()
    r.memory_grad[...] = jnp.zeros_like(r.memory_grad)
    pair_product(r.cross_key, r.cross_value)
    red.poll()
    for row in range(rows):
        r.two_grad[row_at(row)] += dot_t(r.query_grad[row], r.cross_query[...])
    red.poll()
    need(loads.self_output, loads.self_out, loads.self_inverse, loads.self_key, loads.self_value, loads.self_q, loads.self_query)
    target_load.wait()
    full = r.memory_all

    def own_target(i):
        row, inner = i // (span // part), i % (span // part)
        return full[row, pl.ds(mult(me_s * span + inner * part, part), part)].astype(f32)
    norm_back(r.two_grad, r.one_hat, r.one_rstd, vec[3], vec[0], own_target, 3)
    for i in range(3):
        r.vec[pl.ds(i, 1)] = jnp.sum(r.acc[3 + i], axis=0, keepdims=True)
        r.vec[pl.ds(3 + i, 1)] = jnp.sum(r.acc[i], axis=0, keepdims=True)
        r.vec[pl.ds(6 + i, 1)] = jnp.sum(r.sums[i], axis=0, keepdims=True)
    r.vec[pl.ds(9, 7)] = jnp.zeros((7, width), f32)
    red.poll()
    r.block[12] = sum(dot(r.self_out[row], r.branch_low[row_at(row)]) for row in range(rows)).astype(bf16)
    red.poll()
    attention_start(r.self_output, r.self_out, r.self_inverse)
    red.poll()
    keys_again(full, r.self_key, r.self_value)
    red.poll()
    attention_back(hbm.self_kept, r.self_q)
    r.block[13] = sum(t_dot(full[row], r.key_grad[row]) for row in range(rows)).astype(bf16)
    red.poll()
    r.block[14] = sum(t_dot(full[row], r.value_grad[row]) for row in range(rows)).astype(bf16)
    red.poll()
    r.block[15] = sum(t_dot(full[row, place(me_s)], r.query_grad[row]) for row in range(rows)).astype(bf16)
    red.poll()
    pair_product(r.self_key, r.self_value)
    for row in range(rows):
        r.target_grad[row] = r.two_grad[row_at(row)] + dot_t(r.query_grad[row], r.self_query[...])
    red.poll()
    red.poll()
    red.poll()

def backward_call(o, matrices, vectors, heads=8):
    rows, length, width = o.target_all.shape
    tokens, hidden = o.active.shape
    span = tokens // rows
    any_, vm = pl.BlockSpec(memory_space=pl.ANY), pl.BlockSpec(memory_space=pltpu.VMEM)
    s = jax.ShapeDtypeStruct
    operands = dict(o._asdict(), **dict(zip(MATRICES + VECTORS, matrices + vectors)))
    blocks = 8 + 2 * hidden // 512
    outs = BackOut(reduced=s((blocks, 512, width), bf16), target_grad=s((rows, span, width), f32), memory_grad=s((rows, span, width), f32),
        vector_grads=s((16, width), f32))
    big = (rows, length, width)
    scratch = BackScratch(block=((blocks, 512, width), bf16), near=((blocks, 256, width), bf16), landed=((blocks, 256, width), bf16),
        key_t=((rows, width, length), bf16), value=(big, bf16), key_grad=(big, bf16), value_grad=(big, bf16),
        score_grad=((4, length, span), bf16), kept=((8, length, span), bf16), part=((length // span, rows, span, width), bf16),
        part_core=((2, 2, rows, span, width), bf16), part_side=((2, rows, span, width), bf16),
        query_grad_t=((rows, width, span), bf16), query_grad=((rows, span, width), bf16), branch_low=((tokens, width), bf16),
        out_grad_t=((rows, width, span), bf16), out_grad=((rows, span, width), bf16), delta=((rows, heads, 8, span), f32),
        vec=((16, width), f32), vec_landed=((5, 16, width), f32), acc=((6, 8, width), f32))
    dma = pltpu.SemaphoreType.DMA
    return BackOut(*pl.pallas_call(
        functools.partial(backward_kernel, heads),
        out_shape=list(outs),
        in_specs=[vm if k in UNLOADED[3:] else any_ for k in LOADS + UNLOADED],
        out_specs=[any_, vm, vm, vm],
        scratch_shapes=[pltpu.VMEM(operands[k].shape, operands[k].dtype) for k in LOADS] + [pltpu.VMEM(*k) for k in scratch]
            + [dma((len(LOADS),)), dma((8,)), dma((blocks,)), dma((blocks, 10)), dma((blocks,)), dma((6,)), dma((6,)), dma((5,)), dma((5,)), dma],
        compiler_params=pltpu.CompilerParams(collective_id=1, has_side_effects=True, vmem_limit_bytes=63 << 20),
        name="backward",
    )(*(operands[k] for k in LOADS + UNLOADED)))

FINISH_BLOCK = (15, 13, 14, 12, 11, 9, 10, 8)
VECTOR_PLACE = (0, 3, 6, 1, 2, 4, 5, 7, 8)

def finish_kernel(reduced, vector_grads, *refs):
    outs, small = refs[:10], refs[10:19]
    stage, sem = refs[19:]
    slots = stage.shape[0]
    wide = outs[8].shape[1] // 512
    places = [outs[9].at[pl.ds(512 * i, 512)] for i in range(wide)] + [outs[8].at[:, pl.ds(512 * i, 512)] for i in range(wide)]
    places += [None] * 8
    for out, block in zip(outs, FINISH_BLOCK):
        places[block] = out
    for ref, row in zip(small, VECTOR_PLACE):
        ref[...] = vector_grads[row]
    copies = [pltpu.make_async_copy(stage.at[i % slots], place, sem.at[i % slots]) for i, place in enumerate(places)]
    for i, copy in enumerate(copies):
        if i >= slots:
            copies[i - slots].wait()
        stage[i % slots] = reduced[i].astype(f32)
        copy.start()
    for copy in copies[-slots:]:
        copy.wait()

def finish_call(reduced, vector_grads, hidden):
    width = reduced.shape[2]
    any_, vm = pl.BlockSpec(memory_space=pl.ANY), pl.BlockSpec(memory_space=pltpu.VMEM)
    s = jax.ShapeDtypeStruct
    shapes = [s((width, width), f32)] * 8 + [s((width, hidden), f32), s((hidden, width), f32)] + [s((width,), f32)] * 9
    return pl.pallas_call(
        finish_kernel,
        out_shape=shapes,
        in_specs=[vm, vm],
        out_specs=[any_] * 10 + [vm] * 9,
        scratch_shapes=[pltpu.VMEM((6, 512, width), f32), pltpu.SemaphoreType.DMA((6,))],
        compiler_params=pltpu.CompilerParams(vmem_limit_bytes=32 << 20),
        name="finish",
    )(reduced, vector_grads)


def per_device(*args):
    rows, span, width = args[0].shape
    hidden = args[12].shape[1]
    fits = lax.axis_size("rows") == 8 and lax.axis_size("seq") == 4
    if not fits or (rows, span, width, hidden) != (2, 256, 512, 2048) or args[1].shape != args[0].shape:
        return ring_device(*args)
    matrices, vectors = args[4:14], args[14:23]
    kept = forward_call(args[0], args[1], args[2], args[3], matrices, vectors, args[23], HEADS)
    back = backward_call(kept, matrices, vectors, HEADS)
    sums = finish_call(back.reduced, back.vector_grads, hidden)
    return (kept.output, back.target_grad, back.memory_grad) + tuple(sums)


def solution(mesh):
    placed = (
        P("rows", "seq", None),
        P("rows", "seq", None),
        P("rows", None),
        P("rows", None),
        P(),
        P(),
        P(),
        P(),
        P(),
        P(),
        P(),
        P(),
        P(),
        P(),
        P(),
        P(),
        P(),
        P(),
        P(),
        P(),
        P(),
        P(),
        P(),
        P("rows", "seq", None),
    )
    return jax.shard_map(
        per_device,
        mesh=mesh,
        in_specs=placed,
        out_specs=(
            P("rows", "seq", None),
            P("rows", "seq", None),
            P("rows", "seq", None),
            P(),
            P(),
            P(),
            P(),
            P(),
            P(),
            P(),
            P(),
            P(),
            P(),
            P(),
            P(),
            P(),
            P(),
            P(),
            P(),
            P(),
            P(),
            P(),
        ),
        check_vma=False,
    )
```

```python
import functools
import math
from types import SimpleNamespace
from typing import NamedTuple

import jax
import jax.numpy as jnp
from jax import lax
from jax.experimental import pallas as pl
from jax.experimental.pallas import tpu as pltpu
from jax.sharding import PartitionSpec as P

HEADS = 8


masked_score = -1e30


def from_behind(block, axis, distance):
    devices = range(lax.axis_size(axis))
    route = [(i - distance, i) for i in devices if i - distance in devices]
    return lax.ppermute(block, axis, route)


def shifted(block, axis, distance):
    devices = range(lax.axis_size(axis))
    route = [((i - distance) % len(devices), i) for i in devices]
    return lax.ppermute(block, axis, route)


def layer_norm(pre_norm, gain, bias):
    centred = pre_norm - jnp.mean(pre_norm, axis=-1, keepdims=True)
    spread = jnp.mean(centred * centred, axis=-1, keepdims=True)
    return centred * lax.rsqrt(spread + 1e-05) * gain + bias


def residual_norm(previous, branch, omega, gain, bias):
    return layer_norm(previous * omega + branch, gain, bias)


def forward_product(inputs, weight):
    return jnp.dot(inputs, weight, preferred_element_type=jnp.float32)


def weight_product(inputs, grads):
    return jnp.einsum("rsd,rsf->df", inputs, grads, preferred_element_type=jnp.float32)


def input_product(grads, weight):
    return jnp.einsum("rsf,df->rsd", grads, weight, preferred_element_type=jnp.float32)


def split_heads(values, head_count):
    return values.reshape(values.shape[0], values.shape[1], head_count, -1)


def attend_update(running, query_low, key_low, value_low, allowed, score_scale, head_count):
    best, total, accum = running
    raw = (
        jnp.einsum(
            "rqhe,rkhe->rqhk",
            split_heads(query_low, head_count),
            split_heads(key_low, head_count),
            preferred_element_type=jnp.float32,
        )
        * score_scale
    )
    scores = jnp.where(allowed[:, :, None, :], raw, masked_score)
    new_best = jnp.maximum(best, jnp.max(scores, axis=-1))
    weights = jnp.where(allowed[:, :, None, :], jnp.exp(scores - new_best[..., None]), 0.0)
    factor = jnp.exp(best - new_best)
    total = total * factor + jnp.sum(weights, axis=-1)
    accum = accum * factor[..., None] + jnp.einsum(
        "rqhk,rkhe->rqhe",
        weights.astype(jnp.bfloat16),
        split_heads(value_low, head_count),
        preferred_element_type=jnp.float32,
    )
    return (new_best, total, accum)


def attend_grads(
    query_low, key_low, value_low, grad_low, logsum, row_delta, allowed, score_scale, head_count
):
    query_heads = split_heads(query_low, head_count)
    key_heads = split_heads(key_low, head_count)
    value_heads = split_heads(value_low, head_count)
    grad_heads = split_heads(grad_low, head_count)
    raw = (
        jnp.einsum("rqhe,rkhe->rqhk", query_heads, key_heads, preferred_element_type=jnp.float32)
        * score_scale
    )
    scores = jnp.where(allowed[:, :, None, :], raw, masked_score)
    attention_weights = jnp.exp(scores - logsum[..., None])
    value_grad = jnp.einsum(
        "rqhk,rqhe->rkhe",
        attention_weights.astype(jnp.bfloat16),
        grad_heads,
        preferred_element_type=jnp.float32,
    )
    weight_grad = jnp.einsum(
        "rqhe,rkhe->rqhk", grad_heads, value_heads, preferred_element_type=jnp.float32
    )
    score_grad = (attention_weights * (weight_grad - row_delta[..., None])).astype(jnp.bfloat16)
    query_grad = (
        jnp.einsum("rqhk,rkhe->rqhe", score_grad, key_heads, preferred_element_type=jnp.float32)
        * score_scale
    )
    key_grad = (
        jnp.einsum("rqhk,rqhe->rkhe", score_grad, query_heads, preferred_element_type=jnp.float32)
        * score_scale
    )
    query_shape = (query_low.shape[0], query_low.shape[1], query_low.shape[2])
    key_shape = (key_low.shape[0], key_low.shape[1], key_low.shape[2])
    return (
        query_grad.reshape(query_shape),
        key_grad.reshape(key_shape),
        value_grad.reshape(key_shape),
    )


def ring_device(
    target,
    memory,
    target_segments,
    memory_segments,
    self_query,
    self_key,
    self_value,
    self_output,
    cross_query,
    cross_key,
    cross_value,
    cross_output,
    ffn_in,
    ffn_out,
    omega_self,
    omega_cross,
    omega_ffn,
    gain_self,
    bias_self,
    gain_cross,
    bias_cross,
    gain_ffn,
    bias_ffn,
    cotangent,
):
    batch_rows, local_span, model_width = target.shape
    head_count = HEADS
    head_width = model_width // head_count
    score_scale = 1.0 / math.sqrt(head_width)
    self_index = lax.axis_index("seq")
    axis_size = lax.axis_size("seq")
    offsets = jnp.arange(local_span, dtype=jnp.int32)
    local_ids = lax.dynamic_slice_in_dim(target_segments, self_index * local_span, local_span, 1)

    def block_mask(query_source, key_source):
        query_ids = lax.dynamic_slice_in_dim(
            target_segments, query_source * local_span, local_span, 1
        )
        key_ids = lax.dynamic_slice_in_dim(target_segments, key_source * local_span, local_span, 1)
        query_place = query_source * local_span + offsets
        key_place = key_source * local_span + offsets
        matching = query_ids[:, :, None] == key_ids[:, None, :]
        return matching & (key_place[None, None, :] <= query_place[None, :, None])

    empty_state = (
        jnp.full((batch_rows, local_span, head_count), masked_score, jnp.float32),
        jnp.zeros((batch_rows, local_span, head_count), jnp.float32),
        jnp.zeros((batch_rows, local_span, head_count, head_width), jnp.float32),
    )
    self_triple = jnp.concatenate((self_query, self_key, self_value), axis=1)
    triple_low = forward_product(target, self_triple).astype(jnp.bfloat16)
    query_low = triple_low[..., :model_width]
    key_low = triple_low[..., model_width : 2 * model_width]
    value_low = triple_low[..., 2 * model_width :]
    running = attend_update(
        empty_state,
        query_low,
        key_low,
        value_low,
        block_mask(self_index, self_index),
        score_scale,
        head_count,
    )

    def forward_turn(step_index, carry):
        key_pair, running = carry
        key_pair = from_behind((key_pair[0], key_pair[1]), "seq", 1)
        source = (self_index - step_index + axis_size) % axis_size

        def forward_visit(inner):
            return attend_update(
                inner,
                query_low,
                key_pair[0],
                key_pair[1],
                block_mask(self_index, source),
                score_scale,
                head_count,
            )

        running = lax.cond(source <= self_index, forward_visit, lambda inner: inner, running)
        return (key_pair, running)

    key_pair, running = lax.fori_loop(1, axis_size, forward_turn, ((key_low, value_low), running))
    best, total, accum = running
    self_logsum = best + jnp.log(total)
    self_heads = accum / total[..., None]
    self_low = self_heads.reshape(batch_rows, local_span, model_width).astype(jnp.bfloat16)
    self_branch = forward_product(self_low, self_output)
    target_wide = target.astype(jnp.float32)
    hidden_one, pull_one = jax.vjp(
        residual_norm, target_wide, self_branch, omega_self, gain_self, bias_self
    )
    hidden_one_low = hidden_one.astype(jnp.bfloat16)
    cross_query_low = forward_product(hidden_one_low, cross_query).astype(jnp.bfloat16)
    cross_pair = jnp.concatenate((cross_key, cross_value), axis=1)
    memory_pairs = forward_product(
        lax.all_gather(memory, "seq", axis=1, tiled=True), cross_pair
    ).astype(jnp.bfloat16)
    memory_total = memory_pairs.shape[1]
    key_block = 1024
    block_count = memory_total // key_block

    def cross_mask(block_index):
        key_ids = lax.dynamic_slice_in_dim(memory_segments, block_index * key_block, key_block, 1)
        return local_ids[:, :, None] == key_ids[:, None, :]

    def block_pairs(block_index):
        return lax.dynamic_slice_in_dim(memory_pairs, block_index * key_block, key_block, 1)

    def cross_turn(block_index, running):
        pairs = block_pairs(block_index)
        return attend_update(
            running,
            cross_query_low,
            pairs[..., :model_width],
            pairs[..., model_width:],
            cross_mask(block_index),
            score_scale,
            head_count,
        )

    best, total, accum = lax.fori_loop(0, block_count, cross_turn, empty_state)
    cross_logsum = best + jnp.log(total)
    cross_heads = accum / total[..., None]
    cross_low = cross_heads.reshape(batch_rows, local_span, model_width).astype(jnp.bfloat16)
    cross_branch = forward_product(cross_low, cross_output)
    hidden_two, pull_two = jax.vjp(
        residual_norm, hidden_one, cross_branch, omega_cross, gain_cross, bias_cross
    )
    hidden_two_low = hidden_two.astype(jnp.bfloat16)
    upward = forward_product(hidden_two_low, ffn_in)
    activated, pull_gelu = jax.vjp(jax.nn.gelu, upward)
    active_low = activated.astype(jnp.bfloat16)
    ffn_branch = forward_product(active_low, ffn_out)
    result, pull_three = jax.vjp(
        residual_norm, hidden_two, ffn_branch, omega_ffn, gain_ffn, bias_ffn
    )
    two_grad, ffn_branch_grad, omega_ffn_grad, gain_ffn_grad, bias_ffn_grad = pull_three(
        cotangent.astype(jnp.float32)
    )
    ffn_branch_low = ffn_branch_grad.astype(jnp.bfloat16)
    ffn_out_grad = weight_product(active_low, ffn_branch_low)
    upward_grad = pull_gelu(input_product(ffn_branch_low, ffn_out))[0]
    upward_low = upward_grad.astype(jnp.bfloat16)
    ffn_in_grad = weight_product(hidden_two_low, upward_low)
    two_grad = two_grad + input_product(upward_low, ffn_in)
    one_grad, cross_branch_grad, omega_cross_grad, gain_cross_grad, bias_cross_grad = pull_two(
        two_grad
    )
    cross_branch_low = cross_branch_grad.astype(jnp.bfloat16)
    cross_output_grad = weight_product(cross_low, cross_branch_low)
    cross_heads_grad = input_product(cross_branch_low, cross_output).astype(jnp.bfloat16)
    cross_delta = jnp.sum(
        split_heads(cross_heads_grad, head_count).astype(jnp.float32) * cross_heads, axis=-1
    )

    def cross_back(block_index, carry):
        query_grad, pair_grads = carry
        pairs = block_pairs(block_index)
        grads = attend_grads(
            cross_query_low,
            pairs[..., :model_width],
            pairs[..., model_width:],
            cross_heads_grad,
            cross_logsum,
            cross_delta,
            cross_mask(block_index),
            score_scale,
            head_count,
        )
        block_grads = jnp.concatenate((grads[1], grads[2]), axis=2)
        pair_grads = lax.dynamic_update_slice_in_dim(
            pair_grads, block_grads, block_index * key_block, 1
        )
        return (query_grad + grads[0], pair_grads)

    zero_grid = jnp.zeros((batch_rows, local_span, model_width), jnp.float32)
    cross_query_sum, pair_grads = lax.fori_loop(
        0,
        block_count,
        cross_back,
        (zero_grid, jnp.zeros((batch_rows, memory_total, 2 * model_width), jnp.float32)),
    )
    local_pair_grads = lax.psum_scatter(
        pair_grads.astype(jnp.bfloat16), "seq", scatter_dimension=1, tiled=True
    )
    memory_grad = input_product(local_pair_grads, cross_pair)
    pair_weight_grad = weight_product(memory, local_pair_grads)
    cross_query_low_grad = cross_query_sum.astype(jnp.bfloat16)
    cross_query_grad = weight_product(hidden_one_low, cross_query_low_grad)
    one_grad = one_grad + input_product(cross_query_low_grad, cross_query)
    target_residual_grad, self_branch_grad, omega_self_grad, gain_self_grad, bias_self_grad = (
        pull_one(one_grad)
    )
    self_branch_low = self_branch_grad.astype(jnp.bfloat16)
    self_output_grad = weight_product(self_low, self_branch_low)
    self_heads_grad = input_product(self_branch_low, self_output).astype(jnp.bfloat16)
    self_delta = jnp.sum(
        split_heads(self_heads_grad, head_count).astype(jnp.float32) * self_heads, axis=-1
    )

    def key_turn(step_index, carry):
        key_pair, grad_pair, query_grad = carry
        source = (self_index - step_index + axis_size) % axis_size

        def key_visit(inner):
            grads = attend_grads(
                query_low,
                key_pair[0],
                key_pair[1],
                self_heads_grad,
                self_logsum,
                self_delta,
                block_mask(self_index, source),
                score_scale,
                head_count,
            )
            return (inner[0] + grads[0], inner[1] + grads[1], inner[2] + grads[2])

        query_grad, key_grad, value_grad = lax.cond(
            source <= self_index,
            key_visit,
            lambda inner: inner,
            (query_grad, grad_pair[0], grad_pair[1]),
        )
        grad_pair = (
            shifted(key_grad.astype(jnp.bfloat16), "seq", 1).astype(key_grad.dtype),
            shifted(value_grad.astype(jnp.bfloat16), "seq", 1).astype(value_grad.dtype),
        )
        key_pair = from_behind((key_pair[0], key_pair[1]), "seq", 1)
        return (key_pair, grad_pair, query_grad)

    key_pair, grad_pair, query_grad = lax.fori_loop(
        0, axis_size, key_turn, ((key_low, value_low), (zero_grid, zero_grid), zero_grid)
    )
    key_grad, value_grad = grad_pair
    triple_grad_low = jnp.concatenate((query_grad, key_grad, value_grad), axis=2).astype(
        jnp.bfloat16
    )
    target_grad = target_residual_grad + input_product(triple_grad_low, self_triple)
    triple_weight_grad = weight_product(target, triple_grad_low)
    sums = lax.psum(
        (
            triple_weight_grad[:, :model_width],
            triple_weight_grad[:, model_width : 2 * model_width],
            triple_weight_grad[:, 2 * model_width :],
            self_output_grad,
            cross_query_grad,
            pair_weight_grad[:, :model_width],
            pair_weight_grad[:, model_width:],
            cross_output_grad,
            ffn_in_grad,
            ffn_out_grad,
            omega_self_grad,
            omega_cross_grad,
            omega_ffn_grad,
            gain_self_grad,
            bias_self_grad,
            gain_cross_grad,
            bias_cross_grad,
            gain_ffn_grad,
            bias_ffn_grad,
        ),
        ("rows", "seq"),
    )
    return (result.astype(jnp.bfloat16), target_grad, memory_grad) + tuple(sums)


MESH = pl.DeviceIdType.MESH
f32, bf16 = jnp.float32, jnp.bfloat16

def dot(a, b):
    return jnp.dot(a, b, preferred_element_type=f32)

def dot_t(a, b):
    return lax.dot_general(a, b, (((1,), (1,)), ((), ())), preferred_element_type=f32)

def t_dot(a, b):
    return lax.dot_general(a, b, (((0,), (0,)), ((), ())), preferred_element_type=f32)

def mult(i, m):
    return i if isinstance(i, int) else pl.multiple_of(i, m)

def attend_forward(first_block, blocks, keys, key, value_t, query_z, seen, scores, kept, kept_out, kept_sem, out_t, inverse, heads):
    count, piece, slots, queries = blocks * heads, 256, kept.shape[0], seen.shape[2]

    def head_place(i):
        block, head = first_block + i // heads, i % heads
        return block, head, pl.ds(mult(head * 64, 64), 64), pl.ds(mult(head // 2 * 128, 128), 128)

    def first(i, slot):
        block, head, _, pair = head_place(i)
        best = None
        for c in range(keys // piece):
            ks = pl.ds(c * piece, piece)
            s = dot(key[ks, pair], query_z[block, head]) + seen[block, ks]
            scores[slot, ks] = s
            top = jnp.max(s.reshape(piece // 8, 8, queries), axis=0)
            best = top if best is None else jnp.maximum(best, top)
        return best

    def out_copy(i):
        block, head, _, _ = head_place(i)
        return pltpu.make_async_copy(kept.at[i % slots, pl.ds(0, keys)], kept_out.at[block, head, pl.ds(0, keys)], kept_sem.at[i % slots])

    def second(i, slot, best):
        block, head, here, _ = head_place(i)
        best = jnp.max(best, axis=0, keepdims=True)
        total = out = None
        for c in range(keys // piece):
            ks = pl.ds(c * piece, piece)
            p = jnp.exp(scores[slot, ks] - best)
            part = jnp.sum(p.reshape(piece // 8, 8, queries), axis=0)
            total = part if total is None else total + part
            p = p.astype(bf16)
            kept[i % slots, ks] = p
            part = dot(value_t[here, ks], p)
            out = part if out is None else out + part
        scale = 1.0 / jnp.sum(total, axis=0, keepdims=True)
        out_t[block, here, :] = (out * scale).astype(bf16)
        inverse[block, head] = jnp.broadcast_to(scale, (8, queries))

    def body(j, best):
        i = 2 * j
        for e in range(2):
            pl.when(i + e >= slots)(lambda e=e: out_copy(i + e - slots).wait())
        later = first(i + 1, 1)
        second(i, 0, best)
        best = first(jnp.minimum(i + 2, count - 1), 0)
        second(i + 1, 1, later)
        out_copy(i).start()
        out_copy(i + 1).start()
        return best

    lax.fori_loop(0, count // 2, body, first(0, 0))
    for i in range(count - slots, count):
        out_copy(i).wait()

def norm_parts(pre):
    centred = pre - jnp.mean(pre, axis=-1, keepdims=True)
    rstd = lax.rsqrt(jnp.mean(centred * centred, axis=-1, keepdims=True) + 1e-05)
    return centred * rstd, rstd

def pad_pairs(query, query_z, row, heads):
    turned = query.T
    half = lax.broadcasted_iota(jnp.int32, (128, query.shape[0]), 0) // 64
    for head in range(heads):
        pair = turned[head // 2 * 128 : head // 2 * 128 + 128]
        query_z[row, head] = jnp.where(half == head % 2, pair, jnp.zeros_like(pair))

class ForwardIn(NamedTuple):
    target: object
    memory: object
    target_segments: object
    memory_segments: object
    self_query: object
    self_key: object
    self_value: object
    self_output: object
    cross_query: object
    cross_key: object
    cross_value: object
    cross_output: object
    ffn_in: object
    ffn_out: object
    omega_self: object
    omega_cross: object
    omega_ffn: object
    gain_self: object
    bias_self: object
    gain_cross: object
    bias_cross: object
    gain_ffn: object
    bias_ffn: object
    cotangent: object

class ForwardOut(NamedTuple):
    output_blocks: object
    target_all: object
    memory_all: object
    self_kept: object
    cross_kept: object
    self_inverse: object
    cross_inverse: object
    self_out: object
    cross_out: object
    self_q: object
    cross_q: object
    one_low: object
    one_hat: object
    one_rstd: object
    two_low: object
    two_hat: object
    two_rstd: object
    active: object
    upward_grad: object
    branch_grad: object
    two_grad: object
    sums: object

class ForwardScratch(NamedTuple):
    key: object
    value_t: object
    query_z: object
    seen_self: object
    seen_cross: object
    scores: object
    kept: object
    mem_key: object
    mem_value_t: object
    wide: object
    slope: object
    one: object
    two: object
    value_turned: object
    mem_value_turned: object
    grads: object

FORWARD_NAMES = ForwardIn._fields + ForwardOut._fields
MATRICES = ForwardIn._fields[4:14]
VECTORS = ForwardIn._fields[14:23]

def forward_kernel(heads, *refs):
    hbm = SimpleNamespace(**dict(zip(FORWARD_NAMES, refs)))
    own = refs[len(FORWARD_NAMES):-5]
    r = SimpleNamespace(**dict(zip(FORWARD_NAMES[2:4] + VECTORS + MATRICES + ForwardOut._fields + ForwardScratch._fields,
        refs[2:4] + refs[14:23] + own)))
    send, recv, local, load_sem, out_sem = refs[-5:]
    kept_sem = local
    me_r, me_s = lax.axis_index("rows"), lax.axis_index("seq")
    core, side = me_s % 2, me_s // 2
    length, width = r.target_all.shape
    tokens = r.one_low.shape[0]
    blocks = 2
    span = tokens // blocks
    other_core, other_side = me_s + 1 - 2 * core, me_s + 2 - 4 * side

    def place(i):
        return pl.ds(mult(i * span, span), span)

    def remote(src, dst, k, to):
        return pltpu.make_async_remote_copy(src_ref=src, dst_ref=dst, send_sem=send.at[k], recv_sem=recv.at[k],
            device_id=(me_r, to), device_id_type=MESH)

    def share(source, full, k):
        mine, theirs = full.at[place(me_s)], full.at[place(other_side)]
        return (pltpu.make_async_copy(source.at[side], mine, load_sem.at[10 + k // 3]), remote(source.at[1 - side], mine, k, other_side),
            remote(source.at[side], mine, k + 1, other_core), remote(theirs, theirs, k + 2, other_core))

    x_own, x_side, x_core, x_pass = share(hbm.target, r.target_all, 0)
    m_own, m_side, m_core, m_pass = share(hbm.memory, r.memory_all, 3)
    g_own = pltpu.make_async_copy(hbm.cotangent.at[side], r.grads.at[side], load_sem.at[12])
    g_side = remote(hbm.cotangent.at[1 - side], r.grads.at[side], 6, other_side)
    x_own.start()
    m_own.start()
    loads = {k: pltpu.make_async_copy(getattr(hbm, k), getattr(r, k), load_sem.at[i]) for i, k in enumerate(MATRICES)}
    for copy in loads.values():
        copy.start()
    g_own.start()
    loads = SimpleNamespace(**loads)
    outs = []

    def emit(*names):
        for k in names:
            copy = pltpu.make_async_copy(getattr(r, k), getattr(hbm, k), out_sem.at[len(outs)])
            copy.start()
            outs.append(copy)

    barrier = pltpu.get_barrier_semaphore()
    for to in (other_core, other_side):
        pl.semaphore_signal(barrier, inc=1, device_id=(me_r, to), device_id_type=MESH)
    pl.semaphore_wait(barrier, 2)
    x_side.start()
    x_core.start()
    m_core.start()

    def masks():
        def line(ids, at):
            first, second = ids[0:1, at], ids[1:2, at]
            return (first + (second - first) * side).astype(f32)
        mine = [line(r.target_segments, pl.ds(mult((2 * b + core) * span, span), span)) for b in range(blocks)]
        for c in range(length // 128):
            at = pl.ds(c * 128, 128)
            key_place = c * 128 + lax.broadcasted_iota(jnp.int32, (128, span), 0)
            query_place = lax.broadcasted_iota(jnp.int32, (128, span), 1)
            for ids, seen, causal in ((r.target_segments, r.seen_self, True), (r.memory_segments, r.seen_cross, False)):
                column = jnp.broadcast_to(line(ids, at), (128, 128)).T
                column = jnp.concatenate([column] * (span // 128), axis=1)
                for b in range(blocks):
                    if causal and c * 128 >= (b + 1) * length // 2:
                        continue
                    same = column == mine[b]
                    if causal:
                        same = same & (key_place <= query_place + (2 * b + core) * span)
                    seen[b, at] = jnp.where(same, 0.0, -1e30)

    def project(full, key_weight, turned, key, value_t, block):
        at = place(block)
        here = full[at]
        key[at] = dot(here, key_weight[...]).astype(bf16)
        value_t[:, at] = dot_t(turned[...], here).astype(bf16)

    def project_self(block):
        project(r.target_all, r.self_key, r.value_turned, r.key, r.value_t, block)

    def project_cross(block):
        project(r.memory_all, r.cross_key, r.mem_value_turned, r.mem_key, r.mem_value_t, block)

    def queries(low, weight, out):
        for b in range(blocks):
            query = (dot(low(b), weight[...]).astype(bf16) * 0.125).astype(bf16)
            out[b] = query
            pad_pairs(query, r.query_z, b, heads)

    masks()
    for k in (loads.self_query, loads.self_key, loads.self_value, loads.cross_key, loads.cross_value):
        k.wait()
    r.value_turned[...] = r.self_value[...].T
    r.mem_value_turned[...] = r.cross_value[...].T
    x_own.wait()
    project_self(me_s)
    x_core.wait()
    project_self(other_core)
    x_side.wait()
    x_pass.start()
    m_side.start()
    queries(lambda b: r.target_all[place(2 * b + core)], r.self_query, r.self_q)
    project_self(other_side)
    m_own.wait()
    project_cross(me_s)
    x_pass.wait()
    project_self(other_side + 1 - 2 * core)
    m_core.wait()
    project_cross(other_core)
    emit(*ForwardOut._fields[1:2], *ForwardOut._fields[9:10])

    def attend(first_block, count, keys, key, value_t, seen, kept_out, out_t, inverse):
        attend_forward(first_block, count, keys, key, value_t, r.query_z, seen, r.scores, r.kept, kept_out, kept_sem, out_t, inverse, heads)

    attend(0, 1, length // 2, r.key, r.value_t, r.seen_self, hbm.self_kept, r.self_out, r.self_inverse)
    m_side.wait()
    m_pass.start()
    g_side.start()
    attend(1, 1, length, r.key, r.value_t, r.seen_self, hbm.self_kept, r.self_out, r.self_inverse)
    loads.self_output.wait()
    vec = [getattr(r, k)[...].reshape(1, width) for k in VECTORS]
    part = 128
    for b in range(blocks):
        r.wide[pl.ds(b * span, span)] = t_dot(r.self_out[b], r.self_output[...])

    @pl.loop(0, tokens // part)
    def _(i):
        at = pl.ds(mult(i * part, part), part)
        b, inner = i // (span // part), i % (span // part)
        x = r.target_all[pl.ds(mult((2 * b + core) * span + inner * part, part), part)].astype(f32)
        hat, rstd = norm_parts(x * vec[0] + r.wide[at])
        one = hat * vec[3] + vec[4]
        r.one_hat[at] = hat
        r.one_rstd[at] = jnp.broadcast_to(rstd, (part, 128))
        r.one[at] = one
        r.one_low[at] = one.astype(bf16)

    loads.cross_query.wait()
    queries(lambda b: r.one_low[pl.ds(b * span, span)], r.cross_query, r.cross_q)
    project_cross(other_side)
    m_pass.wait()
    project_cross(other_side + 1 - 2 * core)
    emit(*ForwardOut._fields[2:3], *ForwardOut._fields[5:6], *ForwardOut._fields[7:8], *ForwardOut._fields[10:14])
    attend(0, 2, length, r.mem_key, r.mem_value_t, r.seen_cross, hbm.cross_kept, r.cross_out, r.cross_inverse)
    loads.cross_output.wait()
    for b in range(blocks):
        r.wide[pl.ds(b * span, span)] = t_dot(r.cross_out[b], r.cross_output[...])

    @pl.loop(0, tokens // part)
    def _(i):
        at = pl.ds(mult(i * part, part), part)
        hat, rstd = norm_parts(r.one[at] * vec[1] + r.wide[at])
        two = hat * vec[5] + vec[6]
        r.two_hat[at] = hat
        r.two_rstd[at] = jnp.broadcast_to(rstd, (part, 128))
        r.two[at] = two
        r.two_low[at] = two.astype(bf16)

    emit(*ForwardOut._fields[6:7], *ForwardOut._fields[8:9], *ForwardOut._fields[14:17])
    loads.ffn_in.wait()
    loads.ffn_out.wait()
    c0 = math.sqrt(2.0 / math.pi)
    pieces = r.ffn_in.shape[1] // 512
    r.wide[...] = jnp.zeros_like(r.wide)

    @pl.loop(0, pieces)
    def _(j):
        cols = pl.ds(mult(j * 512, 512), 512)
        for half in range(2):
            at = pl.ds(half * (tokens // 2), tokens // 2)
            u = dot(r.two_low[at], r.ffn_in[:, cols])
            square = u * u
            t = jnp.tanh(c0 * u * (1.0 + 0.044715 * square))
            active = (0.5 * u * (1.0 + t)).astype(bf16)
            r.active[at, cols] = active
            r.slope[at, cols] = (0.5 * (1.0 + t) + (0.5 * c0) * u * (1.0 - t * t) * (1.0 + (3 * 0.044715) * square)).astype(bf16)
            r.wide[at] += dot(active, r.ffn_out[cols, :])

    emit(*ForwardOut._fields[17:18])
    g_own.wait()
    g_side.wait()
    r.sums[...] = jnp.zeros_like(r.sums)

    @pl.loop(0, tokens // part)
    def _(i):
        at = pl.ds(mult(i * part, part), part)
        b, inner = i // (span // part), i % (span // part)
        near = pl.ds(mult(inner * part, part), part)
        two = r.two[at]
        hat, rstd = norm_parts(two * vec[2] + r.wide[at])
        r.output_blocks[b, near] = (hat * vec[7] + vec[8]).astype(bf16)
        grad = r.grads[b, near].astype(f32)
        scaled = grad * vec[7]
        back = rstd * (scaled - jnp.mean(scaled, axis=-1, keepdims=True) - hat * jnp.mean(scaled * hat, axis=-1, keepdims=True))
        r.branch_grad[at] = back.astype(bf16)
        r.two_grad[at] = back * vec[2]
        r.sums[0] += jnp.sum((back * two).reshape(part // 8, 8, width), axis=0)
        r.sums[1] += jnp.sum((grad * hat).reshape(part // 8, 8, width), axis=0)
        r.sums[2] += jnp.sum(grad.reshape(part // 8, 8, width), axis=0)

    emit(*ForwardOut._fields[:1], *ForwardOut._fields[19:])

    @pl.loop(0, pieces)
    def _(j):
        cols = pl.ds(mult(j * 512, 512), 512)
        for half in range(2):
            at = pl.ds(half * (tokens // 2), tokens // 2)
            grad = dot_t(r.branch_grad[at], r.ffn_out[cols, :])
            r.upward_grad[at, cols] = (grad * r.slope[at, cols].astype(f32)).astype(bf16)

    emit(*ForwardOut._fields[18:19])
    for copy in outs:
        copy.wait()

def forward_call(target, memory, target_segments, memory_segments, matrices, vectors, cotangent, heads=8):
    blocks, span, width = target.shape
    length = target_segments.shape[1]
    tokens = blocks * span
    hidden = matrices[8].shape[1]
    any_, vm = pl.BlockSpec(memory_space=pl.ANY), pl.BlockSpec(memory_space=pltpu.VMEM)
    s = jax.ShapeDtypeStruct
    full, wide, seen = ((length, width), bf16), ((tokens, width), f32), ((blocks, length, span), f32)
    kept, inverse = s((blocks, heads, length, span), bf16), s((blocks, heads, 8, span), f32)
    outs = ForwardOut(output_blocks=s((blocks, span, width), bf16), target_all=s(*full), memory_all=s(*full),
        self_kept=kept, cross_kept=kept, self_inverse=inverse, cross_inverse=inverse,
        self_out=s((blocks, width, span), bf16), cross_out=s((blocks, width, span), bf16),
        self_q=s((blocks, span, width), bf16), cross_q=s((blocks, span, width), bf16),
        one_low=s((tokens, width), bf16), one_hat=s(*wide), one_rstd=s((tokens, 128), f32),
        two_low=s((tokens, width), bf16), two_hat=s(*wide), two_rstd=s((tokens, 128), f32),
        active=s((tokens, hidden), bf16), upward_grad=s((tokens, hidden), bf16), branch_grad=s((tokens, width), bf16),
        two_grad=s(*wide), sums=s((3, 8, width), f32))
    turned = ((width, length), bf16)
    scratch = ForwardScratch(key=full, value_t=turned, query_z=((blocks, heads, 128, span), bf16),
        seen_self=seen, seen_cross=seen, scores=((2, length, span), f32),
        kept=((4, length, span), bf16), mem_key=full, mem_value_t=turned,
        wide=wide, slope=((tokens, hidden), bf16), one=wide, two=wide,
        value_turned=((width, width), bf16), mem_value_turned=((width, width), bf16), grads=((blocks, span, width), bf16))
    held = [((8, 128), f32) if k in ForwardOut._fields[3:5] else (o.shape, o.dtype) for k, o in zip(ForwardOut._fields, outs)]
    held = [(m.shape, m.dtype) for m in matrices] + held + list(scratch)
    dma = pltpu.SemaphoreType.DMA
    return ForwardOut(*pl.pallas_call(
        functools.partial(forward_kernel, heads),
        out_shape=list(outs),
        in_specs=[any_] * 2 + [vm] * 2 + [any_] * 10 + [vm] * 9 + [any_],
        out_specs=[any_] * len(outs),
        scratch_shapes=[pltpu.VMEM(*k) for k in held] + [dma((7,)), dma((7,)), dma((4,)), dma((13,)), dma((20,))],
        compiler_params=pltpu.CompilerParams(collective_id=0, has_side_effects=True, vmem_limit_bytes=62 << 20),
        name="forward",
    )(target, memory, target_segments, memory_segments, *matrices, *vectors, cotangent))

CLASSES = (1, 4, 0, 1, 4, 4, 0, 5, 1, 4, 1, 1, 3, 0, 1, 0)
PLAN = (
    (0,),
    (19, 1),
    (),
    (),
    (2, 4),
    (0,),
    (1, 3, 6),
    (7,),
    (2, 4, 3, 6, 7),
    (19, 1, 5),
    (),
    (),
    (),
    (2, 1, 5, 0),
    (4, 3),
    (7, 1, 6),
    (2, 4, 8, 1),
    (5,),
    (7, 6),
    (0, 1, 2, 8),
    (16, 4, 9, 3),
    (),
    (18, 5, 11, 7, 10),
    (12,),
    (6,),
    (16, 8, 18, 7, 4, 9, 1, 2, 11, 0, 10, 3),
    (12, 7, 5, 8, 6),
    (2, 1, 3, 0),
    (9,),
    (16, 18, 4, 12),
    (7, 13),
    (1, 8),
    (14, 6),
    (17, 18, 2, 3, 1, 13, 11, 14, 0),
    (15, 9, 10, 5, 4, 17, 2, 15, 12, 13, 7, 8, 14, 6, 5, 11, 18, 10, 3, 0, 9, 2, 4, 8, 17, 5, 12, 11, 2, 15, 18, 13, 10, 14, 8, 3, 5, 7, 11, 0, 13, 6, 10, 9, 14, 7, 11, 15, 4, 13, 12, 10, 14, 8, 11, 4, 3, 15, 13, 10, 14, 5, 3, 15, 0, 13, 9, 14, 5, 6, 0, 15, 12, 8, 9, 11, 6, 13, 15, 12, 10, 8, 14, 9, 11, 13, 15, 12, 11, 13, 9, 10, 9, 12, 15, 10, 14, 12, 15, 14),
)

class Reduction:
    def __init__(self, block, near, landed, reduced, send, recv, own):
        self.block, self.near, self.landed, self.reduced = block, near, landed, reduced
        self.send, self.recv, self.own = send, recv, own
        self.r, self.s = lax.axis_index("rows"), lax.axis_index("seq")
        self.core, self.y = self.s % 2, self.s // 2
        self.x, self.z0, self.z1 = self.r % 2, (self.r // 2) % 2, self.r // 4
        self.count, self.size = block.shape[0], block.shape[1]
        x, y, z0, z1 = self.x, self.y, self.z0, self.z1
        core, ax, ay = (0, 1 - 2 * self.core, self.core), (1 - 2 * x, 0, x), (0, 2 - 4 * y, y)
        an, af = (2 - 4 * z0, 0, z0), (4 - 8 * z1, 0, z1)
        self.orders = ((core, ax, ay, an, af), (core, ay, ax, an, af), (core, an, af, ax, ay), (core, an, af, ay, ax), (core, ax, an, af, ay), (core, ay, an, af, ax))
        self.flows, self.turn, done = {}, 0, {}
        self.polls = []
        for entry in PLAN:
            self.polls.append([(c, done.setdefault(c, []).append(0) or len(done[c]) - 1) for c in entry])

    def partners(self):
        r, s = self.r, self.s
        return ((r, s + 1 - 2 * self.core), (r, s + 2 - 4 * self.y), (r + 1 - 2 * self.x, s),
                (r + 2 - 4 * self.z0, s), (r + 4 - 8 * self.z1, s))

    def start_of(self, j, hops):
        off = 0
        for i in range(j):
            off = off + hops[i][2] * (self.size >> (i + 1))
        return off

    def landing(self, c, j):
        half = self.size >> (j + 1)
        if j == 0:
            return self.near.at[c]
        return self.landed.at[c, pl.ds(self.size // 2 - (self.size >> j), half)]

    def copy(self, c, j, gather):
        hops = self.orders[CLASSES[c]]
        off, half = self.start_of(j, hops), self.size >> (j + 1)
        dr, ds, bit = hops[j]
        if gather:
            mine = pl.ds(pl.multiple_of(off + bit * half, 16), half)
            src, dst = (self.block if j == 4 else self.reduced).at[c, mine], self.reduced.at[c, mine]
        else:
            src, dst = self.block.at[c, pl.ds(pl.multiple_of(off + (1 - bit) * half, 16), half)], self.landing(c, j)
        return pltpu.make_async_remote_copy(src_ref=src, dst_ref=dst, send_sem=self.send.at[c],
            recv_sem=self.recv.at[c, j + 5 * gather], device_id=(self.r + dr, self.s + ds), device_id_type=MESH)

    def own_copy(self, c):
        mine = pl.ds(pl.multiple_of(self.start_of(5, self.orders[CLASSES[c]]), 16), self.size >> 5)
        return pltpu.make_async_copy(self.block.at[c, mine], self.reduced.at[c, mine], self.own.at[c])

    def add(self, c, j):
        keep = pl.ds(pl.multiple_of(self.start_of(j + 1, self.orders[CLASSES[c]]), 16), self.size >> (j + 1))
        self.block[c, keep] = (self.block[c, keep].astype(f32) + self.landing(c, j)[...].astype(f32)).astype(bf16)

    def step(self, c, s):
        if c >= self.count:
            return self.flows[c](s)
        if 1 <= s <= 5:
            self.copy(c, s - 1, 0).wait()
            self.add(c, s - 1)
        elif s > 5:
            self.copy(c, 10 - s, 1).wait()
        if s == 5:
            self.own_copy(c).start()
        elif s == 6:
            self.own_copy(c).wait()
        if s <= 4:
            self.copy(c, s, 0).start()
        elif s <= 9:
            self.copy(c, 9 - s, 1).start()

    def poll(self, index=None):
        if index is None:
            index = self.turn
            self.turn += 1
        for c, s in self.polls[index]:
            self.step(c, s)

    def poll_loop(self, base, count, i):
        for k in range(count):
            if self.polls[base + k]:
                @pl.when(i == k)
                def _():
                    self.poll(base + k)

class Loads(NamedTuple):
    active: object
    branch_grad: object
    two_low: object
    upward_grad: object
    ffn_in: object
    two_grad: object
    two_hat: object
    two_rstd: object
    one_hat: object
    one_rstd: object
    cross_output: object
    cross_out: object
    cross_inverse: object
    memory_all: object
    cross_key: object
    cross_value: object
    cross_q: object
    one_low: object
    cross_query: object
    target_all: object
    self_output: object
    self_out: object
    self_inverse: object
    self_key: object
    self_value: object
    self_q: object
    self_query: object
    sums: object

class BackOut(NamedTuple):
    output: object
    reduced: object
    target_grad: object
    memory_grad: object
    vector_grads: object

class BackScratch(NamedTuple):
    block: object
    near: object
    landed: object
    key_t: object
    value: object
    key_grad: object
    value_grad: object
    score_grad: object
    kept: object
    part: object
    part_core: object
    part_side: object
    query_grad_t: object
    query_grad: object
    branch_low: object
    out_grad_t: object
    out_grad: object
    delta: object
    vec: object
    vec_landed: object
    acc: object
    output_own: object

LOADS = Loads._fields
UNLOADED = ForwardOut._fields[3:5] + ForwardOut._fields[:1] + VECTORS

def backward_kernel(heads, *refs):
    n = len(LOADS + UNLOADED)
    hbm = SimpleNamespace(**dict(zip(LOADS + UNLOADED, refs)))
    r = SimpleNamespace(**dict(zip(BackOut._fields + LOADS + BackScratch._fields, refs[n:])))
    load_sem, kept_sem, send, recv, own_sem, part_send, part_recv, vec_send, vec_recv, out_sem = refs[-10:]
    length, width = r.memory_all.shape
    tokens = r.two_low.shape[0]
    blocks = 2
    span = tokens // blocks
    red = Reduction(r.block, r.near, r.landed, r.reduced, send, recv, own_sem)
    me_r, me_s, core, side = red.r, red.s, red.core, red.y

    loads = Loads(*[pltpu.make_async_copy(getattr(hbm, k), getattr(r, k), load_sem.at[i]) for i, k in enumerate(LOADS)])
    for copy in loads:
        copy.start()

    def need(*copies):
        for copy in copies:
            copy.wait()

    barrier = pltpu.get_barrier_semaphore()
    for to in red.partners():
        pl.semaphore_signal(barrier, inc=1, device_id=to, device_id_type=MESH)
    pl.semaphore_wait(barrier, 5)

    def block_at(b):
        return pl.ds(b * span, span)

    def place(i):
        return pl.ds(mult(i * span, span), span)

    def ffn_block(c):
        if c < 4:
            r.block[c] = t_dot(r.active[:, pl.ds(c * 512, 512)], r.branch_grad[...]).astype(bf16)
        else:
            r.block[c] = t_dot(r.two_low[...], r.upward_grad[:, pl.ds((c - 4) * 512, 512)]).astype(bf16)

    vec = [getattr(hbm, k)[...].reshape(1, width) for k in VECTORS]
    part = 128

    def norm_back(grad_ref, hat_ref, rstd_ref, gain, omega, previous, slot):
        for i in range(3):
            r.acc[slot + i] = jnp.zeros_like(r.acc[slot + i])

        @pl.loop(0, tokens // part)
        def _(i):
            at = pl.ds(mult(i * part, part), part)
            hat, grad = hat_ref[at], grad_ref[at]
            scaled = grad * gain
            back = rstd_ref[at][:, 0:1] * (scaled - jnp.mean(scaled, axis=-1, keepdims=True)
                - hat * jnp.mean(scaled * hat, axis=-1, keepdims=True))
            r.branch_low[at] = back.astype(bf16)
            grad_ref[at] = back * omega
            for k, term in enumerate((back * previous(i), grad * hat, grad)):
                r.acc[slot + k] += jnp.sum(term.reshape(part // 8, 8, width), axis=0)

    def attention_start(weight, out_t, inverse):
        for b in range(blocks):
            grad_t = dot_t(weight[...], r.branch_low[block_at(b)])
            for head in range(heads):
                here = pl.ds(head * 64, 64)
                scaled = grad_t[head * 64 : head * 64 + 64] * inverse[b, head][0:1]
                r.out_grad_t[b, here] = scaled.astype(bf16)
                delta = jnp.sum(scaled * out_t[b, here].astype(f32), axis=0, keepdims=True)
                r.delta[b, head] = jnp.broadcast_to(delta, (8, span))
            r.out_grad[b] = r.out_grad_t[b].T

    def keys_again(full, key_weight, value_weight):
        key_turned = key_weight[...].T
        for c in range(length // 512):
            at = pl.ds(c * 512, 512)
            here = full[at]
            r.key_t[:, at] = dot_t(key_turned, here).astype(bf16)
            r.value[at] = dot(here, value_weight[...]).astype(bf16)

    def attention_back(kept_hbm, query, spans):
        base = red.turn
        pairs, piece = heads // 2, 256
        red.turn += pairs
        tiles = [(b, e) for b in range(blocks) for e in range(2)]
        top = lax.broadcasted_iota(jnp.int32, (128, span), 0) // 64
        left = lax.broadcasted_iota(jnp.int32, (span, 128), 1) // 64

        def pair_at(j):
            return pl.ds(mult(j * 128, 128), 128)

        def fetch(j, b, e):
            slot, ks = j % 3 * 4 + b * 2 + e, pl.ds(0, spans[b])
            return pltpu.make_async_copy(kept_hbm.at[b, 2 * j + e, ks], r.kept.at[slot, ks], kept_sem.at[slot])

        def first(j):
            for b, e in tiles:
                fetch(j, b, e).wait()
            for b, e in tiles:
                grad = jnp.where(top == e, r.out_grad_t[b, pair_at(j), :], jnp.zeros((128, span), bf16))
                delta = r.delta[b, 2 * j + e][0:1]
                for c in range(spans[b] // piece):
                    ks = pl.ds(c * piece, piece)
                    p_grad = dot(r.value[ks, pair_at(j)], grad)
                    r.score_grad[j % 2 * 4 + b * 2 + e, ks] = (r.kept[j % 3 * 4 + b * 2 + e, ks].astype(f32) * (p_grad - delta)).astype(bf16)

        def second(j):
            none = jnp.zeros((span, 128), bf16)
            qs = [jnp.where(left == e, query[b, :, pair_at(j)], none) for b, e in tiles]
            gs = [jnp.where(left == e, r.out_grad[b, :, pair_at(j)], none) for b, e in tiles]
            out = [None] * len(tiles)
            for c in range(length // piece):
                ks = pl.ds(c * piece, piece)
                v_grad = k_grad = None
                for i, (b, e) in enumerate(tiles):
                    if c * piece >= spans[b]:
                        continue
                    ds = r.score_grad[j % 2 * 4 + i, ks]
                    v, k = dot(r.kept[j % 3 * 4 + i, ks], gs[i]), dot(ds, qs[i])
                    v_grad, k_grad = (v, k) if v_grad is None else (v_grad + v, k_grad + k)
                    a = dot(r.key_t[pl.ds(mult(j * 128 + e * 64, 64), 64), ks], ds)
                    out[i] = a if out[i] is None else out[i] + a
                r.value_grad[ks, pair_at(j)] = v_grad.astype(bf16)
                r.key_grad[ks, pair_at(j)] = k_grad.astype(bf16)
            for i, (b, e) in enumerate(tiles):
                r.query_grad_t[b, pl.ds(mult(j * 128 + e * 64, 64), 64), :] = (out[i] * 0.125).astype(bf16)

        for j in range(2):
            for b, e in tiles:
                fetch(j, b, e).start()
        first(0)

        @pl.loop(0, pairs - 1)
        def _(j):
            @pl.when(j + 2 < pairs)
            def _():
                for b, e in tiles:
                    fetch(j + 2, b, e).start()
            first(j + 1)
            second(j)
            red.poll_loop(base, pairs - 1, j)
        second(pairs - 1)
        red.poll(base + pairs - 1)
        for b in range(blocks):
            r.query_grad[b] = r.query_grad_t[b].T

    def pair_product(key_weight, value_weight):
        for i in range(length // span):
            at = block_at(i)
            r.part[i] = (dot_t(r.key_grad[at], key_weight[...]) + dot_t(r.value_grad[at], value_weight[...])).astype(bf16)

    def part_copy(k, src, dst, to):
        return pltpu.make_async_remote_copy(src_ref=src, dst_ref=dst, send_sem=part_send.at[k], recv_sem=part_recv.at[k],
            device_id=(me_r, to), device_id_type=MESH)

    def part_flow(turn, out, rest):
        to_core, to_side = me_s + 1 - 2 * core, me_s + 2 - 4 * side
        far, near = 1 - side, side
        copies = (part_copy(3 * turn, r.part.at[2 * far + 1 - core], r.part_core.at[turn, 0], to_core),
            part_copy(3 * turn + 1, r.part.at[2 * near + 1 - core], r.part_core.at[turn, 1], to_core),
            part_copy(3 * turn + 2, r.part_core.at[turn, 0], r.part_side.at[turn], to_side))

        def step(s):
            if s == 0:
                copies[0].start()
                copies[1].start()
            elif s == 1:
                copies[0].wait()
                r.part_core[turn, 0] = (r.part[2 * far + core].astype(f32) + r.part_core[turn, 0].astype(f32) + rest(far)).astype(bf16)
                copies[2].start()
                copies[1].wait()
                out[near] = r.part[2 * near + core].astype(f32) + r.part_core[turn, 1].astype(f32) + rest(near)
            else:
                copies[2].wait()
                out[far] = r.part_side[turn].astype(f32)
        return step

    def output_flow(s):
        there = pltpu.make_async_remote_copy(src_ref=hbm.output_blocks.at[1 - side], dst_ref=r.output.at[side], send_sem=part_send.at[6],
            recv_sem=part_recv.at[6], device_id=(me_r, me_s + 2 - 4 * side), device_id_type=MESH)
        if s == 0:
            there.start()
            pltpu.make_async_copy(hbm.output_blocks.at[side], r.output_own, out_sem.at[0]).start()
        else:
            there.wait()
            pltpu.make_async_copy(hbm.output_blocks.at[side], r.output_own, out_sem.at[0]).wait()
            pltpu.make_async_copy(r.output_own, r.output.at[side], out_sem.at[1]).start()

    def vec_copy(k):
        return pltpu.make_async_remote_copy(src_ref=r.vec, dst_ref=r.vec_landed.at[k], send_sem=vec_send.at[k],
            recv_sem=vec_recv.at[k], device_id=red.partners()[k], device_id_type=MESH)

    def vec_flow(s):
        if s >= 1:
            vec_copy(s - 1).wait()
            r.vec[...] += r.vec_landed[s - 1]
        if s <= 4:
            vec_copy(s).start()
        else:
            r.vector_grads[...] = r.vec[...]

    red.flows = {16: part_flow(0, r.memory_grad, lambda b: 0.0), 18: vec_flow, 19: output_flow,
        17: part_flow(1, r.target_grad, lambda b: r.two_grad[place(b)])}

    need(loads.active, loads.branch_grad)
    for c in range(8):
        if c == 4:
            need(loads.two_low, loads.upward_grad)
        ffn_block(c)
        red.poll()
    need(loads.ffn_in, loads.two_grad)

    @pl.loop(0, tokens // 128)
    def _(i):
        at = pl.ds(mult(i * 128, 128), 128)
        r.two_grad[at] += dot_t(r.upward_grad[at], r.ffn_in[...])
    red.poll()
    need(loads.two_hat, loads.two_rstd, loads.one_hat, loads.one_rstd, loads.cross_output, loads.cross_out, loads.cross_inverse)
    norm_back(r.two_grad, r.two_hat, r.two_rstd, vec[5], vec[1], lambda i: r.one_hat[pl.ds(mult(i * part, part), part)] * vec[3] + vec[4], 0)
    red.poll()
    r.block[8] = sum(dot(r.cross_out[b], r.branch_low[block_at(b)]) for b in range(blocks)).astype(bf16)
    red.poll()
    attention_start(r.cross_output, r.cross_out, r.cross_inverse)
    red.poll()
    need(loads.memory_all, loads.cross_key, loads.cross_value, loads.cross_q)
    keys_again(r.memory_all, r.cross_key, r.cross_value)
    red.poll()
    attention_back(hbm.cross_kept, r.cross_q, (length, length))
    r.block[9] = t_dot(r.memory_all[...], r.key_grad[...]).astype(bf16)
    red.poll()
    r.block[10] = t_dot(r.memory_all[...], r.value_grad[...]).astype(bf16)
    red.poll()
    need(loads.one_low, loads.cross_query)
    r.block[11] = sum(t_dot(r.one_low[block_at(b)], r.query_grad[b]) for b in range(blocks)).astype(bf16)
    red.poll()
    pair_product(r.cross_key, r.cross_value)
    red.poll()
    for b in range(blocks):
        r.two_grad[block_at(b)] += dot_t(r.query_grad[b], r.cross_query[...])
    red.poll()
    need(loads.target_all, loads.self_output, loads.self_out, loads.self_inverse, loads.self_key, loads.self_value, loads.self_q,
        loads.self_query, loads.sums)
    def own_target(i):
        b, inner = i // (span // part), i % (span // part)
        return r.target_all[pl.ds(mult((2 * b + core) * span + inner * part, part), part)].astype(f32)
    norm_back(r.two_grad, r.one_hat, r.one_rstd, vec[3], vec[0], own_target, 3)
    for i in range(3):
        r.vec[pl.ds(i, 1)] = jnp.sum(r.acc[3 + i], axis=0, keepdims=True)
        r.vec[pl.ds(3 + i, 1)] = jnp.sum(r.acc[i], axis=0, keepdims=True)
        r.vec[pl.ds(6 + i, 1)] = jnp.sum(r.sums[i], axis=0, keepdims=True)
    r.vec[pl.ds(9, 7)] = jnp.zeros((7, width), f32)
    red.poll()
    r.block[12] = sum(dot(r.self_out[b], r.branch_low[block_at(b)]) for b in range(blocks)).astype(bf16)
    red.poll()
    attention_start(r.self_output, r.self_out, r.self_inverse)
    red.poll()
    keys_again(r.target_all, r.self_key, r.self_value)
    red.poll()
    attention_back(hbm.self_kept, r.self_q, (length // 2, length))
    r.block[13] = t_dot(r.target_all[...], r.key_grad[...]).astype(bf16)
    red.poll()
    r.block[14] = t_dot(r.target_all[...], r.value_grad[...]).astype(bf16)
    red.poll()
    r.block[15] = sum(t_dot(r.target_all[place(2 * b + core)], r.query_grad[b]) for b in range(blocks)).astype(bf16)
    red.poll()
    pair_product(r.self_key, r.self_value)
    for b in range(blocks):
        r.two_grad[block_at(b)] += dot_t(r.query_grad[b], r.self_query[...])
    red.poll()
    red.poll()
    pltpu.make_async_copy(r.output_own, r.output.at[side], out_sem.at[1]).wait()

def backward_call(o, matrices, vectors, heads=8):
    length, width = o.target_all.shape
    tokens, hidden = o.active.shape
    blocks = o.self_kept.shape[0]
    span = tokens // blocks
    any_, vm = pl.BlockSpec(memory_space=pl.ANY), pl.BlockSpec(memory_space=pltpu.VMEM)
    s = jax.ShapeDtypeStruct
    operands = dict(o._asdict(), **dict(zip(MATRICES + VECTORS, matrices + vectors)))
    count = 8 + 2 * hidden // 512
    outs = BackOut(output=s((blocks, span, width), bf16), reduced=s((count, 512, width), bf16), target_grad=s((blocks, span, width), f32),
        memory_grad=s((blocks, span, width), f32), vector_grads=s((16, width), f32))
    full, near, block = ((length, width), bf16), ((blocks, span, width), bf16), ((blocks, width, span), bf16)
    scratch = BackScratch(block=((count, 512, width), bf16), near=((count, 256, width), bf16), landed=((count, 256, width), bf16),
        key_t=((width, length), bf16), value=full, key_grad=full, value_grad=full,
        score_grad=((8, length, span), bf16), kept=((12, length, span), bf16), part=((length // span, span, width), bf16),
        part_core=((2, 2, span, width), bf16), part_side=((2, span, width), bf16),
        query_grad_t=block, query_grad=near, branch_low=((tokens, width), bf16),
        out_grad_t=block, out_grad=near, delta=((blocks, heads, 8, span), f32),
        vec=((16, width), f32), vec_landed=((5, 16, width), f32), acc=((6, 8, width), f32), output_own=((span, width), bf16))
    dma = pltpu.SemaphoreType.DMA
    return BackOut(*pl.pallas_call(
        functools.partial(backward_kernel, heads),
        out_shape=list(outs),
        in_specs=[vm if k in VECTORS else any_ for k in LOADS + UNLOADED],
        out_specs=[any_, any_, vm, vm, vm],
        scratch_shapes=[pltpu.VMEM(operands[k].shape, operands[k].dtype) for k in LOADS] + [pltpu.VMEM(*k) for k in scratch]
            + [dma((len(LOADS),)), dma((12,)), dma((count,)), dma((count, 10)), dma((count,)), dma((7,)), dma((7,)), dma((5,)), dma((5,)), dma((2,))],
        compiler_params=pltpu.CompilerParams(collective_id=1, has_side_effects=True, vmem_limit_bytes=63 << 20),
        name="backward",
    )(*(operands[k] for k in LOADS + UNLOADED)))

FINISH_BLOCK = (15, 13, 14, 12, 11, 9, 10, 8)
VECTOR_PLACE = (0, 3, 6, 1, 2, 4, 5, 7, 8)

def finish_kernel(reduced, vector_grads, output, target_grad, memory_grad, *refs):
    outs, small, handed = refs[3:13], refs[13:22], refs[:3]
    low, vec, stage, *between, load_sem, store_sem, sem = refs[22:]
    slots, count = stage.shape[0], reduced.shape[0]
    wide = outs[8].shape[1] // 512
    places = [outs[9].at[pl.ds(512 * i, 512)] for i in range(wide)] + [outs[8].at[:, pl.ds(512 * i, 512)] for i in range(wide)]
    places += [None] * 8
    for out, block in zip(outs, FINISH_BLOCK):
        places[block] = out
    loads = [pltpu.make_async_copy(reduced.at[i], low.at[i], load_sem.at[i]) for i in range(count)]
    for copy in loads:
        copy.start()
    arrive = [pltpu.make_async_copy(a, b, sem.at[i]) for i, (a, b) in enumerate(zip((output, target_grad, memory_grad, vector_grads), (*between, vec)))]
    leave = [pltpu.make_async_copy(a, b, sem.at[4 + i]) for i, (a, b) in enumerate(zip(between, handed))]
    for copy in arrive:
        copy.start()
    copies = [pltpu.make_async_copy(stage.at[i % slots], place, store_sem.at[i % slots]) for i, place in enumerate(places)]
    for i, copy in enumerate(copies):
        if i >= slots:
            copies[i - slots].wait()
        loads[i].wait()
        stage[i % slots] = low[i].astype(f32)
        copy.start()
    for copy in arrive:
        copy.wait()
    for copy in leave:
        copy.start()
    for ref, row in zip(small, VECTOR_PLACE):
        ref[...] = vec[row]
    for copy in copies[-slots:] + leave:
        copy.wait()

def finish_call(back, hidden):
    count, rows, width = back.reduced.shape
    any_, vm = pl.BlockSpec(memory_space=pl.ANY), pl.BlockSpec(memory_space=pltpu.VMEM)
    s = jax.ShapeDtypeStruct
    handed = [back.output, back.target_grad, back.memory_grad]
    shapes = [s(a.shape, a.dtype) for a in handed] + [s((width, width), f32)] * 8 + [s((width, hidden), f32), s((hidden, width), f32)]
    dma = pltpu.SemaphoreType.DMA
    return pl.pallas_call(
        finish_kernel,
        out_shape=shapes + [s((width,), f32)] * 9,
        in_specs=[any_] * 5,
        out_specs=[any_] * 13 + [vm] * 9,
        scratch_shapes=[pltpu.VMEM(back.reduced.shape, bf16), pltpu.VMEM((16, width), f32), pltpu.VMEM((8, rows, width), f32)]
            + [pltpu.VMEM(a.shape, a.dtype) for a in handed] + [dma((count,)), dma((8,)), dma((7,))],
        compiler_params=pltpu.CompilerParams(vmem_limit_bytes=62 << 20),
        name="finish",
    )(back.reduced, back.vector_grads, *handed)


def per_device(*args):
    rows, span, width = args[0].shape
    hidden = args[12].shape[1]
    fits = lax.axis_size("rows") == 8 and lax.axis_size("seq") == 4
    if not fits or (rows, span, width, hidden) != (2, 256, 512, 2048) or args[1].shape != args[0].shape:
        return ring_device(*args)
    matrices, vectors = args[4:14], args[14:23]
    kept = forward_call(args[0], args[1], args[2], args[3], matrices, vectors, args[23], HEADS)
    back = backward_call(kept, matrices, vectors, HEADS)
    return tuple(finish_call(back, hidden))


def solution(mesh):
    placed = (
        P("rows", "seq", None),
        P("rows", "seq", None),
        P("rows", None),
        P("rows", None),
        P(),
        P(),
        P(),
        P(),
        P(),
        P(),
        P(),
        P(),
        P(),
        P(),
        P(),
        P(),
        P(),
        P(),
        P(),
        P(),
        P(),
        P(),
        P(),
        P("rows", "seq", None),
    )
    return jax.shard_map(
        per_device,
        mesh=mesh,
        in_specs=placed,
        out_specs=(
            P("rows", "seq", None),
            P("rows", "seq", None),
            P("rows", "seq", None),
            P(),
            P(),
            P(),
            P(),
            P(),
            P(),
            P(),
            P(),
            P(),
            P(),
            P(),
            P(),
            P(),
            P(),
            P(),
            P(),
            P(),
            P(),
            P(),
        ),
        check_vma=False,
    )
```

```python
import functools
import math
from types import SimpleNamespace
from typing import NamedTuple

import jax
import jax.numpy as jnp
from jax import lax
from jax.experimental import pallas as pl
from jax.experimental.pallas import tpu as pltpu
from jax.sharding import PartitionSpec as P

HEADS = 8


masked_score = -1e30


def from_behind(block, axis, distance):
    devices = range(lax.axis_size(axis))
    route = [(i - distance, i) for i in devices if i - distance in devices]
    return lax.ppermute(block, axis, route)


def shifted(block, axis, distance):
    devices = range(lax.axis_size(axis))
    route = [((i - distance) % len(devices), i) for i in devices]
    return lax.ppermute(block, axis, route)


def layer_norm(pre_norm, gain, bias):
    centred = pre_norm - jnp.mean(pre_norm, axis=-1, keepdims=True)
    spread = jnp.mean(centred * centred, axis=-1, keepdims=True)
    return centred * lax.rsqrt(spread + 1e-05) * gain + bias


def residual_norm(previous, branch, omega, gain, bias):
    return layer_norm(previous * omega + branch, gain, bias)


def forward_product(inputs, weight):
    return jnp.dot(inputs, weight, preferred_element_type=jnp.float32)


def weight_product(inputs, grads):
    return jnp.einsum("rsd,rsf->df", inputs, grads, preferred_element_type=jnp.float32)


def input_product(grads, weight):
    return jnp.einsum("rsf,df->rsd", grads, weight, preferred_element_type=jnp.float32)


def split_heads(values, head_count):
    return values.reshape(values.shape[0], values.shape[1], head_count, -1)


def attend_update(running, query_low, key_low, value_low, allowed, score_scale, head_count):
    best, total, accum = running
    raw = (
        jnp.einsum(
            "rqhe,rkhe->rqhk",
            split_heads(query_low, head_count),
            split_heads(key_low, head_count),
            preferred_element_type=jnp.float32,
        )
        * score_scale
    )
    scores = jnp.where(allowed[:, :, None, :], raw, masked_score)
    new_best = jnp.maximum(best, jnp.max(scores, axis=-1))
    weights = jnp.where(allowed[:, :, None, :], jnp.exp(scores - new_best[..., None]), 0.0)
    factor = jnp.exp(best - new_best)
    total = total * factor + jnp.sum(weights, axis=-1)
    accum = accum * factor[..., None] + jnp.einsum(
        "rqhk,rkhe->rqhe",
        weights.astype(jnp.bfloat16),
        split_heads(value_low, head_count),
        preferred_element_type=jnp.float32,
    )
    return (new_best, total, accum)


def attend_grads(
    query_low, key_low, value_low, grad_low, logsum, row_delta, allowed, score_scale, head_count
):
    query_heads = split_heads(query_low, head_count)
    key_heads = split_heads(key_low, head_count)
    value_heads = split_heads(value_low, head_count)
    grad_heads = split_heads(grad_low, head_count)
    raw = (
        jnp.einsum("rqhe,rkhe->rqhk", query_heads, key_heads, preferred_element_type=jnp.float32)
        * score_scale
    )
    scores = jnp.where(allowed[:, :, None, :], raw, masked_score)
    attention_weights = jnp.exp(scores - logsum[..., None])
    value_grad = jnp.einsum(
        "rqhk,rqhe->rkhe",
        attention_weights.astype(jnp.bfloat16),
        grad_heads,
        preferred_element_type=jnp.float32,
    )
    weight_grad = jnp.einsum(
        "rqhe,rkhe->rqhk", grad_heads, value_heads, preferred_element_type=jnp.float32
    )
    score_grad = (attention_weights * (weight_grad - row_delta[..., None])).astype(jnp.bfloat16)
    query_grad = (
        jnp.einsum("rqhk,rkhe->rqhe", score_grad, key_heads, preferred_element_type=jnp.float32)
        * score_scale
    )
    key_grad = (
        jnp.einsum("rqhk,rqhe->rkhe", score_grad, query_heads, preferred_element_type=jnp.float32)
        * score_scale
    )
    query_shape = (query_low.shape[0], query_low.shape[1], query_low.shape[2])
    key_shape = (key_low.shape[0], key_low.shape[1], key_low.shape[2])
    return (
        query_grad.reshape(query_shape),
        key_grad.reshape(key_shape),
        value_grad.reshape(key_shape),
    )


def ring_device(
    target,
    memory,
    target_segments,
    memory_segments,
    self_query,
    self_key,
    self_value,
    self_output,
    cross_query,
    cross_key,
    cross_value,
    cross_output,
    ffn_in,
    ffn_out,
    omega_self,
    omega_cross,
    omega_ffn,
    gain_self,
    bias_self,
    gain_cross,
    bias_cross,
    gain_ffn,
    bias_ffn,
    cotangent,
):
    batch_rows, local_span, model_width = target.shape
    head_count = HEADS
    head_width = model_width // head_count
    score_scale = 1.0 / math.sqrt(head_width)
    self_index = lax.axis_index("seq")
    axis_size = lax.axis_size("seq")
    offsets = jnp.arange(local_span, dtype=jnp.int32)
    local_ids = lax.dynamic_slice_in_dim(target_segments, self_index * local_span, local_span, 1)

    def block_mask(query_source, key_source):
        query_ids = lax.dynamic_slice_in_dim(
            target_segments, query_source * local_span, local_span, 1
        )
        key_ids = lax.dynamic_slice_in_dim(target_segments, key_source * local_span, local_span, 1)
        query_place = query_source * local_span + offsets
        key_place = key_source * local_span + offsets
        matching = query_ids[:, :, None] == key_ids[:, None, :]
        return matching & (key_place[None, None, :] <= query_place[None, :, None])

    empty_state = (
        jnp.full((batch_rows, local_span, head_count), masked_score, jnp.float32),
        jnp.zeros((batch_rows, local_span, head_count), jnp.float32),
        jnp.zeros((batch_rows, local_span, head_count, head_width), jnp.float32),
    )
    self_triple = jnp.concatenate((self_query, self_key, self_value), axis=1)
    triple_low = forward_product(target, self_triple).astype(jnp.bfloat16)
    query_low = triple_low[..., :model_width]
    key_low = triple_low[..., model_width : 2 * model_width]
    value_low = triple_low[..., 2 * model_width :]
    running = attend_update(
        empty_state,
        query_low,
        key_low,
        value_low,
        block_mask(self_index, self_index),
        score_scale,
        head_count,
    )

    def forward_turn(step_index, carry):
        key_pair, running = carry
        key_pair = from_behind((key_pair[0], key_pair[1]), "seq", 1)
        source = (self_index - step_index + axis_size) % axis_size

        def forward_visit(inner):
            return attend_update(
                inner,
                query_low,
                key_pair[0],
                key_pair[1],
                block_mask(self_index, source),
                score_scale,
                head_count,
            )

        running = lax.cond(source <= self_index, forward_visit, lambda inner: inner, running)
        return (key_pair, running)

    key_pair, running = lax.fori_loop(1, axis_size, forward_turn, ((key_low, value_low), running))
    best, total, accum = running
    self_logsum = best + jnp.log(total)
    self_heads = accum / total[..., None]
    self_low = self_heads.reshape(batch_rows, local_span, model_width).astype(jnp.bfloat16)
    self_branch = forward_product(self_low, self_output)
    target_wide = target.astype(jnp.float32)
    hidden_one, pull_one = jax.vjp(
        residual_norm, target_wide, self_branch, omega_self, gain_self, bias_self
    )
    hidden_one_low = hidden_one.astype(jnp.bfloat16)
    cross_query_low = forward_product(hidden_one_low, cross_query).astype(jnp.bfloat16)
    cross_pair = jnp.concatenate((cross_key, cross_value), axis=1)
    memory_pairs = forward_product(
        lax.all_gather(memory, "seq", axis=1, tiled=True), cross_pair
    ).astype(jnp.bfloat16)
    memory_total = memory_pairs.shape[1]
    key_block = 1024
    block_count = memory_total // key_block

    def cross_mask(block_index):
        key_ids = lax.dynamic_slice_in_dim(memory_segments, block_index * key_block, key_block, 1)
        return local_ids[:, :, None] == key_ids[:, None, :]

    def block_pairs(block_index):
        return lax.dynamic_slice_in_dim(memory_pairs, block_index * key_block, key_block, 1)

    def cross_turn(block_index, running):
        pairs = block_pairs(block_index)
        return attend_update(
            running,
            cross_query_low,
            pairs[..., :model_width],
            pairs[..., model_width:],
            cross_mask(block_index),
            score_scale,
            head_count,
        )

    best, total, accum = lax.fori_loop(0, block_count, cross_turn, empty_state)
    cross_logsum = best + jnp.log(total)
    cross_heads = accum / total[..., None]
    cross_low = cross_heads.reshape(batch_rows, local_span, model_width).astype(jnp.bfloat16)
    cross_branch = forward_product(cross_low, cross_output)
    hidden_two, pull_two = jax.vjp(
        residual_norm, hidden_one, cross_branch, omega_cross, gain_cross, bias_cross
    )
    hidden_two_low = hidden_two.astype(jnp.bfloat16)
    upward = forward_product(hidden_two_low, ffn_in)
    activated, pull_gelu = jax.vjp(jax.nn.gelu, upward)
    active_low = activated.astype(jnp.bfloat16)
    ffn_branch = forward_product(active_low, ffn_out)
    result, pull_three = jax.vjp(
        residual_norm, hidden_two, ffn_branch, omega_ffn, gain_ffn, bias_ffn
    )
    two_grad, ffn_branch_grad, omega_ffn_grad, gain_ffn_grad, bias_ffn_grad = pull_three(
        cotangent.astype(jnp.float32)
    )
    ffn_branch_low = ffn_branch_grad.astype(jnp.bfloat16)
    ffn_out_grad = weight_product(active_low, ffn_branch_low)
    upward_grad = pull_gelu(input_product(ffn_branch_low, ffn_out))[0]
    upward_low = upward_grad.astype(jnp.bfloat16)
    ffn_in_grad = weight_product(hidden_two_low, upward_low)
    two_grad = two_grad + input_product(upward_low, ffn_in)
    one_grad, cross_branch_grad, omega_cross_grad, gain_cross_grad, bias_cross_grad = pull_two(
        two_grad
    )
    cross_branch_low = cross_branch_grad.astype(jnp.bfloat16)
    cross_output_grad = weight_product(cross_low, cross_branch_low)
    cross_heads_grad = input_product(cross_branch_low, cross_output).astype(jnp.bfloat16)
    cross_delta = jnp.sum(
        split_heads(cross_heads_grad, head_count).astype(jnp.float32) * cross_heads, axis=-1
    )

    def cross_back(block_index, carry):
        query_grad, pair_grads = carry
        pairs = block_pairs(block_index)
        grads = attend_grads(
            cross_query_low,
            pairs[..., :model_width],
            pairs[..., model_width:],
            cross_heads_grad,
            cross_logsum,
            cross_delta,
            cross_mask(block_index),
            score_scale,
            head_count,
        )
        block_grads = jnp.concatenate((grads[1], grads[2]), axis=2)
        pair_grads = lax.dynamic_update_slice_in_dim(
            pair_grads, block_grads, block_index * key_block, 1
        )
        return (query_grad + grads[0], pair_grads)

    zero_grid = jnp.zeros((batch_rows, local_span, model_width), jnp.float32)
    cross_query_sum, pair_grads = lax.fori_loop(
        0,
        block_count,
        cross_back,
        (zero_grid, jnp.zeros((batch_rows, memory_total, 2 * model_width), jnp.float32)),
    )
    local_pair_grads = lax.psum_scatter(
        pair_grads.astype(jnp.bfloat16), "seq", scatter_dimension=1, tiled=True
    )
    memory_grad = input_product(local_pair_grads, cross_pair)
    pair_weight_grad = weight_product(memory, local_pair_grads)
    cross_query_low_grad = cross_query_sum.astype(jnp.bfloat16)
    cross_query_grad = weight_product(hidden_one_low, cross_query_low_grad)
    one_grad = one_grad + input_product(cross_query_low_grad, cross_query)
    target_residual_grad, self_branch_grad, omega_self_grad, gain_self_grad, bias_self_grad = (
        pull_one(one_grad)
    )
    self_branch_low = self_branch_grad.astype(jnp.bfloat16)
    self_output_grad = weight_product(self_low, self_branch_low)
    self_heads_grad = input_product(self_branch_low, self_output).astype(jnp.bfloat16)
    self_delta = jnp.sum(
        split_heads(self_heads_grad, head_count).astype(jnp.float32) * self_heads, axis=-1
    )

    def key_turn(step_index, carry):
        key_pair, grad_pair, query_grad = carry
        source = (self_index - step_index + axis_size) % axis_size

        def key_visit(inner):
            grads = attend_grads(
                query_low,
                key_pair[0],
                key_pair[1],
                self_heads_grad,
                self_logsum,
                self_delta,
                block_mask(self_index, source),
                score_scale,
                head_count,
            )
            return (inner[0] + grads[0], inner[1] + grads[1], inner[2] + grads[2])

        query_grad, key_grad, value_grad = lax.cond(
            source <= self_index,
            key_visit,
            lambda inner: inner,
            (query_grad, grad_pair[0], grad_pair[1]),
        )
        grad_pair = (
            shifted(key_grad.astype(jnp.bfloat16), "seq", 1).astype(key_grad.dtype),
            shifted(value_grad.astype(jnp.bfloat16), "seq", 1).astype(value_grad.dtype),
        )
        key_pair = from_behind((key_pair[0], key_pair[1]), "seq", 1)
        return (key_pair, grad_pair, query_grad)

    key_pair, grad_pair, query_grad = lax.fori_loop(
        0, axis_size, key_turn, ((key_low, value_low), (zero_grid, zero_grid), zero_grid)
    )
    key_grad, value_grad = grad_pair
    triple_grad_low = jnp.concatenate((query_grad, key_grad, value_grad), axis=2).astype(
        jnp.bfloat16
    )
    target_grad = target_residual_grad + input_product(triple_grad_low, self_triple)
    triple_weight_grad = weight_product(target, triple_grad_low)
    sums = lax.psum(
        (
            triple_weight_grad[:, :model_width],
            triple_weight_grad[:, model_width : 2 * model_width],
            triple_weight_grad[:, 2 * model_width :],
            self_output_grad,
            cross_query_grad,
            pair_weight_grad[:, :model_width],
            pair_weight_grad[:, model_width:],
            cross_output_grad,
            ffn_in_grad,
            ffn_out_grad,
            omega_self_grad,
            omega_cross_grad,
            omega_ffn_grad,
            gain_self_grad,
            bias_self_grad,
            gain_cross_grad,
            bias_cross_grad,
            gain_ffn_grad,
            bias_ffn_grad,
        ),
        ("rows", "seq"),
    )
    return (result.astype(jnp.bfloat16), target_grad, memory_grad) + tuple(sums)


MESH = pl.DeviceIdType.MESH
f32, bf16 = jnp.float32, jnp.bfloat16

def dot(a, b):
    return jnp.dot(a, b, preferred_element_type=f32)

def dot_t(a, b):
    return lax.dot_general(a, b, (((1,), (1,)), ((), ())), preferred_element_type=f32)

def t_dot(a, b):
    return lax.dot_general(a, b, (((0,), (0,)), ((), ())), preferred_element_type=f32)

def mult(i, m):
    return i if isinstance(i, int) else pl.multiple_of(i, m)

def attend_forward(first_block, blocks, keys, key, value_t, query_z, seen, scores, kept, kept_out, kept_sem, out_t, inverse, heads):
    count, piece, slots, queries = blocks * heads, 256, kept.shape[0], seen.shape[2]

    def head_place(i):
        block, head = first_block + i // heads, i % heads
        return block, head, pl.ds(mult(head * 64, 64), 64), pl.ds(mult(head // 2 * 128, 128), 128)

    def first(i, slot):
        block, head, _, pair = head_place(i)
        best = None
        for c in range(keys // piece):
            ks = pl.ds(c * piece, piece)
            s = dot(key[ks, pair], query_z[block, head]) + seen[block, ks]
            scores[slot, ks] = s
            top = jnp.max(s.reshape(piece // 8, 8, queries), axis=0)
            best = top if best is None else jnp.maximum(best, top)
        return best

    def out_copy(i):
        block, head, _, _ = head_place(i)
        return pltpu.make_async_copy(kept.at[i % slots, pl.ds(0, keys)], kept_out.at[block, head, pl.ds(0, keys)], kept_sem.at[i % slots])

    def second(i, slot, best):
        block, head, here, _ = head_place(i)
        best = jnp.max(best, axis=0, keepdims=True)
        total = out = None
        for c in range(keys // piece):
            ks = pl.ds(c * piece, piece)
            p = jnp.exp(scores[slot, ks] - best)
            part = jnp.sum(p.reshape(piece // 8, 8, queries), axis=0)
            total = part if total is None else total + part
            p = p.astype(bf16)
            kept[i % slots, ks] = p
            part = dot(value_t[here, ks], p)
            out = part if out is None else out + part
        scale = 1.0 / jnp.sum(total, axis=0, keepdims=True)
        out_t[block, here, :] = (out * scale).astype(bf16)
        inverse[block, head] = jnp.broadcast_to(scale, (8, queries))

    def body(j, best):
        i = 2 * j
        for e in range(2):
            pl.when(i + e >= slots)(lambda e=e: out_copy(i + e - slots).wait())
        later = first(i + 1, 1)
        second(i, 0, best)
        best = first(jnp.minimum(i + 2, count - 1), 0)
        second(i + 1, 1, later)
        out_copy(i).start()
        out_copy(i + 1).start()
        return best

    lax.fori_loop(0, count // 2, body, first(0, 0))
    for i in range(count - slots, count):
        out_copy(i).wait()

def norm_parts(pre):
    centred = pre - jnp.mean(pre, axis=-1, keepdims=True)
    rstd = lax.rsqrt(jnp.mean(centred * centred, axis=-1, keepdims=True) + 1e-05)
    return centred * rstd, rstd

def pad_pairs(query, query_z, row, heads):
    turned = query.T
    half = lax.broadcasted_iota(jnp.int32, (128, query.shape[0]), 0) // 64
    for head in range(heads):
        pair = turned[head // 2 * 128 : head // 2 * 128 + 128]
        query_z[row, head] = jnp.where(half == head % 2, pair, jnp.zeros_like(pair))

class ForwardIn(NamedTuple):
    target: object
    memory: object
    target_segments: object
    memory_segments: object
    self_query: object
    self_key: object
    self_value: object
    self_output: object
    cross_query: object
    cross_key: object
    cross_value: object
    cross_output: object
    ffn_in: object
    ffn_out: object
    omega_self: object
    omega_cross: object
    omega_ffn: object
    gain_self: object
    bias_self: object
    gain_cross: object
    bias_cross: object
    gain_ffn: object
    bias_ffn: object
    cotangent: object

class ForwardOut(NamedTuple):
    output_blocks: object
    target_all: object
    memory_all: object
    self_kept: object
    cross_kept: object
    self_inverse: object
    cross_inverse: object
    self_out: object
    cross_out: object
    self_q: object
    cross_q: object
    one_low: object
    one_hat: object
    one_rstd: object
    two_low: object
    two_hat: object
    two_rstd: object
    active: object
    upward_slope: object
    branch_grad: object
    two_grad: object
    sums: object

class ForwardScratch(NamedTuple):
    key: object
    value_t: object
    query_z: object
    seen_self: object
    seen_cross: object
    scores: object
    kept: object
    mem_key: object
    mem_value_t: object
    wide: object
    one: object
    two: object
    value_turned: object
    mem_value_turned: object
    grads: object
    up: object

FORWARD_NAMES = ForwardIn._fields + ForwardOut._fields
MATRICES = ForwardIn._fields[4:14]
VECTORS = ForwardIn._fields[14:23]

def forward_kernel(heads, *refs):
    hbm = SimpleNamespace(**dict(zip(FORWARD_NAMES, refs)))
    own = refs[len(FORWARD_NAMES):-5]
    r = SimpleNamespace(**dict(zip(FORWARD_NAMES[2:4] + VECTORS + MATRICES + ForwardOut._fields + ForwardScratch._fields,
        refs[2:4] + refs[14:23] + own)))
    send, recv, local, load_sem, out_sem = refs[-5:]
    kept_sem = local
    me_r, me_s = lax.axis_index("rows"), lax.axis_index("seq")
    core, side = me_s % 2, me_s // 2
    length, width = r.target_all.shape
    tokens = r.one_low.shape[0]
    blocks = 2
    span = tokens // blocks
    other_core, other_side = me_s + 1 - 2 * core, me_s + 2 - 4 * side

    def place(i):
        return pl.ds(mult(i * span, span), span)

    def remote(src, dst, k, to):
        return pltpu.make_async_remote_copy(src_ref=src, dst_ref=dst, send_sem=send.at[k], recv_sem=recv.at[k],
            device_id=(me_r, to), device_id_type=MESH)

    def share(source, full, k):
        mine, theirs = full.at[place(me_s)], full.at[place(other_side)]
        return (pltpu.make_async_copy(source.at[side], mine, load_sem.at[10 + k // 3]), remote(source.at[1 - side], mine, k, other_side),
            remote(source.at[side], mine, k + 1, other_core), remote(theirs, theirs, k + 2, other_core))

    x_own, x_side, x_core, x_pass = share(hbm.target, r.target_all, 0)
    m_own, m_side, m_core, m_pass = share(hbm.memory, r.memory_all, 3)
    g_own = pltpu.make_async_copy(hbm.cotangent.at[side], r.grads.at[side], load_sem.at[12])
    g_side = remote(hbm.cotangent.at[1 - side], r.grads.at[side], 6, other_side)
    x_own.start()
    m_own.start()
    loads = {k: pltpu.make_async_copy(getattr(hbm, k), getattr(r, k), load_sem.at[i]) for i, k in enumerate(MATRICES)}
    for copy in loads.values():
        copy.start()
    g_own.start()
    loads = SimpleNamespace(**loads)
    outs = []

    def emit(*names):
        for k in names:
            copy = pltpu.make_async_copy(getattr(r, k), getattr(hbm, k), out_sem.at[len(outs)])
            copy.start()
            outs.append(copy)

    barrier = pltpu.get_barrier_semaphore()
    for to in (other_core, other_side):
        pl.semaphore_signal(barrier, inc=1, device_id=(me_r, to), device_id_type=MESH)
    pl.semaphore_wait(barrier, 2)
    x_side.start()
    x_core.start()
    m_core.start()

    def masks():
        def line(ids, at):
            first, second = ids[0:1, at], ids[1:2, at]
            return (first + (second - first) * side).astype(f32)
        mine = [line(r.target_segments, pl.ds(mult((2 * b + core) * span, span), span)) for b in range(blocks)]
        for c in range(length // 128):
            at = pl.ds(c * 128, 128)
            key_place = c * 128 + lax.broadcasted_iota(jnp.int32, (128, span), 0)
            query_place = lax.broadcasted_iota(jnp.int32, (128, span), 1)
            for ids, seen, causal in ((r.target_segments, r.seen_self, True), (r.memory_segments, r.seen_cross, False)):
                column = jnp.broadcast_to(line(ids, at), (128, 128)).T
                column = jnp.concatenate([column] * (span // 128), axis=1)
                for b in range(blocks):
                    if causal and c * 128 >= (b + 1) * length // 2:
                        continue
                    same = column == mine[b]
                    if causal:
                        same = same & (key_place <= query_place + (2 * b + core) * span)
                    seen[b, at] = jnp.where(same, 0.0, -1e30)

    def project(full, key_weight, turned, key, value_t, block):
        at = place(block)
        here = full[at]
        key[at] = dot(here, key_weight[...]).astype(bf16)
        value_t[:, at] = dot_t(turned[...], here).astype(bf16)

    def project_self(block):
        project(r.target_all, r.self_key, r.value_turned, r.key, r.value_t, block)

    def project_cross(block):
        project(r.memory_all, r.cross_key, r.mem_value_turned, r.mem_key, r.mem_value_t, block)

    def queries(low, weight, out):
        for b in range(blocks):
            query = (dot(low(b), weight[...]).astype(bf16) * 0.125).astype(bf16)
            out[b] = query
            pad_pairs(query, r.query_z, b, heads)

    masks()
    for k in (loads.self_query, loads.self_key, loads.self_value, loads.cross_key, loads.cross_value):
        k.wait()
    r.value_turned[...] = r.self_value[...].T
    r.mem_value_turned[...] = r.cross_value[...].T
    x_own.wait()
    project_self(me_s)
    x_core.wait()
    project_self(other_core)
    x_side.wait()
    x_pass.start()
    m_side.start()
    queries(lambda b: r.target_all[place(2 * b + core)], r.self_query, r.self_q)
    project_self(other_side)
    m_own.wait()
    project_cross(me_s)
    x_pass.wait()
    project_self(other_side + 1 - 2 * core)
    m_core.wait()
    project_cross(other_core)
    emit(*ForwardOut._fields[1:2], *ForwardOut._fields[9:10])

    def attend(first_block, count, keys, key, value_t, seen, kept_out, out_t, inverse):
        attend_forward(first_block, count, keys, key, value_t, r.query_z, seen, r.scores, r.kept, kept_out, kept_sem, out_t, inverse, heads)

    attend(0, 1, length // 2, r.key, r.value_t, r.seen_self, hbm.self_kept, r.self_out, r.self_inverse)
    attend(1, 1, length, r.key, r.value_t, r.seen_self, hbm.self_kept, r.self_out, r.self_inverse)
    m_side.wait()
    m_pass.start()
    g_side.start()
    loads.self_output.wait()
    vec = [getattr(r, k)[...].reshape(1, width) for k in VECTORS]
    part = 128
    for b in range(blocks):
        r.wide[pl.ds(b * span, span)] = t_dot(r.self_out[b], r.self_output[...])

    @pl.loop(0, tokens // part)
    def _(i):
        at = pl.ds(mult(i * part, part), part)
        b, inner = i // (span // part), i % (span // part)
        x = r.target_all[pl.ds(mult((2 * b + core) * span + inner * part, part), part)].astype(f32)
        hat, rstd = norm_parts(x * vec[0] + r.wide[at])
        one = hat * vec[3] + vec[4]
        r.one_hat[at] = hat
        r.one_rstd[at] = jnp.broadcast_to(rstd, (part, 128))
        r.one[at] = one
        r.one_low[at] = one.astype(bf16)

    loads.cross_query.wait()
    queries(lambda b: r.one_low[pl.ds(b * span, span)], r.cross_query, r.cross_q)
    project_cross(other_side)
    m_pass.wait()
    project_cross(other_side + 1 - 2 * core)
    emit(*ForwardOut._fields[2:3], *ForwardOut._fields[5:6], *ForwardOut._fields[7:8], *ForwardOut._fields[10:14])
    attend(0, 2, length, r.mem_key, r.mem_value_t, r.seen_cross, hbm.cross_kept, r.cross_out, r.cross_inverse)
    loads.cross_output.wait()
    for b in range(blocks):
        r.wide[pl.ds(b * span, span)] = t_dot(r.cross_out[b], r.cross_output[...])

    @pl.loop(0, tokens // part)
    def _(i):
        at = pl.ds(mult(i * part, part), part)
        hat, rstd = norm_parts(r.one[at] * vec[1] + r.wide[at])
        two = hat * vec[5] + vec[6]
        r.two_hat[at] = hat
        r.two_rstd[at] = jnp.broadcast_to(rstd, (part, 128))
        r.two[at] = two
        r.two_low[at] = two.astype(bf16)

    emit(*ForwardOut._fields[6:7], *ForwardOut._fields[8:9], *ForwardOut._fields[14:17])
    loads.ffn_in.wait()
    loads.ffn_out.wait()
    c0 = math.sqrt(2.0 / math.pi)
    pieces = r.ffn_in.shape[1] // 512
    r.wide[...] = jnp.zeros_like(r.wide)

    halves = [pl.ds(half * (tokens // 2), tokens // 2) for half in range(2)]

    def up(j, half):
        r.up[half] = dot(r.two_low[halves[half]], r.ffn_in[:, pl.ds(mult(j * 512, 512), 512)])

    def down(j, half):
        at, cols = halves[half], pl.ds(mult(j * 512, 512), 512)
        u = r.up[half]
        square = u * u
        t = jnp.tanh(u * (c0 + (c0 * 0.044715) * square))
        rise = 0.5 + 0.5 * t
        active = (u * rise).astype(bf16)
        r.active[at, cols] = active
        r.upward_slope[at, cols] = (rise + u * (rise * (1.0 - t)) * (c0 + (3 * 0.044715 * c0) * square)).astype(bf16)
        r.wide[at] += dot(active, r.ffn_out[cols, :])

    up(0, 0)

    @pl.loop(0, pieces)
    def _(j):
        up(j, 1)
        down(j, 0)
        up(jnp.minimum(j + 1, pieces - 1), 0)
        down(j, 1)

    emit(*ForwardOut._fields[17:19])
    g_own.wait()
    g_side.wait()
    r.sums[...] = jnp.zeros_like(r.sums)

    @pl.loop(0, tokens // part)
    def _(i):
        at = pl.ds(mult(i * part, part), part)
        b, inner = i // (span // part), i % (span // part)
        near = pl.ds(mult(inner * part, part), part)
        two = r.two[at]
        hat, rstd = norm_parts(two * vec[2] + r.wide[at])
        r.output_blocks[b, near] = (hat * vec[7] + vec[8]).astype(bf16)
        grad = r.grads[b, near].astype(f32)
        scaled = grad * vec[7]
        back = rstd * (scaled - jnp.mean(scaled, axis=-1, keepdims=True) - hat * jnp.mean(scaled * hat, axis=-1, keepdims=True))
        r.branch_grad[at] = back.astype(bf16)
        r.two_grad[at] = back * vec[2]
        r.sums[0] += jnp.sum((back * two).reshape(part // 8, 8, width), axis=0)
        r.sums[1] += jnp.sum((grad * hat).reshape(part // 8, 8, width), axis=0)
        r.sums[2] += jnp.sum(grad.reshape(part // 8, 8, width), axis=0)

    emit(*ForwardOut._fields[:1], *ForwardOut._fields[19:])

    for copy in outs:
        copy.wait()

def forward_call(target, memory, target_segments, memory_segments, matrices, vectors, cotangent, heads=8):
    blocks, span, width = target.shape
    length = target_segments.shape[1]
    tokens = blocks * span
    hidden = matrices[8].shape[1]
    any_, vm = pl.BlockSpec(memory_space=pl.ANY), pl.BlockSpec(memory_space=pltpu.VMEM)
    s = jax.ShapeDtypeStruct
    full, wide, seen = ((length, width), bf16), ((tokens, width), f32), ((blocks, length, span), f32)
    kept, inverse = s((blocks, heads, length, span), bf16), s((blocks, heads, 8, span), f32)
    outs = ForwardOut(output_blocks=s((blocks, span, width), bf16), target_all=s(*full), memory_all=s(*full),
        self_kept=kept, cross_kept=kept, self_inverse=inverse, cross_inverse=inverse,
        self_out=s((blocks, width, span), bf16), cross_out=s((blocks, width, span), bf16),
        self_q=s((blocks, span, width), bf16), cross_q=s((blocks, span, width), bf16),
        one_low=s((tokens, width), bf16), one_hat=s(*wide), one_rstd=s((tokens, 128), f32),
        two_low=s((tokens, width), bf16), two_hat=s(*wide), two_rstd=s((tokens, 128), f32),
        active=s((tokens, hidden), bf16), upward_slope=s((tokens, hidden), bf16), branch_grad=s((tokens, width), bf16),
        two_grad=s(*wide), sums=s((3, 8, width), f32))
    turned = ((width, length), bf16)
    scratch = ForwardScratch(key=full, value_t=turned, query_z=((blocks, heads, 128, span), bf16),
        seen_self=seen, seen_cross=seen, scores=((2, length, span), f32),
        kept=((4, length, span), bf16), mem_key=full, mem_value_t=turned,
        wide=wide, one=wide, two=wide,
        value_turned=((width, width), bf16), mem_value_turned=((width, width), bf16), grads=((blocks, span, width), bf16), up=((2, tokens // 2, 512), f32))
    held = [((8, 128), f32) if k in ForwardOut._fields[3:5] else (o.shape, o.dtype) for k, o in zip(ForwardOut._fields, outs)]
    held = [(m.shape, m.dtype) for m in matrices] + held + list(scratch)
    dma = pltpu.SemaphoreType.DMA
    return ForwardOut(*pl.pallas_call(
        functools.partial(forward_kernel, heads),
        out_shape=list(outs),
        in_specs=[any_] * 2 + [vm] * 2 + [any_] * 10 + [vm] * 9 + [any_],
        out_specs=[any_] * len(outs),
        scratch_shapes=[pltpu.VMEM(*k) for k in held] + [dma((7,)), dma((7,)), dma((4,)), dma((13,)), dma((20,))],
        compiler_params=pltpu.CompilerParams(collective_id=0, has_side_effects=True, vmem_limit_bytes=62 << 20),
        name="forward",
    )(target, memory, target_segments, memory_segments, *matrices, *vectors, cotangent))

CLASSES = (0, 4, 0, 1, 1, 1, 0, 0, 2, 4, 1, 4, 1, 1, 4, 1)
PLAN = (
    (0,),
    (19, 1),
    (2,),
    (3,),
    (1, 0, 2, 4),
    (3, 5),
    (6,),
    (7,),
    (4, 5),
    (19, 1, 7, 6),
    (8,),
    (),
    (),
    (3, 1, 0, 8),
    (2, 4),
    (),
    (1, 7, 5),
    (9, 0),
    (10, 8),
    (11, 2),
    (16, 1, 6, 9, 3, 7, 10, 0),
    (11,),
    (18, 1, 4),
    (12, 2),
    (16, 3, 6, 5, 8),
    (18, 7, 0),
    (12, 1, 9, 10, 2, 4),
    (3, 6),
    (7, 0, 11, 5, 8),
    (),
    (1, 13, 10),
    (14, 16),
    (15, 18, 9, 2),
    (17, 3, 13, 7, 6, 14, 4),
    (15, 12, 0, 8, 1, 18, 11, 5, 17, 10, 1, 9, 13, 2, 14, 3, 7, 12, 6, 4, 15, 18, 13, 11, 0, 5, 8, 10, 3, 15, 14, 12, 6, 4, 0, 18, 8, 17, 13, 9, 5, 10, 0, 2, 4, 15, 14, 7, 12, 11, 5, 8, 13, 10, 3, 15, 12, 2, 6, 9, 3, 2, 7, 8, 13, 15, 4, 14, 10, 12, 11, 9, 7, 8, 13, 4, 15, 6, 5, 14, 11, 12, 9, 6, 13, 5, 10, 14, 15, 11, 10, 12, 9, 14, 12, 13, 9, 11, 13, 15, 11, 14, 15, 14),
)

class Reduction:
    def __init__(self, block, near, landed, reduced, send, recv, own):
        self.block, self.near, self.landed, self.reduced = block, near, landed, reduced
        self.send, self.recv, self.own = send, recv, own
        self.r, self.s = lax.axis_index("rows"), lax.axis_index("seq")
        self.core, self.y = self.s % 2, self.s // 2
        self.x, self.z0, self.z1 = self.r % 2, (self.r // 2) % 2, self.r // 4
        self.count, self.size = block.shape[0], block.shape[1]
        x, y, z0, z1 = self.x, self.y, self.z0, self.z1
        core, ax, ay = (0, 1 - 2 * self.core, self.core), (1 - 2 * x, 0, x), (0, 2 - 4 * y, y)
        an, af = (2 - 4 * z0, 0, z0), (4 - 8 * z1, 0, z1)
        self.orders = ((core, ax, ay, an, af), (core, ay, ax, an, af), (core, an, af, ax, ay), (core, an, af, ay, ax), (core, ax, an, af, ay), (core, ay, an, af, ax))
        self.flows, self.turn, done = {}, 0, {}
        self.polls = []
        for entry in PLAN:
            self.polls.append([(c, done.setdefault(c, []).append(0) or len(done[c]) - 1) for c in entry])

    def partners(self):
        r, s = self.r, self.s
        return ((r, s + 1 - 2 * self.core), (r, s + 2 - 4 * self.y), (r + 1 - 2 * self.x, s),
                (r + 2 - 4 * self.z0, s), (r + 4 - 8 * self.z1, s))

    def start_of(self, j, hops):
        off = 0
        for i in range(j):
            off = off + hops[i][2] * (self.size >> (i + 1))
        return off

    def landing(self, c, j):
        half = self.size >> (j + 1)
        if j == 0:
            return self.near.at[c]
        return self.landed.at[c, pl.ds(self.size // 2 - (self.size >> j), half)]

    def copy(self, c, j, gather):
        hops = self.orders[CLASSES[c]]
        off, half = self.start_of(j, hops), self.size >> (j + 1)
        dr, ds, bit = hops[j]
        if gather:
            mine = pl.ds(pl.multiple_of(off + bit * half, 16), half)
            src, dst = (self.block if j == 4 else self.reduced).at[c, mine], self.reduced.at[c, mine]
        else:
            src, dst = self.block.at[c, pl.ds(pl.multiple_of(off + (1 - bit) * half, 16), half)], self.landing(c, j)
        return pltpu.make_async_remote_copy(src_ref=src, dst_ref=dst, send_sem=self.send.at[c],
            recv_sem=self.recv.at[c, j + 5 * gather], device_id=(self.r + dr, self.s + ds), device_id_type=MESH)

    def own_copy(self, c):
        mine = pl.ds(pl.multiple_of(self.start_of(5, self.orders[CLASSES[c]]), 16), self.size >> 5)
        return pltpu.make_async_copy(self.block.at[c, mine], self.reduced.at[c, mine], self.own.at[c])

    def add(self, c, j):
        keep = pl.ds(pl.multiple_of(self.start_of(j + 1, self.orders[CLASSES[c]]), 16), self.size >> (j + 1))
        self.block[c, keep] = (self.block[c, keep].astype(f32) + self.landing(c, j)[...].astype(f32)).astype(bf16)

    def step(self, c, s):
        if c >= self.count:
            return self.flows[c](s)
        if 1 <= s <= 5:
            self.copy(c, s - 1, 0).wait()
            self.add(c, s - 1)
        elif s > 5:
            self.copy(c, 10 - s, 1).wait()
        if s == 5:
            self.own_copy(c).start()
        elif s == 6:
            self.own_copy(c).wait()
        if s <= 4:
            self.copy(c, s, 0).start()
        elif s <= 9:
            self.copy(c, 9 - s, 1).start()

    def poll(self, index=None):
        if index is None:
            index = self.turn
            self.turn += 1
        for c, s in self.polls[index]:
            self.step(c, s)

    def poll_loop(self, base, count, i):
        for k in range(count):
            if self.polls[base + k]:
                @pl.when(i == k)
                def _():
                    self.poll(base + k)

class Loads(NamedTuple):
    active: object
    branch_grad: object
    two_low: object
    upward_slope: object
    ffn_out: object
    ffn_in: object
    two_grad: object
    two_hat: object
    two_rstd: object
    one_hat: object
    one_rstd: object
    cross_output: object
    cross_out: object
    cross_inverse: object
    memory_all: object
    cross_key: object
    cross_value: object
    cross_q: object
    one_low: object
    cross_query: object
    target_all: object
    self_output: object
    self_out: object
    self_inverse: object
    self_key: object
    self_value: object
    self_q: object
    self_query: object
    sums: object

class BackOut(NamedTuple):
    output: object
    reduced: object
    target_grad: object
    memory_grad: object
    vector_grads: object

class BackScratch(NamedTuple):
    block: object
    near: object
    landed: object
    key_t: object
    value: object
    key_grad: object
    value_grad: object
    score_grad: object
    kept: object
    part: object
    part_core: object
    part_side: object
    query_grad_t: object
    query_grad: object
    branch_low: object
    out_grad_t: object
    out_grad: object
    delta: object
    vec: object
    vec_landed: object
    acc: object
    output_own: object

LOADS = Loads._fields
UNLOADED = ForwardOut._fields[3:5] + ForwardOut._fields[:1] + VECTORS

def backward_kernel(heads, *refs):
    n = len(LOADS + UNLOADED)
    hbm = SimpleNamespace(**dict(zip(LOADS + UNLOADED, refs)))
    r = SimpleNamespace(**dict(zip(BackOut._fields + LOADS + BackScratch._fields, refs[n:])))
    load_sem, kept_sem, send, recv, own_sem, part_send, part_recv, vec_send, vec_recv, out_sem = refs[-10:]
    length, width = r.memory_all.shape
    tokens = r.two_low.shape[0]
    blocks = 2
    span = tokens // blocks
    red = Reduction(r.block, r.near, r.landed, r.reduced, send, recv, own_sem)
    me_r, me_s, core, side = red.r, red.s, red.core, red.y

    loads = Loads(*[pltpu.make_async_copy(getattr(hbm, k), getattr(r, k), load_sem.at[i]) for i, k in enumerate(LOADS)])
    for copy in loads:
        copy.start()

    def need(*copies):
        for copy in copies:
            copy.wait()

    barrier = pltpu.get_barrier_semaphore()
    for to in red.partners():
        pl.semaphore_signal(barrier, inc=1, device_id=to, device_id_type=MESH)
    pl.semaphore_wait(barrier, 5)

    def block_at(b):
        return pl.ds(b * span, span)

    def place(i):
        return pl.ds(mult(i * span, span), span)

    def ffn_block(c):
        if c < 4:
            r.block[c] = t_dot(r.active[:, pl.ds(c * 512, 512)], r.branch_grad[...]).astype(bf16)
        else:
            r.block[c] = t_dot(r.two_low[...], r.upward_slope[:, pl.ds((c - 4) * 512, 512)]).astype(bf16)

    def upward_gradient():
        @pl.loop(0, r.upward_slope.shape[1] // 512)
        def _(j):
            cols = pl.ds(mult(j * 512, 512), 512)
            for b in range(blocks):
                grad = dot_t(r.branch_grad[block_at(b)], r.ffn_out[cols, :])
                r.upward_slope[block_at(b), cols] = (grad * r.upward_slope[block_at(b), cols].astype(f32)).astype(bf16)

    vec = [getattr(hbm, k)[...].reshape(1, width) for k in VECTORS]
    part = 128

    def norm_back(grad_ref, hat_ref, rstd_ref, gain, omega, previous, slot):
        for i in range(3):
            r.acc[slot + i] = jnp.zeros_like(r.acc[slot + i])

        @pl.loop(0, tokens // part)
        def _(i):
            at = pl.ds(mult(i * part, part), part)
            hat, grad = hat_ref[at], grad_ref[at]
            scaled = grad * gain
            back = rstd_ref[at][:, 0:1] * (scaled - jnp.mean(scaled, axis=-1, keepdims=True)
                - hat * jnp.mean(scaled * hat, axis=-1, keepdims=True))
            r.branch_low[at] = back.astype(bf16)
            grad_ref[at] = back * omega
            for k, term in enumerate((back * previous(i), grad * hat, grad)):
                r.acc[slot + k] += jnp.sum(term.reshape(part // 8, 8, width), axis=0)

    def attention_start(weight, out_t, inverse):
        for b in range(blocks):
            grad_t = dot_t(weight[...], r.branch_low[block_at(b)])
            for head in range(heads):
                here = pl.ds(head * 64, 64)
                scaled = grad_t[head * 64 : head * 64 + 64] * inverse[b, head][0:1]
                r.out_grad_t[b, here] = scaled.astype(bf16)
                delta = jnp.sum(scaled * out_t[b, here].astype(f32), axis=0, keepdims=True)
                r.delta[b, head] = jnp.broadcast_to(delta, (8, span))
            r.out_grad[b] = r.out_grad_t[b].T

    def keys_again(full, key_weight, value_weight):
        key_turned = key_weight[...].T
        for c in range(length // 512):
            at = pl.ds(c * 512, 512)
            here = full[at]
            r.key_t[:, at] = dot_t(key_turned, here).astype(bf16)
            r.value[at] = dot(here, value_weight[...]).astype(bf16)

    def attention_back(kept_hbm, query, spans):
        base = red.turn
        pairs, piece = heads // 2, 256
        red.turn += pairs
        tiles = [(b, e) for b in range(blocks) for e in range(2)]
        top = lax.broadcasted_iota(jnp.int32, (128, span), 0) // 64
        left = lax.broadcasted_iota(jnp.int32, (span, 128), 1) // 64

        def pair_at(j):
            return pl.ds(mult(j * 128, 128), 128)

        def fetch(j, b, e):
            slot, ks = j % 3 * 4 + b * 2 + e, pl.ds(0, spans[b])
            return pltpu.make_async_copy(kept_hbm.at[b, 2 * j + e, ks], r.kept.at[slot, ks], kept_sem.at[slot])

        def first(j):
            for b, e in tiles:
                fetch(j, b, e).wait()
            for b, e in tiles:
                grad = jnp.where(top == e, r.out_grad_t[b, pair_at(j), :], jnp.zeros((128, span), bf16))
                delta = r.delta[b, 2 * j + e][0:1]
                for c in range(spans[b] // piece):
                    ks = pl.ds(c * piece, piece)
                    p_grad = dot(r.value[ks, pair_at(j)], grad)
                    r.score_grad[j % 2 * 4 + b * 2 + e, ks] = (r.kept[j % 3 * 4 + b * 2 + e, ks].astype(f32) * (p_grad - delta)).astype(bf16)

        def second(j):
            none = jnp.zeros((span, 128), bf16)
            qs = [jnp.where(left == e, query[b, :, pair_at(j)], none) for b, e in tiles]
            gs = [jnp.where(left == e, r.out_grad[b, :, pair_at(j)], none) for b, e in tiles]
            out = [None] * len(tiles)
            for c in range(length // piece):
                ks = pl.ds(c * piece, piece)
                v_grad = k_grad = None
                for i, (b, e) in enumerate(tiles):
                    if c * piece >= spans[b]:
                        continue
                    ds = r.score_grad[j % 2 * 4 + i, ks]
                    v, k = dot(r.kept[j % 3 * 4 + i, ks], gs[i]), dot(ds, qs[i])
                    v_grad, k_grad = (v, k) if v_grad is None else (v_grad + v, k_grad + k)
                    a = dot(r.key_t[pl.ds(mult(j * 128 + e * 64, 64), 64), ks], ds)
                    out[i] = a if out[i] is None else out[i] + a
                r.value_grad[ks, pair_at(j)] = v_grad.astype(bf16)
                r.key_grad[ks, pair_at(j)] = k_grad.astype(bf16)
            for i, (b, e) in enumerate(tiles):
                r.query_grad_t[b, pl.ds(mult(j * 128 + e * 64, 64), 64), :] = (out[i] * 0.125).astype(bf16)

        for j in range(2):
            for b, e in tiles:
                fetch(j, b, e).start()
        first(0)

        @pl.loop(0, pairs - 1)
        def _(j):
            @pl.when(j + 2 < pairs)
            def _():
                for b, e in tiles:
                    fetch(j + 2, b, e).start()
            first(j + 1)
            second(j)
            red.poll_loop(base, pairs - 1, j)
        second(pairs - 1)
        red.poll(base + pairs - 1)
        for b in range(blocks):
            r.query_grad[b] = r.query_grad_t[b].T

    def pair_product(key_weight, value_weight):
        for i in range(length // span):
            at = block_at(i)
            r.part[i] = (dot_t(r.key_grad[at], key_weight[...]) + dot_t(r.value_grad[at], value_weight[...])).astype(bf16)

    def part_copy(k, src, dst, to):
        return pltpu.make_async_remote_copy(src_ref=src, dst_ref=dst, send_sem=part_send.at[k], recv_sem=part_recv.at[k],
            device_id=(me_r, to), device_id_type=MESH)

    def part_flow(turn, out, rest):
        to_core, to_side = me_s + 1 - 2 * core, me_s + 2 - 4 * side
        far, near = 1 - side, side
        copies = (part_copy(3 * turn, r.part.at[2 * far + 1 - core], r.part_core.at[turn, 0], to_core),
            part_copy(3 * turn + 1, r.part.at[2 * near + 1 - core], r.part_core.at[turn, 1], to_core),
            part_copy(3 * turn + 2, r.part_core.at[turn, 0], r.part_side.at[turn], to_side))

        def step(s):
            if s == 0:
                copies[0].start()
                copies[1].start()
            elif s == 1:
                copies[0].wait()
                r.part_core[turn, 0] = (r.part[2 * far + core].astype(f32) + r.part_core[turn, 0].astype(f32) + rest(far)).astype(bf16)
                copies[2].start()
                copies[1].wait()
                out[near] = r.part[2 * near + core].astype(f32) + r.part_core[turn, 1].astype(f32) + rest(near)
            else:
                copies[2].wait()
                out[far] = r.part_side[turn].astype(f32)
        return step

    def output_flow(s):
        there = pltpu.make_async_remote_copy(src_ref=hbm.output_blocks.at[1 - side], dst_ref=r.output.at[side], send_sem=part_send.at[6],
            recv_sem=part_recv.at[6], device_id=(me_r, me_s + 2 - 4 * side), device_id_type=MESH)
        if s == 0:
            there.start()
            pltpu.make_async_copy(hbm.output_blocks.at[side], r.output_own, out_sem.at[0]).start()
        else:
            there.wait()
            pltpu.make_async_copy(hbm.output_blocks.at[side], r.output_own, out_sem.at[0]).wait()
            pltpu.make_async_copy(r.output_own, r.output.at[side], out_sem.at[1]).start()

    def vec_copy(k):
        return pltpu.make_async_remote_copy(src_ref=r.vec, dst_ref=r.vec_landed.at[k], send_sem=vec_send.at[k],
            recv_sem=vec_recv.at[k], device_id=red.partners()[k], device_id_type=MESH)

    def vec_flow(s):
        if s >= 1:
            vec_copy(s - 1).wait()
            r.vec[...] += r.vec_landed[s - 1]
        if s <= 4:
            vec_copy(s).start()
        else:
            r.vector_grads[...] = r.vec[...]

    red.flows = {16: part_flow(0, r.memory_grad, lambda b: 0.0), 18: vec_flow, 19: output_flow,
        17: part_flow(1, r.target_grad, lambda b: r.two_grad[place(b)])}

    need(loads.active, loads.branch_grad)
    for c in range(8):
        if c == 4:
            need(loads.two_low, loads.upward_slope, loads.ffn_out)
            upward_gradient()
        ffn_block(c)
        red.poll()
    need(loads.ffn_in, loads.two_grad)

    @pl.loop(0, tokens // 128)
    def _(i):
        at = pl.ds(mult(i * 128, 128), 128)
        r.two_grad[at] += dot_t(r.upward_slope[at], r.ffn_in[...])
    red.poll()
    need(loads.two_hat, loads.two_rstd, loads.one_hat, loads.one_rstd, loads.cross_output, loads.cross_out, loads.cross_inverse)
    norm_back(r.two_grad, r.two_hat, r.two_rstd, vec[5], vec[1], lambda i: r.one_hat[pl.ds(mult(i * part, part), part)] * vec[3] + vec[4], 0)
    red.poll()
    r.block[8] = sum(dot(r.cross_out[b], r.branch_low[block_at(b)]) for b in range(blocks)).astype(bf16)
    red.poll()
    attention_start(r.cross_output, r.cross_out, r.cross_inverse)
    red.poll()
    need(loads.memory_all, loads.cross_key, loads.cross_value, loads.cross_q)
    keys_again(r.memory_all, r.cross_key, r.cross_value)
    red.poll()
    attention_back(hbm.cross_kept, r.cross_q, (length, length))
    r.block[9] = t_dot(r.memory_all[...], r.key_grad[...]).astype(bf16)
    red.poll()
    r.block[10] = t_dot(r.memory_all[...], r.value_grad[...]).astype(bf16)
    red.poll()
    need(loads.one_low, loads.cross_query)
    r.block[11] = sum(t_dot(r.one_low[block_at(b)], r.query_grad[b]) for b in range(blocks)).astype(bf16)
    red.poll()
    pair_product(r.cross_key, r.cross_value)
    red.poll()
    for b in range(blocks):
        r.two_grad[block_at(b)] += dot_t(r.query_grad[b], r.cross_query[...])
    red.poll()
    need(loads.target_all, loads.self_output, loads.self_out, loads.self_inverse, loads.self_key, loads.self_value, loads.self_q,
        loads.self_query, loads.sums)
    def own_target(i):
        b, inner = i // (span // part), i % (span // part)
        return r.target_all[pl.ds(mult((2 * b + core) * span + inner * part, part), part)].astype(f32)
    norm_back(r.two_grad, r.one_hat, r.one_rstd, vec[3], vec[0], own_target, 3)
    for i in range(3):
        r.vec[pl.ds(i, 1)] = jnp.sum(r.acc[3 + i], axis=0, keepdims=True)
        r.vec[pl.ds(3 + i, 1)] = jnp.sum(r.acc[i], axis=0, keepdims=True)
        r.vec[pl.ds(6 + i, 1)] = jnp.sum(r.sums[i], axis=0, keepdims=True)
    r.vec[pl.ds(9, 7)] = jnp.zeros((7, width), f32)
    red.poll()
    r.block[12] = sum(dot(r.self_out[b], r.branch_low[block_at(b)]) for b in range(blocks)).astype(bf16)
    red.poll()
    attention_start(r.self_output, r.self_out, r.self_inverse)
    red.poll()
    keys_again(r.target_all, r.self_key, r.self_value)
    red.poll()
    attention_back(hbm.self_kept, r.self_q, (length // 2, length))
    r.block[13] = t_dot(r.target_all[...], r.key_grad[...]).astype(bf16)
    red.poll()
    r.block[14] = t_dot(r.target_all[...], r.value_grad[...]).astype(bf16)
    red.poll()
    r.block[15] = sum(t_dot(r.target_all[place(2 * b + core)], r.query_grad[b]) for b in range(blocks)).astype(bf16)
    red.poll()
    pair_product(r.self_key, r.self_value)
    for b in range(blocks):
        r.two_grad[block_at(b)] += dot_t(r.query_grad[b], r.self_query[...])
    red.poll()
    red.poll()
    pltpu.make_async_copy(r.output_own, r.output.at[side], out_sem.at[1]).wait()

def backward_call(o, matrices, vectors, heads=8):
    length, width = o.target_all.shape
    tokens, hidden = o.active.shape
    blocks = o.self_kept.shape[0]
    span = tokens // blocks
    any_, vm = pl.BlockSpec(memory_space=pl.ANY), pl.BlockSpec(memory_space=pltpu.VMEM)
    s = jax.ShapeDtypeStruct
    operands = dict(o._asdict(), **dict(zip(MATRICES + VECTORS, matrices + vectors)))
    count = 8 + 2 * hidden // 512
    outs = BackOut(output=s((blocks, span, width), bf16), reduced=s((count, 512, width), bf16), target_grad=s((blocks, span, width), f32),
        memory_grad=s((blocks, span, width), f32), vector_grads=s((16, width), f32))
    full, near, block = ((length, width), bf16), ((blocks, span, width), bf16), ((blocks, width, span), bf16)
    scratch = BackScratch(block=((count, 512, width), bf16), near=((count, 256, width), bf16), landed=((count, 256, width), bf16),
        key_t=((width, length), bf16), value=full, key_grad=full, value_grad=full,
        score_grad=((8, length, span), bf16), kept=((12, length, span), bf16), part=((length // span, span, width), bf16),
        part_core=((2, 2, span, width), bf16), part_side=((2, span, width), bf16),
        query_grad_t=block, query_grad=near, branch_low=((tokens, width), bf16),
        out_grad_t=block, out_grad=near, delta=((blocks, heads, 8, span), f32),
        vec=((16, width), f32), vec_landed=((5, 16, width), f32), acc=((6, 8, width), f32), output_own=((span, width), bf16))
    dma = pltpu.SemaphoreType.DMA
    return BackOut(*pl.pallas_call(
        functools.partial(backward_kernel, heads),
        out_shape=list(outs),
        in_specs=[vm if k in VECTORS else any_ for k in LOADS + UNLOADED],
        out_specs=[any_, any_, vm, vm, vm],
        scratch_shapes=[pltpu.VMEM(operands[k].shape, operands[k].dtype) for k in LOADS] + [pltpu.VMEM(*k) for k in scratch]
            + [dma((len(LOADS),)), dma((12,)), dma((count,)), dma((count, 10)), dma((count,)), dma((7,)), dma((7,)), dma((5,)), dma((5,)), dma((2,))],
        compiler_params=pltpu.CompilerParams(collective_id=1, has_side_effects=True, vmem_limit_bytes=63 << 20),
        name="backward",
    )(*(operands[k] for k in LOADS + UNLOADED)))

FINISH_BLOCK = (15, 13, 14, 12, 11, 9, 10, 8)
VECTOR_PLACE = (0, 3, 6, 1, 2, 4, 5, 7, 8)

def finish_kernel(reduced, vector_grads, output, target_grad, memory_grad, *refs):
    outs, small, handed = refs[3:13], refs[13:22], refs[:3]
    low, vec, stage, *between, load_sem, store_sem, sem = refs[22:]
    slots, count = stage.shape[0], reduced.shape[0]
    wide = outs[8].shape[1] // 512
    places = [outs[9].at[pl.ds(512 * i, 512)] for i in range(wide)] + [outs[8].at[:, pl.ds(512 * i, 512)] for i in range(wide)]
    places += [None] * 8
    for out, block in zip(outs, FINISH_BLOCK):
        places[block] = out
    loads = [pltpu.make_async_copy(reduced.at[i], low.at[i], load_sem.at[i]) for i in range(count)]
    for copy in loads:
        copy.start()
    arrive = [pltpu.make_async_copy(a, b, sem.at[i]) for i, (a, b) in enumerate(zip((output, target_grad, memory_grad, vector_grads), (*between, vec)))]
    leave = [pltpu.make_async_copy(a, b, sem.at[4 + i]) for i, (a, b) in enumerate(zip(between, handed))]
    for copy in arrive:
        copy.start()
    copies = [pltpu.make_async_copy(stage.at[i % slots], place, store_sem.at[i % slots]) for i, place in enumerate(places)]
    for i, copy in enumerate(copies):
        if i >= slots:
            copies[i - slots].wait()
        loads[i].wait()
        stage[i % slots] = low[i].astype(f32)
        copy.start()
    for copy in arrive:
        copy.wait()
    for copy in leave:
        copy.start()
    for ref, row in zip(small, VECTOR_PLACE):
        ref[...] = vec[row]
    for copy in copies[-slots:] + leave:
        copy.wait()

def finish_call(back, hidden):
    count, rows, width = back.reduced.shape
    any_, vm = pl.BlockSpec(memory_space=pl.ANY), pl.BlockSpec(memory_space=pltpu.VMEM)
    s = jax.ShapeDtypeStruct
    handed = [back.output, back.target_grad, back.memory_grad]
    shapes = [s(a.shape, a.dtype) for a in handed] + [s((width, width), f32)] * 8 + [s((width, hidden), f32), s((hidden, width), f32)]
    dma = pltpu.SemaphoreType.DMA
    return pl.pallas_call(
        finish_kernel,
        out_shape=shapes + [s((width,), f32)] * 9,
        in_specs=[any_] * 5,
        out_specs=[any_] * 13 + [vm] * 9,
        scratch_shapes=[pltpu.VMEM(back.reduced.shape, bf16), pltpu.VMEM((16, width), f32), pltpu.VMEM((8, rows, width), f32)]
            + [pltpu.VMEM(a.shape, a.dtype) for a in handed] + [dma((count,)), dma((8,)), dma((7,))],
        compiler_params=pltpu.CompilerParams(vmem_limit_bytes=62 << 20),
        name="finish",
    )(back.reduced, back.vector_grads, *handed)


def per_device(*args):
    rows, span, width = args[0].shape
    hidden = args[12].shape[1]
    fits = lax.axis_size("rows") == 8 and lax.axis_size("seq") == 4
    if not fits or (rows, span, width, hidden) != (2, 256, 512, 2048) or args[1].shape != args[0].shape:
        return ring_device(*args)
    matrices, vectors = args[4:14], args[14:23]
    kept = forward_call(args[0], args[1], args[2], args[3], matrices, vectors, args[23], HEADS)
    back = backward_call(kept, matrices, vectors, HEADS)
    return tuple(finish_call(back, hidden))


def solution(mesh):
    placed = (
        P("rows", "seq", None),
        P("rows", "seq", None),
        P("rows", None),
        P("rows", None),
        P(),
        P(),
        P(),
        P(),
        P(),
        P(),
        P(),
        P(),
        P(),
        P(),
        P(),
        P(),
        P(),
        P(),
        P(),
        P(),
        P(),
        P(),
        P(),
        P("rows", "seq", None),
    )
    return jax.shard_map(
        per_device,
        mesh=mesh,
        in_specs=placed,
        out_specs=(
            P("rows", "seq", None),
            P("rows", "seq", None),
            P("rows", "seq", None),
            P(),
            P(),
            P(),
            P(),
            P(),
            P(),
            P(),
            P(),
            P(),
            P(),
            P(),
            P(),
            P(),
            P(),
            P(),
            P(),
            P(),
            P(),
            P(),
        ),
        check_vma=False,
    )
```

```python
import functools
import math
from types import SimpleNamespace
from typing import NamedTuple

import jax
import jax.numpy as jnp
from jax import lax
from jax.experimental import pallas as pl
from jax.experimental.pallas import tpu as pltpu
from jax.sharding import PartitionSpec as P

HEADS = 8


masked_score = -1e30


def from_behind(block, axis, distance):
    devices = range(lax.axis_size(axis))
    route = [(i - distance, i) for i in devices if i - distance in devices]
    return lax.ppermute(block, axis, route)


def shifted(block, axis, distance):
    devices = range(lax.axis_size(axis))
    route = [((i - distance) % len(devices), i) for i in devices]
    return lax.ppermute(block, axis, route)


def layer_norm(pre_norm, gain, bias):
    centred = pre_norm - jnp.mean(pre_norm, axis=-1, keepdims=True)
    spread = jnp.mean(centred * centred, axis=-1, keepdims=True)
    return centred * lax.rsqrt(spread + 1e-05) * gain + bias


def residual_norm(previous, branch, omega, gain, bias):
    return layer_norm(previous * omega + branch, gain, bias)


def forward_product(inputs, weight):
    return jnp.dot(inputs, weight, preferred_element_type=jnp.float32)


def weight_product(inputs, grads):
    return jnp.einsum("rsd,rsf->df", inputs, grads, preferred_element_type=jnp.float32)


def input_product(grads, weight):
    return jnp.einsum("rsf,df->rsd", grads, weight, preferred_element_type=jnp.float32)


def split_heads(values, head_count):
    return values.reshape(values.shape[0], values.shape[1], head_count, -1)


def attend_update(running, query_low, key_low, value_low, allowed, score_scale, head_count):
    best, total, accum = running
    raw = (
        jnp.einsum(
            "rqhe,rkhe->rqhk",
            split_heads(query_low, head_count),
            split_heads(key_low, head_count),
            preferred_element_type=jnp.float32,
        )
        * score_scale
    )
    scores = jnp.where(allowed[:, :, None, :], raw, masked_score)
    new_best = jnp.maximum(best, jnp.max(scores, axis=-1))
    weights = jnp.where(allowed[:, :, None, :], jnp.exp(scores - new_best[..., None]), 0.0)
    factor = jnp.exp(best - new_best)
    total = total * factor + jnp.sum(weights, axis=-1)
    accum = accum * factor[..., None] + jnp.einsum(
        "rqhk,rkhe->rqhe",
        weights.astype(jnp.bfloat16),
        split_heads(value_low, head_count),
        preferred_element_type=jnp.float32,
    )
    return (new_best, total, accum)


def attend_grads(
    query_low, key_low, value_low, grad_low, logsum, row_delta, allowed, score_scale, head_count
):
    query_heads = split_heads(query_low, head_count)
    key_heads = split_heads(key_low, head_count)
    value_heads = split_heads(value_low, head_count)
    grad_heads = split_heads(grad_low, head_count)
    raw = (
        jnp.einsum("rqhe,rkhe->rqhk", query_heads, key_heads, preferred_element_type=jnp.float32)
        * score_scale
    )
    scores = jnp.where(allowed[:, :, None, :], raw, masked_score)
    attention_weights = jnp.exp(scores - logsum[..., None])
    value_grad = jnp.einsum(
        "rqhk,rqhe->rkhe",
        attention_weights.astype(jnp.bfloat16),
        grad_heads,
        preferred_element_type=jnp.float32,
    )
    weight_grad = jnp.einsum(
        "rqhe,rkhe->rqhk", grad_heads, value_heads, preferred_element_type=jnp.float32
    )
    score_grad = (attention_weights * (weight_grad - row_delta[..., None])).astype(jnp.bfloat16)
    query_grad = (
        jnp.einsum("rqhk,rkhe->rqhe", score_grad, key_heads, preferred_element_type=jnp.float32)
        * score_scale
    )
    key_grad = (
        jnp.einsum("rqhk,rqhe->rkhe", score_grad, query_heads, preferred_element_type=jnp.float32)
        * score_scale
    )
    query_shape = (query_low.shape[0], query_low.shape[1], query_low.shape[2])
    key_shape = (key_low.shape[0], key_low.shape[1], key_low.shape[2])
    return (
        query_grad.reshape(query_shape),
        key_grad.reshape(key_shape),
        value_grad.reshape(key_shape),
    )


def ring_device(
    target,
    memory,
    target_segments,
    memory_segments,
    self_query,
    self_key,
    self_value,
    self_output,
    cross_query,
    cross_key,
    cross_value,
    cross_output,
    ffn_in,
    ffn_out,
    omega_self,
    omega_cross,
    omega_ffn,
    gain_self,
    bias_self,
    gain_cross,
    bias_cross,
    gain_ffn,
    bias_ffn,
    cotangent,
):
    batch_rows, local_span, model_width = target.shape
    head_count = HEADS
    head_width = model_width // head_count
    score_scale = 1.0 / math.sqrt(head_width)
    self_index = lax.axis_index("seq")
    axis_size = lax.axis_size("seq")
    offsets = jnp.arange(local_span, dtype=jnp.int32)
    local_ids = lax.dynamic_slice_in_dim(target_segments, self_index * local_span, local_span, 1)

    def block_mask(query_source, key_source):
        query_ids = lax.dynamic_slice_in_dim(
            target_segments, query_source * local_span, local_span, 1
        )
        key_ids = lax.dynamic_slice_in_dim(target_segments, key_source * local_span, local_span, 1)
        query_place = query_source * local_span + offsets
        key_place = key_source * local_span + offsets
        matching = query_ids[:, :, None] == key_ids[:, None, :]
        return matching & (key_place[None, None, :] <= query_place[None, :, None])

    empty_state = (
        jnp.full((batch_rows, local_span, head_count), masked_score, jnp.float32),
        jnp.zeros((batch_rows, local_span, head_count), jnp.float32),
        jnp.zeros((batch_rows, local_span, head_count, head_width), jnp.float32),
    )
    self_triple = jnp.concatenate((self_query, self_key, self_value), axis=1)
    triple_low = forward_product(target, self_triple).astype(jnp.bfloat16)
    query_low = triple_low[..., :model_width]
    key_low = triple_low[..., model_width : 2 * model_width]
    value_low = triple_low[..., 2 * model_width :]
    running = attend_update(
        empty_state,
        query_low,
        key_low,
        value_low,
        block_mask(self_index, self_index),
        score_scale,
        head_count,
    )

    def forward_turn(step_index, carry):
        key_pair, running = carry
        key_pair = from_behind((key_pair[0], key_pair[1]), "seq", 1)
        source = (self_index - step_index + axis_size) % axis_size

        def forward_visit(inner):
            return attend_update(
                inner,
                query_low,
                key_pair[0],
                key_pair[1],
                block_mask(self_index, source),
                score_scale,
                head_count,
            )

        running = lax.cond(source <= self_index, forward_visit, lambda inner: inner, running)
        return (key_pair, running)

    key_pair, running = lax.fori_loop(1, axis_size, forward_turn, ((key_low, value_low), running))
    best, total, accum = running
    self_logsum = best + jnp.log(total)
    self_heads = accum / total[..., None]
    self_low = self_heads.reshape(batch_rows, local_span, model_width).astype(jnp.bfloat16)
    self_branch = forward_product(self_low, self_output)
    target_wide = target.astype(jnp.float32)
    hidden_one, pull_one = jax.vjp(
        residual_norm, target_wide, self_branch, omega_self, gain_self, bias_self
    )
    hidden_one_low = hidden_one.astype(jnp.bfloat16)
    cross_query_low = forward_product(hidden_one_low, cross_query).astype(jnp.bfloat16)
    cross_pair = jnp.concatenate((cross_key, cross_value), axis=1)
    memory_pairs = forward_product(
        lax.all_gather(memory, "seq", axis=1, tiled=True), cross_pair
    ).astype(jnp.bfloat16)
    memory_total = memory_pairs.shape[1]
    key_block = 1024
    block_count = memory_total // key_block

    def cross_mask(block_index):
        key_ids = lax.dynamic_slice_in_dim(memory_segments, block_index * key_block, key_block, 1)
        return local_ids[:, :, None] == key_ids[:, None, :]

    def block_pairs(block_index):
        return lax.dynamic_slice_in_dim(memory_pairs, block_index * key_block, key_block, 1)

    def cross_turn(block_index, running):
        pairs = block_pairs(block_index)
        return attend_update(
            running,
            cross_query_low,
            pairs[..., :model_width],
            pairs[..., model_width:],
            cross_mask(block_index),
            score_scale,
            head_count,
        )

    best, total, accum = lax.fori_loop(0, block_count, cross_turn, empty_state)
    cross_logsum = best + jnp.log(total)
    cross_heads = accum / total[..., None]
    cross_low = cross_heads.reshape(batch_rows, local_span, model_width).astype(jnp.bfloat16)
    cross_branch = forward_product(cross_low, cross_output)
    hidden_two, pull_two = jax.vjp(
        residual_norm, hidden_one, cross_branch, omega_cross, gain_cross, bias_cross
    )
    hidden_two_low = hidden_two.astype(jnp.bfloat16)
    upward = forward_product(hidden_two_low, ffn_in)
    activated, pull_gelu = jax.vjp(jax.nn.gelu, upward)
    active_low = activated.astype(jnp.bfloat16)
    ffn_branch = forward_product(active_low, ffn_out)
    result, pull_three = jax.vjp(
        residual_norm, hidden_two, ffn_branch, omega_ffn, gain_ffn, bias_ffn
    )
    two_grad, ffn_branch_grad, omega_ffn_grad, gain_ffn_grad, bias_ffn_grad = pull_three(
        cotangent.astype(jnp.float32)
    )
    ffn_branch_low = ffn_branch_grad.astype(jnp.bfloat16)
    ffn_out_grad = weight_product(active_low, ffn_branch_low)
    upward_grad = pull_gelu(input_product(ffn_branch_low, ffn_out))[0]
    upward_low = upward_grad.astype(jnp.bfloat16)
    ffn_in_grad = weight_product(hidden_two_low, upward_low)
    two_grad = two_grad + input_product(upward_low, ffn_in)
    one_grad, cross_branch_grad, omega_cross_grad, gain_cross_grad, bias_cross_grad = pull_two(
        two_grad
    )
    cross_branch_low = cross_branch_grad.astype(jnp.bfloat16)
    cross_output_grad = weight_product(cross_low, cross_branch_low)
    cross_heads_grad = input_product(cross_branch_low, cross_output).astype(jnp.bfloat16)
    cross_delta = jnp.sum(
        split_heads(cross_heads_grad, head_count).astype(jnp.float32) * cross_heads, axis=-1
    )

    def cross_back(block_index, carry):
        query_grad, pair_grads = carry
        pairs = block_pairs(block_index)
        grads = attend_grads(
            cross_query_low,
            pairs[..., :model_width],
            pairs[..., model_width:],
            cross_heads_grad,
            cross_logsum,
            cross_delta,
            cross_mask(block_index),
            score_scale,
            head_count,
        )
        block_grads = jnp.concatenate((grads[1], grads[2]), axis=2)
        pair_grads = lax.dynamic_update_slice_in_dim(
            pair_grads, block_grads, block_index * key_block, 1
        )
        return (query_grad + grads[0], pair_grads)

    zero_grid = jnp.zeros((batch_rows, local_span, model_width), jnp.float32)
    cross_query_sum, pair_grads = lax.fori_loop(
        0,
        block_count,
        cross_back,
        (zero_grid, jnp.zeros((batch_rows, memory_total, 2 * model_width), jnp.float32)),
    )
    local_pair_grads = lax.psum_scatter(
        pair_grads.astype(jnp.bfloat16), "seq", scatter_dimension=1, tiled=True
    )
    memory_grad = input_product(local_pair_grads, cross_pair)
    pair_weight_grad = weight_product(memory, local_pair_grads)
    cross_query_low_grad = cross_query_sum.astype(jnp.bfloat16)
    cross_query_grad = weight_product(hidden_one_low, cross_query_low_grad)
    one_grad = one_grad + input_product(cross_query_low_grad, cross_query)
    target_residual_grad, self_branch_grad, omega_self_grad, gain_self_grad, bias_self_grad = (
        pull_one(one_grad)
    )
    self_branch_low = self_branch_grad.astype(jnp.bfloat16)
    self_output_grad = weight_product(self_low, self_branch_low)
    self_heads_grad = input_product(self_branch_low, self_output).astype(jnp.bfloat16)
    self_delta = jnp.sum(
        split_heads(self_heads_grad, head_count).astype(jnp.float32) * self_heads, axis=-1
    )

    def key_turn(step_index, carry):
        key_pair, grad_pair, query_grad = carry
        source = (self_index - step_index + axis_size) % axis_size

        def key_visit(inner):
            grads = attend_grads(
                query_low,
                key_pair[0],
                key_pair[1],
                self_heads_grad,
                self_logsum,
                self_delta,
                block_mask(self_index, source),
                score_scale,
                head_count,
            )
            return (inner[0] + grads[0], inner[1] + grads[1], inner[2] + grads[2])

        query_grad, key_grad, value_grad = lax.cond(
            source <= self_index,
            key_visit,
            lambda inner: inner,
            (query_grad, grad_pair[0], grad_pair[1]),
        )
        grad_pair = (
            shifted(key_grad.astype(jnp.bfloat16), "seq", 1).astype(key_grad.dtype),
            shifted(value_grad.astype(jnp.bfloat16), "seq", 1).astype(value_grad.dtype),
        )
        key_pair = from_behind((key_pair[0], key_pair[1]), "seq", 1)
        return (key_pair, grad_pair, query_grad)

    key_pair, grad_pair, query_grad = lax.fori_loop(
        0, axis_size, key_turn, ((key_low, value_low), (zero_grid, zero_grid), zero_grid)
    )
    key_grad, value_grad = grad_pair
    triple_grad_low = jnp.concatenate((query_grad, key_grad, value_grad), axis=2).astype(
        jnp.bfloat16
    )
    target_grad = target_residual_grad + input_product(triple_grad_low, self_triple)
    triple_weight_grad = weight_product(target, triple_grad_low)
    sums = lax.psum(
        (
            triple_weight_grad[:, :model_width],
            triple_weight_grad[:, model_width : 2 * model_width],
            triple_weight_grad[:, 2 * model_width :],
            self_output_grad,
            cross_query_grad,
            pair_weight_grad[:, :model_width],
            pair_weight_grad[:, model_width:],
            cross_output_grad,
            ffn_in_grad,
            ffn_out_grad,
            omega_self_grad,
            omega_cross_grad,
            omega_ffn_grad,
            gain_self_grad,
            bias_self_grad,
            gain_cross_grad,
            bias_cross_grad,
            gain_ffn_grad,
            bias_ffn_grad,
        ),
        ("rows", "seq"),
    )
    return (result.astype(jnp.bfloat16), target_grad, memory_grad) + tuple(sums)


MESH = pl.DeviceIdType.MESH
f32, bf16 = jnp.float32, jnp.bfloat16

def dot(a, b):
    return jnp.dot(a, b, preferred_element_type=f32)

def dot_t(a, b):
    return lax.dot_general(a, b, (((1,), (1,)), ((), ())), preferred_element_type=f32)

def t_dot(a, b):
    return lax.dot_general(a, b, (((0,), (0,)), ((), ())), preferred_element_type=f32)

def mult(i, m):
    return i if isinstance(i, int) else pl.multiple_of(i, m)

def attend_forward(first_block, blocks, keys, key, value_t, query_z, seen, scores, kept, kept_out, kept_sem, out_t, inverse, heads):
    count, piece, slots, queries = blocks * heads, 256, kept.shape[0], seen.shape[2]

    def head_place(i):
        block, head = first_block + i // heads, i % heads
        return block, head, pl.ds(mult(head * 64, 64), 64), pl.ds(mult(head // 2 * 128, 128), 128)

    def first(i, slot):
        block, head, _, pair = head_place(i)
        best = None
        for c in range(keys // piece):
            ks = pl.ds(c * piece, piece)
            s = dot(key[ks, pair], query_z[block, head]) + seen[block, ks]
            scores[slot, ks] = s
            top = jnp.max(s.reshape(piece // 8, 8, queries), axis=0)
            best = top if best is None else jnp.maximum(best, top)
        return best

    def out_copy(i):
        block, head, _, _ = head_place(i)
        return pltpu.make_async_copy(kept.at[i % slots, pl.ds(0, keys)], kept_out.at[block, head, pl.ds(0, keys)], kept_sem.at[i % slots])

    def second(i, slot, best):
        block, head, here, _ = head_place(i)
        best = jnp.max(best, axis=0, keepdims=True)
        total = out = None
        for c in range(keys // piece):
            ks = pl.ds(c * piece, piece)
            p = jnp.exp(scores[slot, ks] - best)
            part = jnp.sum(p.reshape(piece // 8, 8, queries), axis=0)
            total = part if total is None else total + part
            p = p.astype(bf16)
            kept[i % slots, ks] = p
            part = dot(value_t[here, ks], p)
            out = part if out is None else out + part
        scale = 1.0 / jnp.sum(total, axis=0, keepdims=True)
        out_t[block, here, :] = (out * scale).astype(bf16)
        inverse[block, head] = jnp.broadcast_to(scale, (8, queries))

    def body(j, best):
        i = 2 * j
        for e in range(2):
            pl.when(i + e >= slots)(lambda e=e: out_copy(i + e - slots).wait())
        later = first(i + 1, 1)
        second(i, 0, best)
        best = first(jnp.minimum(i + 2, count - 1), 0)
        second(i + 1, 1, later)
        out_copy(i).start()
        out_copy(i + 1).start()
        return best

    lax.fori_loop(0, count // 2, body, first(0, 0))
    for i in range(count - slots, count):
        out_copy(i).wait()

def norm_parts(pre):
    centred = pre - jnp.mean(pre, axis=-1, keepdims=True)
    rstd = lax.rsqrt(jnp.mean(centred * centred, axis=-1, keepdims=True) + 1e-05)
    return centred * rstd, rstd

def pad_pairs(query, query_z, row, heads):
    turned = query.T
    half = lax.broadcasted_iota(jnp.int32, (128, query.shape[0]), 0) // 64
    for head in range(heads):
        pair = turned[head // 2 * 128 : head // 2 * 128 + 128]
        query_z[row, head] = jnp.where(half == head % 2, pair, jnp.zeros_like(pair))

class ForwardIn(NamedTuple):
    target: object
    memory: object
    target_segments: object
    memory_segments: object
    self_query: object
    self_key: object
    self_value: object
    self_output: object
    cross_query: object
    cross_key: object
    cross_value: object
    cross_output: object
    ffn_in: object
    ffn_out: object
    omega_self: object
    omega_cross: object
    omega_ffn: object
    gain_self: object
    bias_self: object
    gain_cross: object
    bias_cross: object
    gain_ffn: object
    bias_ffn: object
    cotangent: object

class ForwardOut(NamedTuple):
    output_blocks: object
    target_all: object
    memory_all: object
    self_kept: object
    cross_kept: object
    self_inverse: object
    cross_inverse: object
    self_out: object
    cross_out: object
    self_q: object
    cross_q: object
    one_low: object
    one_hat: object
    one_rstd: object
    two_low: object
    two_hat: object
    two_rstd: object
    active: object
    upward_slope: object
    branch_grad: object
    two_grad: object
    sums: object

class ForwardScratch(NamedTuple):
    key: object
    value_t: object
    query_z: object
    seen_self: object
    seen_cross: object
    scores: object
    kept: object
    mem_key: object
    mem_value_t: object
    wide: object
    one: object
    two: object
    value_turned: object
    mem_value_turned: object
    grads: object
    up: object

FORWARD_NAMES = ForwardIn._fields + ForwardOut._fields
MATRICES = ForwardIn._fields[4:14]
VECTORS = ForwardIn._fields[14:23]

def forward_kernel(heads, *refs):
    hbm = SimpleNamespace(**dict(zip(FORWARD_NAMES, refs)))
    own = refs[len(FORWARD_NAMES):-5]
    r = SimpleNamespace(**dict(zip(FORWARD_NAMES[2:4] + VECTORS + MATRICES + ForwardOut._fields + ForwardScratch._fields,
        refs[2:4] + refs[14:23] + own)))
    send, recv, local, load_sem, out_sem = refs[-5:]
    kept_sem = local
    me_r, me_s = lax.axis_index("rows"), lax.axis_index("seq")
    core, side = me_s % 2, me_s // 2
    length, width = r.target_all.shape
    tokens = r.one_low.shape[0]
    blocks = 2
    span = tokens // blocks
    other_core, other_side = me_s + 1 - 2 * core, me_s + 2 - 4 * side

    def place(i):
        return pl.ds(mult(i * span, span), span)

    def remote(src, dst, k, to):
        return pltpu.make_async_remote_copy(src_ref=src, dst_ref=dst, send_sem=send.at[k], recv_sem=recv.at[k],
            device_id=(me_r, to), device_id_type=MESH)

    def share(source, full, k):
        mine, theirs = full.at[place(me_s)], full.at[place(other_side)]
        return (pltpu.make_async_copy(source.at[side], mine, load_sem.at[10 + k // 3]), remote(source.at[1 - side], mine, k, other_side),
            remote(source.at[side], mine, k + 1, other_core), remote(theirs, theirs, k + 2, other_core))

    x_own, x_side, x_core, x_pass = share(hbm.target, r.target_all, 0)
    m_own, m_side, m_core, m_pass = share(hbm.memory, r.memory_all, 3)
    g_own = pltpu.make_async_copy(hbm.cotangent.at[side], r.grads.at[side], load_sem.at[12])
    g_side = remote(hbm.cotangent.at[1 - side], r.grads.at[side], 6, other_side)
    x_own.start()
    m_own.start()
    loads = {k: pltpu.make_async_copy(getattr(hbm, k), getattr(r, k), load_sem.at[i]) for i, k in enumerate(MATRICES)}
    for copy in loads.values():
        copy.start()
    g_own.start()
    loads = SimpleNamespace(**loads)
    outs = []

    def emit(*names):
        for k in names:
            copy = pltpu.make_async_copy(getattr(r, k), getattr(hbm, k), out_sem.at[len(outs)])
            copy.start()
            outs.append(copy)

    barrier = pltpu.get_barrier_semaphore()
    for to in (other_core, other_side):
        pl.semaphore_signal(barrier, inc=1, device_id=(me_r, to), device_id_type=MESH)
    pl.semaphore_wait(barrier, 2)
    x_side.start()
    x_core.start()
    m_core.start()

    def masks():
        def line(ids, at):
            first, second = ids[0:1, at], ids[1:2, at]
            return (first + (second - first) * side).astype(f32)
        mine = [line(r.target_segments, pl.ds(mult((2 * b + core) * span, span), span)) for b in range(blocks)]
        for c in range(length // 128):
            at = pl.ds(c * 128, 128)
            key_place = c * 128 + lax.broadcasted_iota(jnp.int32, (128, span), 0)
            query_place = lax.broadcasted_iota(jnp.int32, (128, span), 1)
            for ids, seen, causal in ((r.target_segments, r.seen_self, True), (r.memory_segments, r.seen_cross, False)):
                column = jnp.broadcast_to(line(ids, at), (128, 128)).T
                column = jnp.concatenate([column] * (span // 128), axis=1)
                for b in range(blocks):
                    if causal and c * 128 >= (b + 1) * length // 2:
                        continue
                    same = column == mine[b]
                    if causal:
                        same = same & (key_place <= query_place + (2 * b + core) * span)
                    seen[b, at] = jnp.where(same, 0.0, -1e30)

    def project(full, key_weight, turned, key, value_t, block):
        at = place(block)
        here = full[at]
        key[at] = dot(here, key_weight[...]).astype(bf16)
        value_t[:, at] = dot_t(turned[...], here).astype(bf16)

    def project_self(block):
        project(r.target_all, r.self_key, r.value_turned, r.key, r.value_t, block)

    def project_cross(block):
        project(r.memory_all, r.cross_key, r.mem_value_turned, r.mem_key, r.mem_value_t, block)

    def queries(low, weight, out):
        for b in range(blocks):
            query = (dot(low(b), weight[...]).astype(bf16) * 0.125).astype(bf16)
            out[b] = query
            pad_pairs(query, r.query_z, b, heads)

    masks()
    for k in (loads.self_query, loads.self_key, loads.self_value, loads.cross_key, loads.cross_value):
        k.wait()
    r.value_turned[...] = r.self_value[...].T
    r.mem_value_turned[...] = r.cross_value[...].T
    x_own.wait()
    project_self(me_s)
    x_core.wait()
    project_self(other_core)
    x_side.wait()
    x_pass.start()
    m_side.start()
    queries(lambda b: r.target_all[place(2 * b + core)], r.self_query, r.self_q)
    project_self(other_side)
    m_own.wait()
    project_cross(me_s)
    x_pass.wait()
    project_self(other_side + 1 - 2 * core)
    m_core.wait()
    project_cross(other_core)
    emit(*ForwardOut._fields[1:2], *ForwardOut._fields[9:10])

    def attend(first_block, count, keys, key, value_t, seen, kept_out, out_t, inverse):
        attend_forward(first_block, count, keys, key, value_t, r.query_z, seen, r.scores, r.kept, kept_out, kept_sem, out_t, inverse, heads)

    attend(0, 1, length // 2, r.key, r.value_t, r.seen_self, hbm.self_kept, r.self_out, r.self_inverse)
    attend(1, 1, length, r.key, r.value_t, r.seen_self, hbm.self_kept, r.self_out, r.self_inverse)
    m_side.wait()
    m_pass.start()
    g_side.start()
    loads.self_output.wait()
    vec = [getattr(r, k)[...].reshape(1, width) for k in VECTORS]
    part = 128
    for b in range(blocks):
        r.wide[pl.ds(b * span, span)] = t_dot(r.self_out[b], r.self_output[...])

    @pl.loop(0, tokens // part)
    def _(i):
        at = pl.ds(mult(i * part, part), part)
        b, inner = i // (span // part), i % (span // part)
        x = r.target_all[pl.ds(mult((2 * b + core) * span + inner * part, part), part)].astype(f32)
        hat, rstd = norm_parts(x * vec[0] + r.wide[at])
        one = hat * vec[3] + vec[4]
        r.one_hat[at] = hat
        r.one_rstd[at] = jnp.broadcast_to(rstd, (part, 128))
        r.one[at] = one
        r.one_low[at] = one.astype(bf16)

    loads.cross_query.wait()
    queries(lambda b: r.one_low[pl.ds(b * span, span)], r.cross_query, r.cross_q)
    project_cross(other_side)
    m_pass.wait()
    project_cross(other_side + 1 - 2 * core)
    emit(*ForwardOut._fields[2:3], *ForwardOut._fields[5:6], *ForwardOut._fields[7:8], *ForwardOut._fields[10:14])
    attend(0, 2, length, r.mem_key, r.mem_value_t, r.seen_cross, hbm.cross_kept, r.cross_out, r.cross_inverse)
    loads.cross_output.wait()
    for b in range(blocks):
        r.wide[pl.ds(b * span, span)] = t_dot(r.cross_out[b], r.cross_output[...])

    @pl.loop(0, tokens // part)
    def _(i):
        at = pl.ds(mult(i * part, part), part)
        hat, rstd = norm_parts(r.one[at] * vec[1] + r.wide[at])
        two = hat * vec[5] + vec[6]
        r.two_hat[at] = hat
        r.two_rstd[at] = jnp.broadcast_to(rstd, (part, 128))
        r.two[at] = two
        r.two_low[at] = two.astype(bf16)

    emit(*ForwardOut._fields[6:7], *ForwardOut._fields[8:9], *ForwardOut._fields[14:17])
    loads.ffn_in.wait()
    loads.ffn_out.wait()
    c0 = math.sqrt(2.0 / math.pi)
    pieces = r.ffn_in.shape[1] // 512
    r.wide[...] = jnp.zeros_like(r.wide)

    halves = [pl.ds(half * (tokens // 2), tokens // 2) for half in range(2)]

    def up(j, half):
        r.up[half] = dot(r.two_low[halves[half]], r.ffn_in[:, pl.ds(mult(j * 512, 512), 512)])

    def down(j, half):
        at, cols = halves[half], pl.ds(mult(j * 512, 512), 512)
        u = r.up[half]
        square = u * u
        t = jnp.tanh(u * (c0 + (c0 * 0.044715) * square))
        rise = 0.5 + 0.5 * t
        active = (u * rise).astype(bf16)
        r.active[at, cols] = active
        r.upward_slope[at, cols] = (rise + u * (rise * (1.0 - t)) * (c0 + (3 * 0.044715 * c0) * square)).astype(bf16)
        r.wide[at] += dot(active, r.ffn_out[cols, :])

    up(0, 0)

    @pl.loop(0, pieces)
    def _(j):
        up(j, 1)
        down(j, 0)
        up(jnp.minimum(j + 1, pieces - 1), 0)
        down(j, 1)

    emit(*ForwardOut._fields[17:19])
    g_own.wait()
    g_side.wait()
    r.sums[...] = jnp.zeros_like(r.sums)

    @pl.loop(0, tokens // part)
    def _(i):
        at = pl.ds(mult(i * part, part), part)
        b, inner = i // (span // part), i % (span // part)
        near = pl.ds(mult(inner * part, part), part)
        two = r.two[at]
        hat, rstd = norm_parts(two * vec[2] + r.wide[at])
        r.output_blocks[b, near] = (hat * vec[7] + vec[8]).astype(bf16)
        grad = r.grads[b, near].astype(f32)
        scaled = grad * vec[7]
        back = rstd * (scaled - jnp.mean(scaled, axis=-1, keepdims=True) - hat * jnp.mean(scaled * hat, axis=-1, keepdims=True))
        r.branch_grad[at] = back.astype(bf16)
        r.two_grad[at] = back * vec[2]
        r.sums[0] += jnp.sum((back * two).reshape(part // 8, 8, width), axis=0)
        r.sums[1] += jnp.sum((grad * hat).reshape(part // 8, 8, width), axis=0)
        r.sums[2] += jnp.sum(grad.reshape(part // 8, 8, width), axis=0)

    emit(*ForwardOut._fields[:1], *ForwardOut._fields[19:])

    for copy in outs:
        copy.wait()

def forward_call(target, memory, target_segments, memory_segments, matrices, vectors, cotangent, heads=8):
    blocks, span, width = target.shape
    length = target_segments.shape[1]
    tokens = blocks * span
    hidden = matrices[8].shape[1]
    any_, vm = pl.BlockSpec(memory_space=pl.ANY), pl.BlockSpec(memory_space=pltpu.VMEM)
    s = jax.ShapeDtypeStruct
    full, wide, seen = ((length, width), bf16), ((tokens, width), f32), ((blocks, length, span), f32)
    kept, inverse = s((blocks, heads, length, span), bf16), s((blocks, heads, 8, span), f32)
    outs = ForwardOut(output_blocks=s((blocks, span, width), bf16), target_all=s(*full), memory_all=s(*full),
        self_kept=kept, cross_kept=kept, self_inverse=inverse, cross_inverse=inverse,
        self_out=s((blocks, width, span), bf16), cross_out=s((blocks, width, span), bf16),
        self_q=s((blocks, span, width), bf16), cross_q=s((blocks, span, width), bf16),
        one_low=s((tokens, width), bf16), one_hat=s(*wide), one_rstd=s((tokens, 128), f32),
        two_low=s((tokens, width), bf16), two_hat=s(*wide), two_rstd=s((tokens, 128), f32),
        active=s((tokens, hidden), bf16), upward_slope=s((tokens, hidden), bf16), branch_grad=s((tokens, width), bf16),
        two_grad=s(*wide), sums=s((3, 8, width), f32))
    turned = ((width, length), bf16)
    scratch = ForwardScratch(key=full, value_t=turned, query_z=((blocks, heads, 128, span), bf16),
        seen_self=seen, seen_cross=seen, scores=((2, length, span), f32),
        kept=((4, length, span), bf16), mem_key=full, mem_value_t=turned,
        wide=wide, one=wide, two=wide,
        value_turned=((width, width), bf16), mem_value_turned=((width, width), bf16), grads=((blocks, span, width), bf16), up=((2, tokens // 2, 512), f32))
    held = [((8, 128), f32) if k in ForwardOut._fields[3:5] else (o.shape, o.dtype) for k, o in zip(ForwardOut._fields, outs)]
    held = [(m.shape, m.dtype) for m in matrices] + held + list(scratch)
    dma = pltpu.SemaphoreType.DMA
    return ForwardOut(*pl.pallas_call(
        functools.partial(forward_kernel, heads),
        out_shape=list(outs),
        in_specs=[any_] * 2 + [vm] * 2 + [any_] * 10 + [vm] * 9 + [any_],
        out_specs=[any_] * len(outs),
        scratch_shapes=[pltpu.VMEM(*k) for k in held] + [dma((7,)), dma((7,)), dma((4,)), dma((13,)), dma((20,))],
        compiler_params=pltpu.CompilerParams(collective_id=0, has_side_effects=True, vmem_limit_bytes=62 << 20),
        name="forward",
    )(target, memory, target_segments, memory_segments, *matrices, *vectors, cotangent))

CLASSES = (0, 4, 0, 1, 1, 1, 0, 0, 2, 4, 1, 4, 1, 1, 4, 1)
PLAN = (
    (0,),
    (19, 1),
    (2,),
    (3,),
    (1, 0, 2, 4),
    (3, 5),
    (6,),
    (7,),
    (4, 5),
    (19, 1, 7, 6),
    (8,),
    (),
    (),
    (3, 1, 0, 8),
    (2, 4),
    (),
    (1, 7, 5),
    (9, 0),
    (10, 8),
    (11, 2),
    (16, 1, 6, 9, 3, 7, 10, 0),
    (11,),
    (18, 1, 4),
    (12, 2),
    (16, 3, 6, 5, 8),
    (18, 7, 0),
    (12, 1, 9, 10, 2, 4),
    (3, 6),
    (7, 0, 11, 5, 8),
    (),
    (1, 13, 10),
    (14, 16),
    (15, 18, 9, 2),
    (17, 3, 13, 7, 6, 14, 4),
    (15, 12, 0, 8, 1, 18, 11, 5, 17, 10, 1, 9, 13, 2, 14, 3, 7, 12, 6, 4, 15, 18, 13, 11, 0, 5, 8, 10, 3, 15, 14, 12, 6, 4, 0, 18, 8, 17, 13, 9, 5, 10, 0, 2, 4, 15, 14, 7, 12, 11, 5, 8, 13, 10, 3, 15, 12, 2, 6, 9, 3, 2, 7, 8, 13, 15, 4, 14, 10, 12, 11, 9, 7, 8, 13, 4, 15, 6, 5, 14, 11, 12, 9, 6, 13, 5, 10, 14, 15, 11, 10, 12, 9, 14, 12, 13, 9, 11, 13, 15, 11, 14, 15, 14),
)

class Reduction:
    def __init__(self, block, near, landed, reduced, send, recv, own):
        self.block, self.near, self.landed, self.reduced = block, near, landed, reduced
        self.send, self.recv, self.own = send, recv, own
        self.r, self.s = lax.axis_index("rows"), lax.axis_index("seq")
        self.core, self.y = self.s % 2, self.s // 2
        self.x, self.z0, self.z1 = self.r % 2, (self.r // 2) % 2, self.r // 4
        self.count, self.size = block.shape[0], block.shape[1]
        x, y, z0, z1 = self.x, self.y, self.z0, self.z1
        core, ax, ay = (0, 1 - 2 * self.core, self.core), (1 - 2 * x, 0, x), (0, 2 - 4 * y, y)
        an, af = (2 - 4 * z0, 0, z0), (4 - 8 * z1, 0, z1)
        self.orders = ((core, ax, ay, an, af), (core, ay, ax, an, af), (core, an, af, ax, ay), (core, an, af, ay, ax), (core, ax, an, af, ay), (core, ay, an, af, ax))
        self.flows, self.turn, done = {}, 0, {}
        self.polls = []
        for entry in PLAN:
            self.polls.append([(c, done.setdefault(c, []).append(0) or len(done[c]) - 1) for c in entry])

    def partners(self):
        r, s = self.r, self.s
        return ((r, s + 1 - 2 * self.core), (r, s + 2 - 4 * self.y), (r + 1 - 2 * self.x, s),
                (r + 2 - 4 * self.z0, s), (r + 4 - 8 * self.z1, s))

    def start_of(self, j, hops):
        off = 0
        for i in range(j):
            off = off + hops[i][2] * (self.size >> (i + 1))
        return off

    def landing(self, c, j):
        half = self.size >> (j + 1)
        if j == 0:
            return self.near.at[c]
        return self.landed.at[c, pl.ds(self.size // 2 - (self.size >> j), half)]

    def copy(self, c, j, gather):
        hops = self.orders[CLASSES[c]]
        off, half = self.start_of(j, hops), self.size >> (j + 1)
        dr, ds, bit = hops[j]
        if gather:
            mine = pl.ds(pl.multiple_of(off + bit * half, 16), half)
            src, dst = (self.block if j == 4 else self.reduced).at[c, mine], self.reduced.at[c, mine]
        else:
            src, dst = self.block.at[c, pl.ds(pl.multiple_of(off + (1 - bit) * half, 16), half)], self.landing(c, j)
        return pltpu.make_async_remote_copy(src_ref=src, dst_ref=dst, send_sem=self.send.at[c],
            recv_sem=self.recv.at[c, j + 5 * gather], device_id=(self.r + dr, self.s + ds), device_id_type=MESH)

    def own_copy(self, c):
        mine = pl.ds(pl.multiple_of(self.start_of(5, self.orders[CLASSES[c]]), 16), self.size >> 5)
        return pltpu.make_async_copy(self.block.at[c, mine], self.reduced.at[c, mine], self.own.at[c])

    def add(self, c, j):
        keep = pl.ds(pl.multiple_of(self.start_of(j + 1, self.orders[CLASSES[c]]), 16), self.size >> (j + 1))
        self.block[c, keep] = (self.block[c, keep].astype(f32) + self.landing(c, j)[...].astype(f32)).astype(bf16)

    def step(self, c, s):
        if c >= self.count:
            return self.flows[c](s)
        if 1 <= s <= 5:
            self.copy(c, s - 1, 0).wait()
            self.add(c, s - 1)
        elif s > 5:
            self.copy(c, 10 - s, 1).wait()
        if s == 5:
            self.own_copy(c).start()
        elif s == 6:
            self.own_copy(c).wait()
        if s <= 4:
            self.copy(c, s, 0).start()
        elif s <= 9:
            self.copy(c, 9 - s, 1).start()

    def poll(self, index=None):
        if index is None:
            index = self.turn
            self.turn += 1
        for c, s in self.polls[index]:
            self.step(c, s)

    def poll_loop(self, base, count, i):
        for k in range(count):
            if self.polls[base + k]:
                @pl.when(i == k)
                def _():
                    self.poll(base + k)

class Loads(NamedTuple):
    active: object
    branch_grad: object
    two_low: object
    upward_slope: object
    ffn_out: object
    ffn_in: object
    two_grad: object
    two_hat: object
    two_rstd: object
    one_hat: object
    one_rstd: object
    cross_output: object
    cross_out: object
    cross_inverse: object
    memory_all: object
    cross_key: object
    cross_value: object
    cross_q: object
    one_low: object
    cross_query: object
    target_all: object
    self_output: object
    self_out: object
    self_inverse: object
    self_key: object
    self_value: object
    self_q: object
    self_query: object
    sums: object

class BackOut(NamedTuple):
    output: object
    reduced: object
    target_grad: object
    memory_grad: object
    vector_grads: object

class BackScratch(NamedTuple):
    block: object
    near: object
    landed: object
    key_t: object
    value: object
    key_grad: object
    value_grad: object
    score_grad: object
    kept: object
    part: object
    part_core: object
    part_side: object
    query_grad_t: object
    query_grad: object
    branch_low: object
    out_grad_t: object
    out_grad: object
    delta: object
    vec: object
    vec_landed: object
    acc: object
    output_own: object

LOADS = Loads._fields
UNLOADED = ForwardOut._fields[3:5] + ForwardOut._fields[:1] + VECTORS

def backward_kernel(heads, *refs):
    n = len(LOADS + UNLOADED)
    hbm = SimpleNamespace(**dict(zip(LOADS + UNLOADED, refs)))
    r = SimpleNamespace(**dict(zip(BackOut._fields + LOADS + BackScratch._fields, refs[n:])))
    load_sem, kept_sem, send, recv, own_sem, part_send, part_recv, vec_send, vec_recv, out_sem = refs[-10:]
    length, width = r.memory_all.shape
    tokens = r.two_low.shape[0]
    blocks = 2
    span = tokens // blocks
    red = Reduction(r.block, r.near, r.landed, r.reduced, send, recv, own_sem)
    me_r, me_s, core, side = red.r, red.s, red.core, red.y

    loads = Loads(*[pltpu.make_async_copy(getattr(hbm, k), getattr(r, k), load_sem.at[i]) for i, k in enumerate(LOADS)])
    for copy in loads:
        copy.start()

    def need(*copies):
        for copy in copies:
            copy.wait()

    barrier = pltpu.get_barrier_semaphore()
    for to in red.partners():
        pl.semaphore_signal(barrier, inc=1, device_id=to, device_id_type=MESH)
    pl.semaphore_wait(barrier, 5)

    def block_at(b):
        return pl.ds(b * span, span)

    def place(i):
        return pl.ds(mult(i * span, span), span)

    def ffn_block(c):
        if c < 4:
            r.block[c] = t_dot(r.active[:, pl.ds(c * 512, 512)], r.branch_grad[...]).astype(bf16)
        else:
            r.block[c] = t_dot(r.two_low[...], r.upward_slope[:, pl.ds((c - 4) * 512, 512)]).astype(bf16)

    def upward_gradient():
        @pl.loop(0, r.upward_slope.shape[1] // 512)
        def _(j):
            cols = pl.ds(mult(j * 512, 512), 512)
            for b in range(blocks):
                grad = dot_t(r.branch_grad[block_at(b)], r.ffn_out[cols, :])
                r.upward_slope[block_at(b), cols] = (grad * r.upward_slope[block_at(b), cols].astype(f32)).astype(bf16)

    vec = [getattr(hbm, k)[...].reshape(1, width) for k in VECTORS]
    part = 128

    def norm_back(grad_ref, hat_ref, rstd_ref, gain, omega, previous, slot):
        for i in range(3):
            r.acc[slot + i] = jnp.zeros_like(r.acc[slot + i])

        @pl.loop(0, tokens // part)
        def _(i):
            at = pl.ds(mult(i * part, part), part)
            hat, grad = hat_ref[at], grad_ref[at]
            scaled = grad * gain
            back = rstd_ref[at][:, 0:1] * (scaled - jnp.mean(scaled, axis=-1, keepdims=True)
                - hat * jnp.mean(scaled * hat, axis=-1, keepdims=True))
            r.branch_low[at] = back.astype(bf16)
            grad_ref[at] = back * omega
            for k, term in enumerate((back * previous(i), grad * hat, grad)):
                r.acc[slot + k] += jnp.sum(term.reshape(part // 8, 8, width), axis=0)

    def attention_start(weight, out_t, inverse):
        for b in range(blocks):
            grad_t = dot_t(weight[...], r.branch_low[block_at(b)])
            for head in range(heads):
                here = pl.ds(head * 64, 64)
                scaled = grad_t[head * 64 : head * 64 + 64] * inverse[b, head][0:1]
                r.out_grad_t[b, here] = scaled.astype(bf16)
                delta = jnp.sum(scaled * out_t[b, here].astype(f32), axis=0, keepdims=True)
                r.delta[b, head] = jnp.broadcast_to(delta, (8, span))
            r.out_grad[b] = r.out_grad_t[b].T

    def keys_again(full, key_weight, value_weight):
        key_turned = key_weight[...].T
        for c in range(length // 512):
            at = pl.ds(c * 512, 512)
            here = full[at]
            r.key_t[:, at] = dot_t(key_turned, here).astype(bf16)
            r.value[at] = dot(here, value_weight[...]).astype(bf16)

    def attention_back(kept_hbm, query, spans):
        base = red.turn
        pairs, piece = heads // 2, 256
        red.turn += pairs
        tiles = [(b, e) for b in range(blocks) for e in range(2)]
        top = lax.broadcasted_iota(jnp.int32, (128, span), 0) // 64
        left = lax.broadcasted_iota(jnp.int32, (span, 128), 1) // 64

        def pair_at(j):
            return pl.ds(mult(j * 128, 128), 128)

        def fetch(j, b, e):
            slot, ks = j % 3 * 4 + b * 2 + e, pl.ds(0, spans[b])
            return pltpu.make_async_copy(kept_hbm.at[b, 2 * j + e, ks], r.kept.at[slot, ks], kept_sem.at[slot])

        def first(j):
            for b, e in tiles:
                fetch(j, b, e).wait()
            for b, e in tiles:
                grad = jnp.where(top == e, r.out_grad_t[b, pair_at(j), :], jnp.zeros((128, span), bf16))
                delta = r.delta[b, 2 * j + e][0:1]
                for c in range(spans[b] // piece):
                    ks = pl.ds(c * piece, piece)
                    p_grad = dot(r.value[ks, pair_at(j)], grad)
                    r.score_grad[j % 2 * 4 + b * 2 + e, ks] = (r.kept[j % 3 * 4 + b * 2 + e, ks].astype(f32) * (p_grad - delta)).astype(bf16)

        def second(j):
            none = jnp.zeros((span, 128), bf16)
            qs = [jnp.where(left == e, query[b, :, pair_at(j)], none) for b, e in tiles]
            gs = [jnp.where(left == e, r.out_grad[b, :, pair_at(j)], none) for b, e in tiles]
            out = [None] * len(tiles)
            for c in range(length // piece):
                ks = pl.ds(c * piece, piece)
                v_grad = k_grad = None
                for i, (b, e) in enumerate(tiles):
                    if c * piece >= spans[b]:
                        continue
                    ds = r.score_grad[j % 2 * 4 + i, ks]
                    v, k = dot(r.kept[j % 3 * 4 + i, ks], gs[i]), dot(ds, qs[i])
                    v_grad, k_grad = (v, k) if v_grad is None else (v_grad + v, k_grad + k)
                    a = dot(r.key_t[pl.ds(mult(j * 128 + e * 64, 64), 64), ks], ds)
                    out[i] = a if out[i] is None else out[i] + a
                r.value_grad[ks, pair_at(j)] = v_grad.astype(bf16)
                r.key_grad[ks, pair_at(j)] = k_grad.astype(bf16)
            for i, (b, e) in enumerate(tiles):
                r.query_grad_t[b, pl.ds(mult(j * 128 + e * 64, 64), 64), :] = (out[i] * 0.125).astype(bf16)

        for j in range(2):
            for b, e in tiles:
                fetch(j, b, e).start()
        first(0)

        @pl.loop(0, pairs - 1)
        def _(j):
            @pl.when(j + 2 < pairs)
            def _():
                for b, e in tiles:
                    fetch(j + 2, b, e).start()
            first(j + 1)
            second(j)
            red.poll_loop(base, pairs - 1, j)
        second(pairs - 1)
        red.poll(base + pairs - 1)
        for b in range(blocks):
            r.query_grad[b] = r.query_grad_t[b].T

    def pair_product(key_weight, value_weight):
        for i in range(length // span):
            at = block_at(i)
            r.part[i] = (dot_t(r.key_grad[at], key_weight[...]) + dot_t(r.value_grad[at], value_weight[...])).astype(bf16)

    def part_copy(k, src, dst, to):
        return pltpu.make_async_remote_copy(src_ref=src, dst_ref=dst, send_sem=part_send.at[k], recv_sem=part_recv.at[k],
            device_id=(me_r, to), device_id_type=MESH)

    def part_flow(turn, out, rest):
        to_core, to_side = me_s + 1 - 2 * core, me_s + 2 - 4 * side
        far, near = 1 - side, side
        copies = (part_copy(3 * turn, r.part.at[2 * far + 1 - core], r.part_core.at[turn, 0], to_core),
            part_copy(3 * turn + 1, r.part.at[2 * near + 1 - core], r.part_core.at[turn, 1], to_core),
            part_copy(3 * turn + 2, r.part_core.at[turn, 0], r.part_side.at[turn], to_side))

        def step(s):
            if s == 0:
                copies[0].start()
                copies[1].start()
            elif s == 1:
                copies[0].wait()
                r.part_core[turn, 0] = (r.part[2 * far + core].astype(f32) + r.part_core[turn, 0].astype(f32) + rest(far)).astype(bf16)
                copies[2].start()
                copies[1].wait()
                out[near] = r.part[2 * near + core].astype(f32) + r.part_core[turn, 1].astype(f32) + rest(near)
            else:
                copies[2].wait()
                out[far] = r.part_side[turn].astype(f32)
        return step

    def output_flow(s):
        there = pltpu.make_async_remote_copy(src_ref=hbm.output_blocks.at[1 - side], dst_ref=r.output.at[side], send_sem=part_send.at[6],
            recv_sem=part_recv.at[6], device_id=(me_r, me_s + 2 - 4 * side), device_id_type=MESH)
        if s == 0:
            there.start()
            pltpu.make_async_copy(hbm.output_blocks.at[side], r.output_own, out_sem.at[0]).start()
        else:
            there.wait()
            pltpu.make_async_copy(hbm.output_blocks.at[side], r.output_own, out_sem.at[0]).wait()
            pltpu.make_async_copy(r.output_own, r.output.at[side], out_sem.at[1]).start()

    def vec_copy(k):
        return pltpu.make_async_remote_copy(src_ref=r.vec, dst_ref=r.vec_landed.at[k], send_sem=vec_send.at[k],
            recv_sem=vec_recv.at[k], device_id=red.partners()[k], device_id_type=MESH)

    def vec_flow(s):
        if s >= 1:
            vec_copy(s - 1).wait()
            r.vec[...] += r.vec_landed[s - 1]
        if s <= 4:
            vec_copy(s).start()
        else:
            r.vector_grads[...] = r.vec[...]

    red.flows = {16: part_flow(0, r.memory_grad, lambda b: 0.0), 18: vec_flow, 19: output_flow,
        17: part_flow(1, r.target_grad, lambda b: r.two_grad[place(b)])}

    need(loads.active, loads.branch_grad)
    for c in range(8):
        if c == 4:
            need(loads.two_low, loads.upward_slope, loads.ffn_out)
            upward_gradient()
        ffn_block(c)
        red.poll()
    need(loads.ffn_in, loads.two_grad)

    @pl.loop(0, tokens // 128)
    def _(i):
        at = pl.ds(mult(i * 128, 128), 128)
        r.two_grad[at] += dot_t(r.upward_slope[at], r.ffn_in[...])
    red.poll()
    need(loads.two_hat, loads.two_rstd, loads.one_hat, loads.one_rstd, loads.cross_output, loads.cross_out, loads.cross_inverse)
    norm_back(r.two_grad, r.two_hat, r.two_rstd, vec[5], vec[1], lambda i: r.one_hat[pl.ds(mult(i * part, part), part)] * vec[3] + vec[4], 0)
    red.poll()
    r.block[8] = sum(dot(r.cross_out[b], r.branch_low[block_at(b)]) for b in range(blocks)).astype(bf16)
    red.poll()
    attention_start(r.cross_output, r.cross_out, r.cross_inverse)
    red.poll()
    need(loads.memory_all, loads.cross_key, loads.cross_value, loads.cross_q)
    keys_again(r.memory_all, r.cross_key, r.cross_value)
    red.poll()
    attention_back(hbm.cross_kept, r.cross_q, (length, length))
    r.block[9] = t_dot(r.memory_all[...], r.key_grad[...]).astype(bf16)
    red.poll()
    r.block[10] = t_dot(r.memory_all[...], r.value_grad[...]).astype(bf16)
    red.poll()
    need(loads.one_low, loads.cross_query)
    r.block[11] = sum(t_dot(r.one_low[block_at(b)], r.query_grad[b]) for b in range(blocks)).astype(bf16)
    red.poll()
    pair_product(r.cross_key, r.cross_value)
    red.poll()
    for b in range(blocks):
        r.two_grad[block_at(b)] += dot_t(r.query_grad[b], r.cross_query[...])
    red.poll()
    need(loads.target_all, loads.self_output, loads.self_out, loads.self_inverse, loads.self_key, loads.self_value, loads.self_q,
        loads.self_query, loads.sums)
    def own_target(i):
        b, inner = i // (span // part), i % (span // part)
        return r.target_all[pl.ds(mult((2 * b + core) * span + inner * part, part), part)].astype(f32)
    norm_back(r.two_grad, r.one_hat, r.one_rstd, vec[3], vec[0], own_target, 3)
    for i in range(3):
        r.vec[pl.ds(i, 1)] = jnp.sum(r.acc[3 + i], axis=0, keepdims=True)
        r.vec[pl.ds(3 + i, 1)] = jnp.sum(r.acc[i], axis=0, keepdims=True)
        r.vec[pl.ds(6 + i, 1)] = jnp.sum(r.sums[i], axis=0, keepdims=True)
    r.vec[pl.ds(9, 7)] = jnp.zeros((7, width), f32)
    red.poll()
    r.block[12] = sum(dot(r.self_out[b], r.branch_low[block_at(b)]) for b in range(blocks)).astype(bf16)
    red.poll()
    attention_start(r.self_output, r.self_out, r.self_inverse)
    red.poll()
    keys_again(r.target_all, r.self_key, r.self_value)
    red.poll()
    attention_back(hbm.self_kept, r.self_q, (length // 2, length))
    r.block[13] = t_dot(r.target_all[...], r.key_grad[...]).astype(bf16)
    red.poll()
    r.block[14] = t_dot(r.target_all[...], r.value_grad[...]).astype(bf16)
    red.poll()
    r.block[15] = sum(t_dot(r.target_all[place(2 * b + core)], r.query_grad[b]) for b in range(blocks)).astype(bf16)
    red.poll()
    pair_product(r.self_key, r.self_value)
    for b in range(blocks):
        r.two_grad[block_at(b)] += dot_t(r.query_grad[b], r.self_query[...])
    red.poll()
    red.poll()
    pltpu.make_async_copy(r.output_own, r.output.at[side], out_sem.at[1]).wait()

def backward_call(o, matrices, vectors, heads=8):
    length, width = o.target_all.shape
    tokens, hidden = o.active.shape
    blocks = o.self_kept.shape[0]
    span = tokens // blocks
    any_, vm = pl.BlockSpec(memory_space=pl.ANY), pl.BlockSpec(memory_space=pltpu.VMEM)
    s = jax.ShapeDtypeStruct
    operands = dict(o._asdict(), **dict(zip(MATRICES + VECTORS, matrices + vectors)))
    count = 8 + 2 * hidden // 512
    outs = BackOut(output=s((blocks, span, width), bf16), reduced=s((count, 512, width), bf16), target_grad=s((blocks, span, width), f32),
        memory_grad=s((blocks, span, width), f32), vector_grads=s((16, width), f32))
    full, near, block = ((length, width), bf16), ((blocks, span, width), bf16), ((blocks, width, span), bf16)
    scratch = BackScratch(block=((count, 512, width), bf16), near=((count, 256, width), bf16), landed=((count, 256, width), bf16),
        key_t=((width, length), bf16), value=full, key_grad=full, value_grad=full,
        score_grad=((8, length, span), bf16), kept=((12, length, span), bf16), part=((length // span, span, width), bf16),
        part_core=((2, 2, span, width), bf16), part_side=((2, span, width), bf16),
        query_grad_t=block, query_grad=near, branch_low=((tokens, width), bf16),
        out_grad_t=block, out_grad=near, delta=((blocks, heads, 8, span), f32),
        vec=((16, width), f32), vec_landed=((5, 16, width), f32), acc=((6, 8, width), f32), output_own=((span, width), bf16))
    dma = pltpu.SemaphoreType.DMA
    return BackOut(*pl.pallas_call(
        functools.partial(backward_kernel, heads),
        out_shape=list(outs),
        in_specs=[vm if k in VECTORS else any_ for k in LOADS + UNLOADED],
        out_specs=[any_, any_, vm, vm, vm],
        scratch_shapes=[pltpu.VMEM(operands[k].shape, operands[k].dtype) for k in LOADS] + [pltpu.VMEM(*k) for k in scratch]
            + [dma((len(LOADS),)), dma((12,)), dma((count,)), dma((count, 10)), dma((count,)), dma((7,)), dma((7,)), dma((5,)), dma((5,)), dma((2,))],
        compiler_params=pltpu.CompilerParams(collective_id=1, has_side_effects=True, vmem_limit_bytes=63 << 20),
        name="backward",
    )(*(operands[k] for k in LOADS + UNLOADED)))

FINISH_BLOCK = (15, 13, 14, 12, 11, 9, 10, 8)
VECTOR_PLACE = (0, 3, 6, 1, 2, 4, 5, 7, 8)

def finish_kernel(reduced, vector_grads, output, target_grad, memory_grad, *refs):
    outs, small, handed = refs[3:13], refs[13:22], refs[:3]
    low, vec, stage, *between, load_sem, store_sem, sem = refs[22:]
    slots, count = stage.shape[0], reduced.shape[0]
    wide = outs[8].shape[1] // 512
    places = [outs[9].at[pl.ds(512 * i, 512)] for i in range(wide)] + [outs[8].at[:, pl.ds(512 * i, 512)] for i in range(wide)]
    places += [None] * 8
    for out, block in zip(outs, FINISH_BLOCK):
        places[block] = out
    loads = [pltpu.make_async_copy(reduced.at[i], low.at[i], load_sem.at[i]) for i in range(count)]
    ahead = 4
    for copy in loads[:ahead]:
        copy.start()
    arrive = [pltpu.make_async_copy(a, b, sem.at[i]) for i, (a, b) in enumerate(zip((output, target_grad, memory_grad, vector_grads), (*between, vec)))]
    leave = [pltpu.make_async_copy(a, b, sem.at[4 + i]) for i, (a, b) in enumerate(zip(between, handed))]
    for copy in arrive:
        copy.start()
    copies = [pltpu.make_async_copy(stage.at[i % slots], place, store_sem.at[i % slots]) for i, place in enumerate(places)]
    for i, copy in enumerate(copies):
        if i >= slots:
            copies[i - slots].wait()
        if i + ahead < count:
            loads[i + ahead].start()
        loads[i].wait()
        stage[i % slots] = low[i].astype(f32)
        copy.start()
    for copy in arrive:
        copy.wait()
    for copy in leave:
        copy.start()
    for ref, row in zip(small, VECTOR_PLACE):
        ref[...] = vec[row]
    for copy in copies[-slots:] + leave:
        copy.wait()

def finish_call(back, hidden):
    count, rows, width = back.reduced.shape
    any_, vm = pl.BlockSpec(memory_space=pl.ANY), pl.BlockSpec(memory_space=pltpu.VMEM)
    s = jax.ShapeDtypeStruct
    handed = [back.output, back.target_grad, back.memory_grad]
    shapes = [s(a.shape, a.dtype) for a in handed] + [s((width, width), f32)] * 8 + [s((width, hidden), f32), s((hidden, width), f32)]
    dma = pltpu.SemaphoreType.DMA
    return pl.pallas_call(
        finish_kernel,
        out_shape=shapes + [s((width,), f32)] * 9,
        in_specs=[any_] * 5,
        out_specs=[any_] * 13 + [vm] * 9,
        scratch_shapes=[pltpu.VMEM(back.reduced.shape, bf16), pltpu.VMEM((16, width), f32), pltpu.VMEM((8, rows, width), f32)]
            + [pltpu.VMEM(a.shape, a.dtype) for a in handed] + [dma((count,)), dma((8,)), dma((7,))],
        compiler_params=pltpu.CompilerParams(vmem_limit_bytes=62 << 20),
        name="finish",
    )(back.reduced, back.vector_grads, *handed)


def per_device(*args):
    rows, span, width = args[0].shape
    hidden = args[12].shape[1]
    fits = lax.axis_size("rows") == 8 and lax.axis_size("seq") == 4
    if not fits or (rows, span, width, hidden) != (2, 256, 512, 2048) or args[1].shape != args[0].shape:
        return ring_device(*args)
    matrices, vectors = args[4:14], args[14:23]
    kept = forward_call(args[0], args[1], args[2], args[3], matrices, vectors, args[23], HEADS)
    back = backward_call(kept, matrices, vectors, HEADS)
    return tuple(finish_call(back, hidden))


def solution(mesh):
    placed = (
        P("rows", "seq", None),
        P("rows", "seq", None),
        P("rows", None),
        P("rows", None),
        P(),
        P(),
        P(),
        P(),
        P(),
        P(),
        P(),
        P(),
        P(),
        P(),
        P(),
        P(),
        P(),
        P(),
        P(),
        P(),
        P(),
        P(),
        P(),
        P("rows", "seq", None),
    )
    return jax.shard_map(
        per_device,
        mesh=mesh,
        in_specs=placed,
        out_specs=(
            P("rows", "seq", None),
            P("rows", "seq", None),
            P("rows", "seq", None),
            P(),
            P(),
            P(),
            P(),
            P(),
            P(),
            P(),
            P(),
            P(),
            P(),
            P(),
            P(),
            P(),
            P(),
            P(),
            P(),
            P(),
            P(),
            P(),
        ),
        check_vma=False,
    )
```

```python
import functools
import math
from types import SimpleNamespace
from typing import NamedTuple

import jax
import jax.numpy as jnp
from jax import lax
from jax.experimental import pallas as pl
from jax.experimental.pallas import tpu as pltpu
from jax.sharding import PartitionSpec as P

HEADS = 8


masked_score = -1e30


def from_behind(block, axis, distance):
    devices = range(lax.axis_size(axis))
    route = [(i - distance, i) for i in devices if i - distance in devices]
    return lax.ppermute(block, axis, route)


def shifted(block, axis, distance):
    devices = range(lax.axis_size(axis))
    route = [((i - distance) % len(devices), i) for i in devices]
    return lax.ppermute(block, axis, route)


def layer_norm(pre_norm, gain, bias):
    centred = pre_norm - jnp.mean(pre_norm, axis=-1, keepdims=True)
    spread = jnp.mean(centred * centred, axis=-1, keepdims=True)
    return centred * lax.rsqrt(spread + 1e-05) * gain + bias


def residual_norm(previous, branch, omega, gain, bias):
    return layer_norm(previous * omega + branch, gain, bias)


def forward_product(inputs, weight):
    return jnp.dot(inputs, weight, preferred_element_type=jnp.float32)


def weight_product(inputs, grads):
    return jnp.einsum("rsd,rsf->df", inputs, grads, preferred_element_type=jnp.float32)


def input_product(grads, weight):
    return jnp.einsum("rsf,df->rsd", grads, weight, preferred_element_type=jnp.float32)


def split_heads(values, head_count):
    return values.reshape(values.shape[0], values.shape[1], head_count, -1)


def attend_update(running, query_low, key_low, value_low, allowed, score_scale, head_count):
    best, total, accum = running
    raw = (
        jnp.einsum(
            "rqhe,rkhe->rqhk",
            split_heads(query_low, head_count),
            split_heads(key_low, head_count),
            preferred_element_type=jnp.float32,
        )
        * score_scale
    )
    scores = jnp.where(allowed[:, :, None, :], raw, masked_score)
    new_best = jnp.maximum(best, jnp.max(scores, axis=-1))
    weights = jnp.where(allowed[:, :, None, :], jnp.exp(scores - new_best[..., None]), 0.0)
    factor = jnp.exp(best - new_best)
    total = total * factor + jnp.sum(weights, axis=-1)
    accum = accum * factor[..., None] + jnp.einsum(
        "rqhk,rkhe->rqhe",
        weights.astype(jnp.bfloat16),
        split_heads(value_low, head_count),
        preferred_element_type=jnp.float32,
    )
    return (new_best, total, accum)


def attend_grads(
    query_low, key_low, value_low, grad_low, logsum, row_delta, allowed, score_scale, head_count
):
    query_heads = split_heads(query_low, head_count)
    key_heads = split_heads(key_low, head_count)
    value_heads = split_heads(value_low, head_count)
    grad_heads = split_heads(grad_low, head_count)
    raw = (
        jnp.einsum("rqhe,rkhe->rqhk", query_heads, key_heads, preferred_element_type=jnp.float32)
        * score_scale
    )
    scores = jnp.where(allowed[:, :, None, :], raw, masked_score)
    attention_weights = jnp.exp(scores - logsum[..., None])
    value_grad = jnp.einsum(
        "rqhk,rqhe->rkhe",
        attention_weights.astype(jnp.bfloat16),
        grad_heads,
        preferred_element_type=jnp.float32,
    )
    weight_grad = jnp.einsum(
        "rqhe,rkhe->rqhk", grad_heads, value_heads, preferred_element_type=jnp.float32
    )
    score_grad = (attention_weights * (weight_grad - row_delta[..., None])).astype(jnp.bfloat16)
    query_grad = (
        jnp.einsum("rqhk,rkhe->rqhe", score_grad, key_heads, preferred_element_type=jnp.float32)
        * score_scale
    )
    key_grad = (
        jnp.einsum("rqhk,rqhe->rkhe", score_grad, query_heads, preferred_element_type=jnp.float32)
        * score_scale
    )
    query_shape = (query_low.shape[0], query_low.shape[1], query_low.shape[2])
    key_shape = (key_low.shape[0], key_low.shape[1], key_low.shape[2])
    return (
        query_grad.reshape(query_shape),
        key_grad.reshape(key_shape),
        value_grad.reshape(key_shape),
    )


def ring_device(
    target,
    memory,
    target_segments,
    memory_segments,
    self_query,
    self_key,
    self_value,
    self_output,
    cross_query,
    cross_key,
    cross_value,
    cross_output,
    ffn_in,
    ffn_out,
    omega_self,
    omega_cross,
    omega_ffn,
    gain_self,
    bias_self,
    gain_cross,
    bias_cross,
    gain_ffn,
    bias_ffn,
    cotangent,
):
    batch_rows, local_span, model_width = target.shape
    head_count = HEADS
    head_width = model_width // head_count
    score_scale = 1.0 / math.sqrt(head_width)
    self_index = lax.axis_index("seq")
    axis_size = lax.axis_size("seq")
    offsets = jnp.arange(local_span, dtype=jnp.int32)
    local_ids = lax.dynamic_slice_in_dim(target_segments, self_index * local_span, local_span, 1)

    def block_mask(query_source, key_source):
        query_ids = lax.dynamic_slice_in_dim(
            target_segments, query_source * local_span, local_span, 1
        )
        key_ids = lax.dynamic_slice_in_dim(target_segments, key_source * local_span, local_span, 1)
        query_place = query_source * local_span + offsets
        key_place = key_source * local_span + offsets
        matching = query_ids[:, :, None] == key_ids[:, None, :]
        return matching & (key_place[None, None, :] <= query_place[None, :, None])

    empty_state = (
        jnp.full((batch_rows, local_span, head_count), masked_score, jnp.float32),
        jnp.zeros((batch_rows, local_span, head_count), jnp.float32),
        jnp.zeros((batch_rows, local_span, head_count, head_width), jnp.float32),
    )
    self_triple = jnp.concatenate((self_query, self_key, self_value), axis=1)
    triple_low = forward_product(target, self_triple).astype(jnp.bfloat16)
    query_low = triple_low[..., :model_width]
    key_low = triple_low[..., model_width : 2 * model_width]
    value_low = triple_low[..., 2 * model_width :]
    running = attend_update(
        empty_state,
        query_low,
        key_low,
        value_low,
        block_mask(self_index, self_index),
        score_scale,
        head_count,
    )

    def forward_turn(step_index, carry):
        key_pair, running = carry
        key_pair = from_behind((key_pair[0], key_pair[1]), "seq", 1)
        source = (self_index - step_index + axis_size) % axis_size

        def forward_visit(inner):
            return attend_update(
                inner,
                query_low,
                key_pair[0],
                key_pair[1],
                block_mask(self_index, source),
                score_scale,
                head_count,
            )

        running = lax.cond(source <= self_index, forward_visit, lambda inner: inner, running)
        return (key_pair, running)

    key_pair, running = lax.fori_loop(1, axis_size, forward_turn, ((key_low, value_low), running))
    best, total, accum = running
    self_logsum = best + jnp.log(total)
    self_heads = accum / total[..., None]
    self_low = self_heads.reshape(batch_rows, local_span, model_width).astype(jnp.bfloat16)
    self_branch = forward_product(self_low, self_output)
    target_wide = target.astype(jnp.float32)
    hidden_one, pull_one = jax.vjp(
        residual_norm, target_wide, self_branch, omega_self, gain_self, bias_self
    )
    hidden_one_low = hidden_one.astype(jnp.bfloat16)
    cross_query_low = forward_product(hidden_one_low, cross_query).astype(jnp.bfloat16)
    cross_pair = jnp.concatenate((cross_key, cross_value), axis=1)
    memory_pairs = forward_product(
        lax.all_gather(memory, "seq", axis=1, tiled=True), cross_pair
    ).astype(jnp.bfloat16)
    memory_total = memory_pairs.shape[1]
    key_block = 1024
    block_count = memory_total // key_block

    def cross_mask(block_index):
        key_ids = lax.dynamic_slice_in_dim(memory_segments, block_index * key_block, key_block, 1)
        return local_ids[:, :, None] == key_ids[:, None, :]

    def block_pairs(block_index):
        return lax.dynamic_slice_in_dim(memory_pairs, block_index * key_block, key_block, 1)

    def cross_turn(block_index, running):
        pairs = block_pairs(block_index)
        return attend_update(
            running,
            cross_query_low,
            pairs[..., :model_width],
            pairs[..., model_width:],
            cross_mask(block_index),
            score_scale,
            head_count,
        )

    best, total, accum = lax.fori_loop(0, block_count, cross_turn, empty_state)
    cross_logsum = best + jnp.log(total)
    cross_heads = accum / total[..., None]
    cross_low = cross_heads.reshape(batch_rows, local_span, model_width).astype(jnp.bfloat16)
    cross_branch = forward_product(cross_low, cross_output)
    hidden_two, pull_two = jax.vjp(
        residual_norm, hidden_one, cross_branch, omega_cross, gain_cross, bias_cross
    )
    hidden_two_low = hidden_two.astype(jnp.bfloat16)
    upward = forward_product(hidden_two_low, ffn_in)
    activated, pull_gelu = jax.vjp(jax.nn.gelu, upward)
    active_low = activated.astype(jnp.bfloat16)
    ffn_branch = forward_product(active_low, ffn_out)
    result, pull_three = jax.vjp(
        residual_norm, hidden_two, ffn_branch, omega_ffn, gain_ffn, bias_ffn
    )
    two_grad, ffn_branch_grad, omega_ffn_grad, gain_ffn_grad, bias_ffn_grad = pull_three(
        cotangent.astype(jnp.float32)
    )
    ffn_branch_low = ffn_branch_grad.astype(jnp.bfloat16)
    ffn_out_grad = weight_product(active_low, ffn_branch_low)
    upward_grad = pull_gelu(input_product(ffn_branch_low, ffn_out))[0]
    upward_low = upward_grad.astype(jnp.bfloat16)
    ffn_in_grad = weight_product(hidden_two_low, upward_low)
    two_grad = two_grad + input_product(upward_low, ffn_in)
    one_grad, cross_branch_grad, omega_cross_grad, gain_cross_grad, bias_cross_grad = pull_two(
        two_grad
    )
    cross_branch_low = cross_branch_grad.astype(jnp.bfloat16)
    cross_output_grad = weight_product(cross_low, cross_branch_low)
    cross_heads_grad = input_product(cross_branch_low, cross_output).astype(jnp.bfloat16)
    cross_delta = jnp.sum(
        split_heads(cross_heads_grad, head_count).astype(jnp.float32) * cross_heads, axis=-1
    )

    def cross_back(block_index, carry):
        query_grad, pair_grads = carry
        pairs = block_pairs(block_index)
        grads = attend_grads(
            cross_query_low,
            pairs[..., :model_width],
            pairs[..., model_width:],
            cross_heads_grad,
            cross_logsum,
            cross_delta,
            cross_mask(block_index),
            score_scale,
            head_count,
        )
        block_grads = jnp.concatenate((grads[1], grads[2]), axis=2)
        pair_grads = lax.dynamic_update_slice_in_dim(
            pair_grads, block_grads, block_index * key_block, 1
        )
        return (query_grad + grads[0], pair_grads)

    zero_grid = jnp.zeros((batch_rows, local_span, model_width), jnp.float32)
    cross_query_sum, pair_grads = lax.fori_loop(
        0,
        block_count,
        cross_back,
        (zero_grid, jnp.zeros((batch_rows, memory_total, 2 * model_width), jnp.float32)),
    )
    local_pair_grads = lax.psum_scatter(
        pair_grads.astype(jnp.bfloat16), "seq", scatter_dimension=1, tiled=True
    )
    memory_grad = input_product(local_pair_grads, cross_pair)
    pair_weight_grad = weight_product(memory, local_pair_grads)
    cross_query_low_grad = cross_query_sum.astype(jnp.bfloat16)
    cross_query_grad = weight_product(hidden_one_low, cross_query_low_grad)
    one_grad = one_grad + input_product(cross_query_low_grad, cross_query)
    target_residual_grad, self_branch_grad, omega_self_grad, gain_self_grad, bias_self_grad = (
        pull_one(one_grad)
    )
    self_branch_low = self_branch_grad.astype(jnp.bfloat16)
    self_output_grad = weight_product(self_low, self_branch_low)
    self_heads_grad = input_product(self_branch_low, self_output).astype(jnp.bfloat16)
    self_delta = jnp.sum(
        split_heads(self_heads_grad, head_count).astype(jnp.float32) * self_heads, axis=-1
    )

    def key_turn(step_index, carry):
        key_pair, grad_pair, query_grad = carry
        source = (self_index - step_index + axis_size) % axis_size

        def key_visit(inner):
            grads = attend_grads(
                query_low,
                key_pair[0],
                key_pair[1],
                self_heads_grad,
                self_logsum,
                self_delta,
                block_mask(self_index, source),
                score_scale,
                head_count,
            )
            return (inner[0] + grads[0], inner[1] + grads[1], inner[2] + grads[2])

        query_grad, key_grad, value_grad = lax.cond(
            source <= self_index,
            key_visit,
            lambda inner: inner,
            (query_grad, grad_pair[0], grad_pair[1]),
        )
        grad_pair = (
            shifted(key_grad.astype(jnp.bfloat16), "seq", 1).astype(key_grad.dtype),
            shifted(value_grad.astype(jnp.bfloat16), "seq", 1).astype(value_grad.dtype),
        )
        key_pair = from_behind((key_pair[0], key_pair[1]), "seq", 1)
        return (key_pair, grad_pair, query_grad)

    key_pair, grad_pair, query_grad = lax.fori_loop(
        0, axis_size, key_turn, ((key_low, value_low), (zero_grid, zero_grid), zero_grid)
    )
    key_grad, value_grad = grad_pair
    triple_grad_low = jnp.concatenate((query_grad, key_grad, value_grad), axis=2).astype(
        jnp.bfloat16
    )
    target_grad = target_residual_grad + input_product(triple_grad_low, self_triple)
    triple_weight_grad = weight_product(target, triple_grad_low)
    sums = lax.psum(
        (
            triple_weight_grad[:, :model_width],
            triple_weight_grad[:, model_width : 2 * model_width],
            triple_weight_grad[:, 2 * model_width :],
            self_output_grad,
            cross_query_grad,
            pair_weight_grad[:, :model_width],
            pair_weight_grad[:, model_width:],
            cross_output_grad,
            ffn_in_grad,
            ffn_out_grad,
            omega_self_grad,
            omega_cross_grad,
            omega_ffn_grad,
            gain_self_grad,
            bias_self_grad,
            gain_cross_grad,
            bias_cross_grad,
            gain_ffn_grad,
            bias_ffn_grad,
        ),
        ("rows", "seq"),
    )
    return (result.astype(jnp.bfloat16), target_grad, memory_grad) + tuple(sums)


MESH = pl.DeviceIdType.MESH
f32, bf16 = jnp.float32, jnp.bfloat16

def dot(a, b):
    return jnp.dot(a, b, preferred_element_type=f32)

def dot_t(a, b):
    return lax.dot_general(a, b, (((1,), (1,)), ((), ())), preferred_element_type=f32)

def t_dot(a, b):
    return lax.dot_general(a, b, (((0,), (0,)), ((), ())), preferred_element_type=f32)

def mult(i, m):
    return i if isinstance(i, int) else pl.multiple_of(i, m)

def attend_forward(first_block, blocks, keys, key, value_t, query_z, seen, scores, kept, kept_out, kept_sem, out_t, inverse, heads):
    count, piece, slots, queries = blocks * heads, 256, kept.shape[0], seen.shape[2]

    def head_place(i):
        block, head = first_block + i // heads, i % heads
        return block, head, pl.ds(mult(head * 64, 64), 64), pl.ds(mult(head // 2 * 128, 128), 128)

    def first(i, slot):
        block, head, _, pair = head_place(i)
        best = None
        for c in range(keys // piece):
            ks = pl.ds(c * piece, piece)
            s = dot(key[ks, pair], query_z[block, head]) + seen[block, ks]
            scores[slot, ks] = s
            top = jnp.max(s.reshape(piece // 8, 8, queries), axis=0)
            best = top if best is None else jnp.maximum(best, top)
        return best

    def out_copy(i):
        block, head, _, _ = head_place(i)
        return pltpu.make_async_copy(kept.at[i % slots, pl.ds(0, keys)], kept_out.at[block, head, pl.ds(0, keys)], kept_sem.at[i % slots])

    def second(i, slot, best):
        block, head, here, _ = head_place(i)
        best = jnp.max(best, axis=0, keepdims=True)
        total = out = None
        for c in range(keys // piece):
            ks = pl.ds(c * piece, piece)
            p = jnp.exp(scores[slot, ks] - best)
            part = jnp.sum(p.reshape(piece // 8, 8, queries), axis=0)
            total = part if total is None else total + part
            p = p.astype(bf16)
            kept[i % slots, ks] = p
            part = dot(value_t[here, ks], p)
            out = part if out is None else out + part
        scale = 1.0 / jnp.sum(total, axis=0, keepdims=True)
        out_t[block, here, :] = (out * scale).astype(bf16)
        inverse[block, head] = jnp.broadcast_to(scale, (8, queries))

    def body(j, best):
        i = 2 * j
        for e in range(2):
            pl.when(i + e >= slots)(lambda e=e: out_copy(i + e - slots).wait())
        later = first(i + 1, 1)
        second(i, 0, best)
        best = first(jnp.minimum(i + 2, count - 1), 0)
        second(i + 1, 1, later)
        out_copy(i).start()
        out_copy(i + 1).start()
        return best

    lax.fori_loop(0, count // 2, body, first(0, 0))
    for i in range(count - slots, count):
        out_copy(i).wait()

def norm_parts(pre):
    centred = pre - jnp.mean(pre, axis=-1, keepdims=True)
    rstd = lax.rsqrt(jnp.mean(centred * centred, axis=-1, keepdims=True) + 1e-05)
    return centred * rstd, rstd

def pad_pairs(query, query_z, row, heads):
    turned = query.T
    half = lax.broadcasted_iota(jnp.int32, (128, query.shape[0]), 0) // 64
    for head in range(heads):
        pair = turned[head // 2 * 128 : head // 2 * 128 + 128]
        query_z[row, head] = jnp.where(half == head % 2, pair, jnp.zeros_like(pair))

class ForwardIn(NamedTuple):
    target: object
    memory: object
    target_segments: object
    memory_segments: object
    self_query: object
    self_key: object
    self_value: object
    self_output: object
    cross_query: object
    cross_key: object
    cross_value: object
    cross_output: object
    ffn_in: object
    ffn_out: object
    omega_self: object
    omega_cross: object
    omega_ffn: object
    gain_self: object
    bias_self: object
    gain_cross: object
    bias_cross: object
    gain_ffn: object
    bias_ffn: object
    cotangent: object

class ForwardOut(NamedTuple):
    output_blocks: object
    target_all: object
    memory_all: object
    self_kept: object
    cross_kept: object
    self_inverse: object
    cross_inverse: object
    self_out: object
    cross_out: object
    self_q: object
    cross_q: object
    one_low: object
    one_hat: object
    one_rstd: object
    two_low: object
    two_hat: object
    two_rstd: object
    active: object
    upward_slope: object
    branch_grad: object
    two_grad: object
    sums: object

class ForwardScratch(NamedTuple):
    key: object
    value_t: object
    query_z: object
    seen_self: object
    seen_cross: object
    scores: object
    kept: object
    mem_key: object
    mem_value_t: object
    wide: object
    one: object
    two: object
    value_turned: object
    mem_value_turned: object
    grads: object
    up: object

FORWARD_NAMES = ForwardIn._fields + ForwardOut._fields
MATRICES = ForwardIn._fields[4:14]
VECTORS = ForwardIn._fields[14:23]

def forward_kernel(heads, *refs):
    hbm = SimpleNamespace(**dict(zip(FORWARD_NAMES, refs)))
    own = refs[len(FORWARD_NAMES):-5]
    r = SimpleNamespace(**dict(zip(FORWARD_NAMES[2:4] + VECTORS + MATRICES + ForwardOut._fields + ForwardScratch._fields,
        refs[2:4] + refs[14:23] + own)))
    send, recv, local, load_sem, out_sem = refs[-5:]
    kept_sem = local
    me_r, me_s = lax.axis_index("rows"), lax.axis_index("seq")
    core, side = me_s % 2, me_s // 2
    length, width = r.target_all.shape
    tokens = r.one_low.shape[0]
    blocks = 2
    span = tokens // blocks
    other_core, other_side = me_s + 1 - 2 * core, me_s + 2 - 4 * side

    def place(i):
        return pl.ds(mult(i * span, span), span)

    def remote(src, dst, k, to):
        return pltpu.make_async_remote_copy(src_ref=src, dst_ref=dst, send_sem=send.at[k], recv_sem=recv.at[k],
            device_id=(me_r, to), device_id_type=MESH)

    def share(source, full, k):
        mine, theirs = full.at[place(me_s)], full.at[place(other_side)]
        return (pltpu.make_async_copy(source.at[side], mine, load_sem.at[10 + k // 3]), remote(source.at[1 - side], mine, k, other_side),
            remote(source.at[side], mine, k + 1, other_core), remote(theirs, theirs, k + 2, other_core))

    x_own, x_side, x_core, x_pass = share(hbm.target, r.target_all, 0)
    m_own, m_side, m_core, m_pass = share(hbm.memory, r.memory_all, 3)
    g_own = pltpu.make_async_copy(hbm.cotangent.at[side], r.grads.at[side], load_sem.at[12])
    g_side = remote(hbm.cotangent.at[1 - side], r.grads.at[side], 6, other_side)
    x_own.start()
    m_own.start()
    loads = {k: pltpu.make_async_copy(getattr(hbm, k), getattr(r, k), load_sem.at[i]) for i, k in enumerate(MATRICES)}
    for copy in loads.values():
        copy.start()
    g_own.start()
    loads = SimpleNamespace(**loads)
    outs = []

    def emit(*names):
        for k in names:
            copy = pltpu.make_async_copy(getattr(r, k), getattr(hbm, k), out_sem.at[len(outs)])
            copy.start()
            outs.append(copy)

    barrier = pltpu.get_barrier_semaphore()
    for to in (other_core, other_side):
        pl.semaphore_signal(barrier, inc=1, device_id=(me_r, to), device_id_type=MESH)
    pl.semaphore_wait(barrier, 2)
    x_side.start()
    x_core.start()
    m_core.start()

    def masks():
        def line(ids, at):
            first, second = ids[0:1, at], ids[1:2, at]
            return (first + (second - first) * side).astype(f32)
        mine = [line(r.target_segments, pl.ds(mult((2 * b + core) * span, span), span)) for b in range(blocks)]
        for c in range(length // 128):
            at = pl.ds(c * 128, 128)
            key_place = c * 128 + lax.broadcasted_iota(jnp.int32, (128, span), 0)
            query_place = lax.broadcasted_iota(jnp.int32, (128, span), 1)
            for ids, seen, causal in ((r.target_segments, r.seen_self, True), (r.memory_segments, r.seen_cross, False)):
                column = jnp.broadcast_to(line(ids, at), (128, 128)).T
                column = jnp.concatenate([column] * (span // 128), axis=1)
                for b in range(blocks):
                    if causal and c * 128 >= (b + 1) * length // 2:
                        continue
                    same = column == mine[b]
                    if causal:
                        same = same & (key_place <= query_place + (2 * b + core) * span)
                    seen[b, at] = jnp.where(same, 0.0, -1e30)

    def project(full, key_weight, turned, key, value_t, block):
        at = place(block)
        here = full[at]
        key[at] = dot(here, key_weight[...]).astype(bf16)
        value_t[:, at] = dot_t(turned[...], here).astype(bf16)

    def project_self(block):
        project(r.target_all, r.self_key, r.value_turned, r.key, r.value_t, block)

    def project_cross(block):
        project(r.memory_all, r.cross_key, r.mem_value_turned, r.mem_key, r.mem_value_t, block)

    def queries(low, weight, out):
        for b in range(blocks):
            query = (dot(low(b), weight[...]).astype(bf16) * 0.125).astype(bf16)
            out[b] = query
            pad_pairs(query, r.query_z, b, heads)

    masks()
    for k in (loads.self_query, loads.self_key, loads.self_value, loads.cross_key, loads.cross_value):
        k.wait()
    r.value_turned[...] = r.self_value[...].T
    r.mem_value_turned[...] = r.cross_value[...].T
    x_own.wait()
    project_self(me_s)
    x_core.wait()
    project_self(other_core)
    m_own.wait()
    project_cross(me_s)
    m_core.wait()
    project_cross(other_core)
    x_side.wait()
    x_pass.start()
    m_side.start()
    queries(lambda b: r.target_all[place(2 * b + core)], r.self_query, r.self_q)
    project_self(other_side)
    x_pass.wait()
    project_self(other_side + 1 - 2 * core)
    emit(*ForwardOut._fields[1:2], *ForwardOut._fields[9:10])

    def attend(first_block, count, keys, key, value_t, seen, kept_out, out_t, inverse):
        attend_forward(first_block, count, keys, key, value_t, r.query_z, seen, r.scores, r.kept, kept_out, kept_sem, out_t, inverse, heads)

    attend(0, 1, length // 2, r.key, r.value_t, r.seen_self, hbm.self_kept, r.self_out, r.self_inverse)
    attend(1, 1, length, r.key, r.value_t, r.seen_self, hbm.self_kept, r.self_out, r.self_inverse)
    m_side.wait()
    m_pass.start()
    g_side.start()
    loads.self_output.wait()
    vec = [getattr(r, k)[...].reshape(1, width) for k in VECTORS]
    part = 128
    for b in range(blocks):
        r.wide[pl.ds(b * span, span)] = t_dot(r.self_out[b], r.self_output[...])

    @pl.loop(0, tokens // part)
    def _(i):
        at = pl.ds(mult(i * part, part), part)
        b, inner = i // (span // part), i % (span // part)
        x = r.target_all[pl.ds(mult((2 * b + core) * span + inner * part, part), part)].astype(f32)
        hat, rstd = norm_parts(x * vec[0] + r.wide[at])
        one = hat * vec[3] + vec[4]
        r.one_hat[at] = hat
        r.one_rstd[at] = jnp.broadcast_to(rstd, (part, 128))
        r.one[at] = one
        r.one_low[at] = one.astype(bf16)

    loads.cross_query.wait()
    queries(lambda b: r.one_low[pl.ds(b * span, span)], r.cross_query, r.cross_q)
    project_cross(other_side)
    m_pass.wait()
    project_cross(other_side + 1 - 2 * core)
    emit(*ForwardOut._fields[2:3], *ForwardOut._fields[5:6], *ForwardOut._fields[7:8], *ForwardOut._fields[10:14])
    attend(0, 2, length, r.mem_key, r.mem_value_t, r.seen_cross, hbm.cross_kept, r.cross_out, r.cross_inverse)
    loads.cross_output.wait()
    for b in range(blocks):
        r.wide[pl.ds(b * span, span)] = t_dot(r.cross_out[b], r.cross_output[...])

    @pl.loop(0, tokens // part)
    def _(i):
        at = pl.ds(mult(i * part, part), part)
        hat, rstd = norm_parts(r.one[at] * vec[1] + r.wide[at])
        two = hat * vec[5] + vec[6]
        r.two_hat[at] = hat
        r.two_rstd[at] = jnp.broadcast_to(rstd, (part, 128))
        r.two[at] = two
        r.two_low[at] = two.astype(bf16)

    emit(*ForwardOut._fields[6:7], *ForwardOut._fields[8:9], *ForwardOut._fields[14:17])
    loads.ffn_in.wait()
    loads.ffn_out.wait()
    c0 = math.sqrt(2.0 / math.pi)
    pieces = r.ffn_in.shape[1] // 512
    r.wide[...] = jnp.zeros_like(r.wide)

    halves = [pl.ds(half * (tokens // 2), tokens // 2) for half in range(2)]

    def up(j, half):
        r.up[half] = dot(r.two_low[halves[half]], r.ffn_in[:, pl.ds(mult(j * 512, 512), 512)])

    def down(j, half):
        at, cols = halves[half], pl.ds(mult(j * 512, 512), 512)
        u = r.up[half]
        square = u * u
        t = jnp.tanh(u * (c0 + (c0 * 0.044715) * square))
        rise = 0.5 + 0.5 * t
        active = (u * rise).astype(bf16)
        r.active[at, cols] = active
        r.upward_slope[at, cols] = (rise + u * (rise * (1.0 - t)) * (c0 + (3 * 0.044715 * c0) * square)).astype(bf16)
        r.wide[at] += dot(active, r.ffn_out[cols, :])

    up(0, 0)

    @pl.loop(0, pieces)
    def _(j):
        up(j, 1)
        down(j, 0)
        up(jnp.minimum(j + 1, pieces - 1), 0)
        down(j, 1)

    emit(*ForwardOut._fields[17:19])
    g_own.wait()
    g_side.wait()
    r.sums[...] = jnp.zeros_like(r.sums)

    @pl.loop(0, tokens // part)
    def _(i):
        at = pl.ds(mult(i * part, part), part)
        b, inner = i // (span // part), i % (span // part)
        near = pl.ds(mult(inner * part, part), part)
        two = r.two[at]
        hat, rstd = norm_parts(two * vec[2] + r.wide[at])
        r.output_blocks[b, near] = (hat * vec[7] + vec[8]).astype(bf16)
        grad = r.grads[b, near].astype(f32)
        scaled = grad * vec[7]
        back = rstd * (scaled - jnp.mean(scaled, axis=-1, keepdims=True) - hat * jnp.mean(scaled * hat, axis=-1, keepdims=True))
        r.branch_grad[at] = back.astype(bf16)
        r.two_grad[at] = back * vec[2]
        r.sums[0] += jnp.sum((back * two).reshape(part // 8, 8, width), axis=0)
        r.sums[1] += jnp.sum((grad * hat).reshape(part // 8, 8, width), axis=0)
        r.sums[2] += jnp.sum(grad.reshape(part // 8, 8, width), axis=0)

    emit(*ForwardOut._fields[:1], *ForwardOut._fields[19:])

    for copy in outs:
        copy.wait()

def forward_call(target, memory, target_segments, memory_segments, matrices, vectors, cotangent, heads=8):
    blocks, span, width = target.shape
    length = target_segments.shape[1]
    tokens = blocks * span
    hidden = matrices[8].shape[1]
    any_, vm = pl.BlockSpec(memory_space=pl.ANY), pl.BlockSpec(memory_space=pltpu.VMEM)
    s = jax.ShapeDtypeStruct
    full, wide, seen = ((length, width), bf16), ((tokens, width), f32), ((blocks, length, span), f32)
    kept, inverse = s((blocks, heads, length, span), bf16), s((blocks, heads, 8, span), f32)
    outs = ForwardOut(output_blocks=s((blocks, span, width), bf16), target_all=s(*full), memory_all=s(*full),
        self_kept=kept, cross_kept=kept, self_inverse=inverse, cross_inverse=inverse,
        self_out=s((blocks, width, span), bf16), cross_out=s((blocks, width, span), bf16),
        self_q=s((blocks, span, width), bf16), cross_q=s((blocks, span, width), bf16),
        one_low=s((tokens, width), bf16), one_hat=s(*wide), one_rstd=s((tokens, 128), f32),
        two_low=s((tokens, width), bf16), two_hat=s(*wide), two_rstd=s((tokens, 128), f32),
        active=s((tokens, hidden), bf16), upward_slope=s((tokens, hidden), bf16), branch_grad=s((tokens, width), bf16),
        two_grad=s(*wide), sums=s((3, 8, width), f32))
    turned = ((width, length), bf16)
    scratch = ForwardScratch(key=full, value_t=turned, query_z=((blocks, heads, 128, span), bf16),
        seen_self=seen, seen_cross=seen, scores=((2, length, span), f32),
        kept=((4, length, span), bf16), mem_key=full, mem_value_t=turned,
        wide=wide, one=wide, two=wide,
        value_turned=((width, width), bf16), mem_value_turned=((width, width), bf16), grads=((blocks, span, width), bf16), up=((2, tokens // 2, 512), f32))
    held = [((8, 128), f32) if k in ForwardOut._fields[3:5] else (o.shape, o.dtype) for k, o in zip(ForwardOut._fields, outs)]
    held = [(m.shape, m.dtype) for m in matrices] + held + list(scratch)
    dma = pltpu.SemaphoreType.DMA
    return ForwardOut(*pl.pallas_call(
        functools.partial(forward_kernel, heads),
        out_shape=list(outs),
        in_specs=[any_] * 2 + [vm] * 2 + [any_] * 10 + [vm] * 9 + [any_],
        out_specs=[any_] * len(outs),
        scratch_shapes=[pltpu.VMEM(*k) for k in held] + [dma((7,)), dma((7,)), dma((4,)), dma((13,)), dma((20,))],
        compiler_params=pltpu.CompilerParams(collective_id=0, has_side_effects=True, vmem_limit_bytes=62 << 20),
        name="forward",
    )(target, memory, target_segments, memory_segments, *matrices, *vectors, cotangent))

CLASSES = (0, 4, 0, 1, 1, 1, 0, 0, 2, 4, 1, 4, 1, 1, 4, 1)
PLAN = (
    (0,),
    (19, 1),
    (2,),
    (3,),
    (1, 0, 2, 4),
    (3, 5),
    (6,),
    (7,),
    (4, 5),
    (19, 1, 7, 6),
    (8,),
    (),
    (),
    (3, 1, 0, 8),
    (2, 4),
    (),
    (1, 7, 5),
    (9, 0),
    (10, 8),
    (11, 2),
    (16, 1, 6, 9, 3, 7, 10, 0),
    (11,),
    (18, 1, 4),
    (12, 2),
    (16, 3, 6, 5, 8),
    (18, 7, 0),
    (12, 1, 9, 10, 2, 4),
    (3, 6),
    (7, 0, 11, 5, 8),
    (),
    (1, 13, 10),
    (14, 16),
    (15, 18, 9, 2),
    (17, 3, 13, 7, 6, 14, 4),
    (15, 12, 0, 8, 1, 18, 11, 5, 17, 10, 1, 9, 13, 2, 14, 3, 7, 12, 6, 4, 15, 18, 13, 11, 0, 5, 8, 10, 3, 15, 14, 12, 6, 4, 0, 18, 8, 17, 13, 9, 5, 10, 0, 2, 4, 15, 14, 7, 12, 11, 5, 8, 13, 10, 3, 15, 12, 2, 6, 9, 3, 2, 7, 8, 13, 15, 4, 14, 10, 12, 11, 9, 7, 8, 13, 4, 15, 6, 5, 14, 11, 12, 9, 6, 13, 5, 10, 14, 15, 11, 10, 12, 9, 14, 12, 13, 9, 11, 13, 15, 11, 14, 15, 14),
)

class Reduction:
    def __init__(self, block, near, landed, reduced, send, recv, own):
        self.block, self.near, self.landed, self.reduced = block, near, landed, reduced
        self.send, self.recv, self.own = send, recv, own
        self.r, self.s = lax.axis_index("rows"), lax.axis_index("seq")
        self.core, self.y = self.s % 2, self.s // 2
        self.x, self.z0, self.z1 = self.r % 2, (self.r // 2) % 2, self.r // 4
        self.count, self.size = block.shape[0], block.shape[1]
        x, y, z0, z1 = self.x, self.y, self.z0, self.z1
        core, ax, ay = (0, 1 - 2 * self.core, self.core), (1 - 2 * x, 0, x), (0, 2 - 4 * y, y)
        an, af = (2 - 4 * z0, 0, z0), (4 - 8 * z1, 0, z1)
        self.orders = ((core, ax, ay, an, af), (core, ay, ax, an, af), (core, an, af, ax, ay), (core, an, af, ay, ax), (core, ax, an, af, ay), (core, ay, an, af, ax))
        self.flows, self.turn, done = {}, 0, {}
        self.polls = []
        for entry in PLAN:
            self.polls.append([(c, done.setdefault(c, []).append(0) or len(done[c]) - 1) for c in entry])

    def partners(self):
        r, s = self.r, self.s
        return ((r, s + 1 - 2 * self.core), (r, s + 2 - 4 * self.y), (r + 1 - 2 * self.x, s),
                (r + 2 - 4 * self.z0, s), (r + 4 - 8 * self.z1, s))

    def start_of(self, j, hops):
        off = 0
        for i in range(j):
            off = off + hops[i][2] * (self.size >> (i + 1))
        return off

    def landing(self, c, j):
        half = self.size >> (j + 1)
        if j == 0:
            return self.near.at[c]
        return self.landed.at[c, pl.ds(self.size // 2 - (self.size >> j), half)]

    def copy(self, c, j, gather):
        hops = self.orders[CLASSES[c]]
        off, half = self.start_of(j, hops), self.size >> (j + 1)
        dr, ds, bit = hops[j]
        if gather:
            mine = pl.ds(pl.multiple_of(off + bit * half, 16), half)
            src, dst = (self.block if j == 4 else self.reduced).at[c, mine], self.reduced.at[c, mine]
        else:
            src, dst = self.block.at[c, pl.ds(pl.multiple_of(off + (1 - bit) * half, 16), half)], self.landing(c, j)
        return pltpu.make_async_remote_copy(src_ref=src, dst_ref=dst, send_sem=self.send.at[c],
            recv_sem=self.recv.at[c, j + 5 * gather], device_id=(self.r + dr, self.s + ds), device_id_type=MESH)

    def own_copy(self, c):
        mine = pl.ds(pl.multiple_of(self.start_of(5, self.orders[CLASSES[c]]), 16), self.size >> 5)
        return pltpu.make_async_copy(self.block.at[c, mine], self.reduced.at[c, mine], self.own.at[c])

    def add(self, c, j):
        keep = pl.ds(pl.multiple_of(self.start_of(j + 1, self.orders[CLASSES[c]]), 16), self.size >> (j + 1))
        self.block[c, keep] = (self.block[c, keep].astype(f32) + self.landing(c, j)[...].astype(f32)).astype(bf16)

    def step(self, c, s):
        if c >= self.count:
            return self.flows[c](s)
        if 1 <= s <= 5:
            self.copy(c, s - 1, 0).wait()
            self.add(c, s - 1)
        elif s > 5:
            self.copy(c, 10 - s, 1).wait()
        if s == 5:
            self.own_copy(c).start()
        elif s == 6:
            self.own_copy(c).wait()
        if s <= 4:
            self.copy(c, s, 0).start()
        elif s <= 9:
            self.copy(c, 9 - s, 1).start()

    def poll(self, index=None):
        if index is None:
            index = self.turn
            self.turn += 1
        for c, s in self.polls[index]:
            self.step(c, s)

    def poll_loop(self, base, count, i):
        for k in range(count):
            if self.polls[base + k]:
                @pl.when(i == k)
                def _():
                    self.poll(base + k)

class Loads(NamedTuple):
    active: object
    branch_grad: object
    two_low: object
    upward_slope: object
    ffn_out: object
    ffn_in: object
    two_grad: object
    two_hat: object
    two_rstd: object
    one_hat: object
    one_rstd: object
    cross_output: object
    cross_out: object
    cross_inverse: object
    memory_all: object
    cross_key: object
    cross_value: object
    cross_q: object
    one_low: object
    cross_query: object
    target_all: object
    self_output: object
    self_out: object
    self_inverse: object
    self_key: object
    self_value: object
    self_q: object
    self_query: object
    sums: object

class BackOut(NamedTuple):
    output: object
    reduced: object
    target_grad: object
    memory_grad: object
    vector_grads: object

class BackScratch(NamedTuple):
    block: object
    near: object
    landed: object
    key_t: object
    value: object
    key_grad: object
    value_grad: object
    score_grad: object
    kept: object
    part: object
    part_core: object
    part_side: object
    query_grad_t: object
    query_grad: object
    branch_low: object
    out_grad_t: object
    out_grad: object
    delta: object
    vec: object
    vec_landed: object
    acc: object
    output_own: object

LOADS = Loads._fields
UNLOADED = ForwardOut._fields[3:5] + ForwardOut._fields[:1] + VECTORS

def backward_kernel(heads, *refs):
    n = len(LOADS + UNLOADED)
    hbm = SimpleNamespace(**dict(zip(LOADS + UNLOADED, refs)))
    r = SimpleNamespace(**dict(zip(BackOut._fields + LOADS + BackScratch._fields, refs[n:])))
    load_sem, kept_sem, send, recv, own_sem, part_send, part_recv, vec_send, vec_recv, out_sem = refs[-10:]
    length, width = r.memory_all.shape
    tokens = r.two_low.shape[0]
    blocks = 2
    span = tokens // blocks
    red = Reduction(r.block, r.near, r.landed, r.reduced, send, recv, own_sem)
    me_r, me_s, core, side = red.r, red.s, red.core, red.y

    loads = Loads(*[pltpu.make_async_copy(getattr(hbm, k), getattr(r, k), load_sem.at[i]) for i, k in enumerate(LOADS)])
    for copy in loads:
        copy.start()

    def need(*copies):
        for copy in copies:
            copy.wait()

    barrier = pltpu.get_barrier_semaphore()
    for to in red.partners():
        pl.semaphore_signal(barrier, inc=1, device_id=to, device_id_type=MESH)

    def block_at(b):
        return pl.ds(b * span, span)

    def place(i):
        return pl.ds(mult(i * span, span), span)

    def ffn_block(c):
        if c < 4:
            r.block[c] = t_dot(r.active[:, pl.ds(c * 512, 512)], r.branch_grad[...]).astype(bf16)
        else:
            r.block[c] = t_dot(r.two_low[...], r.upward_slope[:, pl.ds((c - 4) * 512, 512)]).astype(bf16)

    def upward_gradient():
        @pl.loop(0, r.upward_slope.shape[1] // 512)
        def _(j):
            cols = pl.ds(mult(j * 512, 512), 512)
            for b in range(blocks):
                grad = dot_t(r.branch_grad[block_at(b)], r.ffn_out[cols, :])
                r.upward_slope[block_at(b), cols] = (grad * r.upward_slope[block_at(b), cols].astype(f32)).astype(bf16)

    vec = [getattr(hbm, k)[...].reshape(1, width) for k in VECTORS]
    part = 128

    def norm_back(grad_ref, hat_ref, rstd_ref, gain, omega, previous, slot):
        for i in range(3):
            r.acc[slot + i] = jnp.zeros_like(r.acc[slot + i])

        @pl.loop(0, tokens // part)
        def _(i):
            at = pl.ds(mult(i * part, part), part)
            hat, grad = hat_ref[at], grad_ref[at]
            scaled = grad * gain
            back = rstd_ref[at][:, 0:1] * (scaled - jnp.mean(scaled, axis=-1, keepdims=True)
                - hat * jnp.mean(scaled * hat, axis=-1, keepdims=True))
            r.branch_low[at] = back.astype(bf16)
            grad_ref[at] = back * omega
            for k, term in enumerate((back * previous(i), grad * hat, grad)):
                r.acc[slot + k] += jnp.sum(term.reshape(part // 8, 8, width), axis=0)

    def attention_start(weight, out_t, inverse):
        for b in range(blocks):
            grad_t = dot_t(weight[...], r.branch_low[block_at(b)])
            for head in range(heads):
                here = pl.ds(head * 64, 64)
                scaled = grad_t[head * 64 : head * 64 + 64] * inverse[b, head][0:1]
                r.out_grad_t[b, here] = scaled.astype(bf16)
                delta = jnp.sum(scaled * out_t[b, here].astype(f32), axis=0, keepdims=True)
                r.delta[b, head] = jnp.broadcast_to(delta, (8, span))
            r.out_grad[b] = r.out_grad_t[b].T

    def keys_again(full, key_weight, value_weight):
        key_turned = key_weight[...].T
        for c in range(length // 512):
            at = pl.ds(c * 512, 512)
            here = full[at]
            r.key_t[:, at] = dot_t(key_turned, here).astype(bf16)
            r.value[at] = dot(here, value_weight[...]).astype(bf16)

    def attention_back(kept_hbm, query, spans):
        base = red.turn
        pairs, piece = heads // 2, 256
        red.turn += pairs
        tiles = [(b, e) for b in range(blocks) for e in range(2)]
        top = lax.broadcasted_iota(jnp.int32, (128, span), 0) // 64
        left = lax.broadcasted_iota(jnp.int32, (span, 128), 1) // 64

        def pair_at(j):
            return pl.ds(mult(j * 128, 128), 128)

        def fetch(j, b, e):
            slot, ks = j % 3 * 4 + b * 2 + e, pl.ds(0, spans[b])
            return pltpu.make_async_copy(kept_hbm.at[b, 2 * j + e, ks], r.kept.at[slot, ks], kept_sem.at[slot])

        def first(j):
            for b, e in tiles:
                fetch(j, b, e).wait()
            for b, e in tiles:
                grad = jnp.where(top == e, r.out_grad_t[b, pair_at(j), :], jnp.zeros((128, span), bf16))
                delta = r.delta[b, 2 * j + e][0:1]
                for c in range(spans[b] // piece):
                    ks = pl.ds(c * piece, piece)
                    p_grad = dot(r.value[ks, pair_at(j)], grad)
                    r.score_grad[j % 2 * 4 + b * 2 + e, ks] = (r.kept[j % 3 * 4 + b * 2 + e, ks].astype(f32) * (p_grad - delta)).astype(bf16)

        def second(j):
            none = jnp.zeros((span, 128), bf16)
            qs = [jnp.where(left == e, query[b, :, pair_at(j)], none) for b, e in tiles]
            gs = [jnp.where(left == e, r.out_grad[b, :, pair_at(j)], none) for b, e in tiles]
            out = [None] * len(tiles)
            for c in range(length // piece):
                ks = pl.ds(c * piece, piece)
                v_grad = k_grad = None
                for i, (b, e) in enumerate(tiles):
                    if c * piece >= spans[b]:
                        continue
                    ds = r.score_grad[j % 2 * 4 + i, ks]
                    v, k = dot(r.kept[j % 3 * 4 + i, ks], gs[i]), dot(ds, qs[i])
                    v_grad, k_grad = (v, k) if v_grad is None else (v_grad + v, k_grad + k)
                    a = dot(r.key_t[pl.ds(mult(j * 128 + e * 64, 64), 64), ks], ds)
                    out[i] = a if out[i] is None else out[i] + a
                r.value_grad[ks, pair_at(j)] = v_grad.astype(bf16)
                r.key_grad[ks, pair_at(j)] = k_grad.astype(bf16)
            for i, (b, e) in enumerate(tiles):
                r.query_grad_t[b, pl.ds(mult(j * 128 + e * 64, 64), 64), :] = (out[i] * 0.125).astype(bf16)

        for j in range(2):
            for b, e in tiles:
                fetch(j, b, e).start()
        first(0)

        @pl.loop(0, pairs - 1)
        def _(j):
            @pl.when(j + 2 < pairs)
            def _():
                for b, e in tiles:
                    fetch(j + 2, b, e).start()
            first(j + 1)
            second(j)
            red.poll_loop(base, pairs - 1, j)
        second(pairs - 1)
        red.poll(base + pairs - 1)
        for b in range(blocks):
            r.query_grad[b] = r.query_grad_t[b].T

    def pair_product(key_weight, value_weight):
        for i in range(length // span):
            at = block_at(i)
            r.part[i] = (dot_t(r.key_grad[at], key_weight[...]) + dot_t(r.value_grad[at], value_weight[...])).astype(bf16)

    def part_copy(k, src, dst, to):
        return pltpu.make_async_remote_copy(src_ref=src, dst_ref=dst, send_sem=part_send.at[k], recv_sem=part_recv.at[k],
            device_id=(me_r, to), device_id_type=MESH)

    def part_flow(turn, out, rest):
        to_core, to_side = me_s + 1 - 2 * core, me_s + 2 - 4 * side
        far, near = 1 - side, side
        copies = (part_copy(3 * turn, r.part.at[2 * far + 1 - core], r.part_core.at[turn, 0], to_core),
            part_copy(3 * turn + 1, r.part.at[2 * near + 1 - core], r.part_core.at[turn, 1], to_core),
            part_copy(3 * turn + 2, r.part_core.at[turn, 0], r.part_side.at[turn], to_side))

        def step(s):
            if s == 0:
                copies[0].start()
                copies[1].start()
            elif s == 1:
                copies[0].wait()
                r.part_core[turn, 0] = (r.part[2 * far + core].astype(f32) + r.part_core[turn, 0].astype(f32) + rest(far)).astype(bf16)
                copies[2].start()
                copies[1].wait()
                out[near] = r.part[2 * near + core].astype(f32) + r.part_core[turn, 1].astype(f32) + rest(near)
            else:
                copies[2].wait()
                out[far] = r.part_side[turn].astype(f32)
        return step

    def output_flow(s):
        there = pltpu.make_async_remote_copy(src_ref=hbm.output_blocks.at[1 - side], dst_ref=r.output.at[side], send_sem=part_send.at[6],
            recv_sem=part_recv.at[6], device_id=(me_r, me_s + 2 - 4 * side), device_id_type=MESH)
        if s == 0:
            there.start()
            pltpu.make_async_copy(hbm.output_blocks.at[side], r.output_own, out_sem.at[0]).start()
        else:
            there.wait()
            pltpu.make_async_copy(hbm.output_blocks.at[side], r.output_own, out_sem.at[0]).wait()
            pltpu.make_async_copy(r.output_own, r.output.at[side], out_sem.at[1]).start()

    def vec_copy(k):
        return pltpu.make_async_remote_copy(src_ref=r.vec, dst_ref=r.vec_landed.at[k], send_sem=vec_send.at[k],
            recv_sem=vec_recv.at[k], device_id=red.partners()[k], device_id_type=MESH)

    def vec_flow(s):
        if s >= 1:
            vec_copy(s - 1).wait()
            r.vec[...] += r.vec_landed[s - 1]
        if s <= 4:
            vec_copy(s).start()
        else:
            r.vector_grads[...] = r.vec[...]

    red.flows = {16: part_flow(0, r.memory_grad, lambda b: 0.0), 18: vec_flow, 19: output_flow,
        17: part_flow(1, r.target_grad, lambda b: r.two_grad[place(b)])}

    need(loads.active, loads.branch_grad)
    for c in range(8):
        if c == 4:
            need(loads.two_low, loads.upward_slope, loads.ffn_out)
            upward_gradient()
        ffn_block(c)
        if c == 0:
            pl.semaphore_wait(barrier, 5)
        red.poll()
    need(loads.ffn_in, loads.two_grad)

    @pl.loop(0, tokens // 128)
    def _(i):
        at = pl.ds(mult(i * 128, 128), 128)
        r.two_grad[at] += dot_t(r.upward_slope[at], r.ffn_in[...])
    red.poll()
    need(loads.two_hat, loads.two_rstd, loads.one_hat, loads.one_rstd, loads.cross_output, loads.cross_out, loads.cross_inverse)
    norm_back(r.two_grad, r.two_hat, r.two_rstd, vec[5], vec[1], lambda i: r.one_hat[pl.ds(mult(i * part, part), part)] * vec[3] + vec[4], 0)
    red.poll()
    r.block[8] = sum(dot(r.cross_out[b], r.branch_low[block_at(b)]) for b in range(blocks)).astype(bf16)
    red.poll()
    attention_start(r.cross_output, r.cross_out, r.cross_inverse)
    red.poll()
    need(loads.memory_all, loads.cross_key, loads.cross_value, loads.cross_q)
    keys_again(r.memory_all, r.cross_key, r.cross_value)
    red.poll()
    attention_back(hbm.cross_kept, r.cross_q, (length, length))
    r.block[9] = t_dot(r.memory_all[...], r.key_grad[...]).astype(bf16)
    red.poll()
    r.block[10] = t_dot(r.memory_all[...], r.value_grad[...]).astype(bf16)
    red.poll()
    need(loads.one_low, loads.cross_query)
    r.block[11] = sum(t_dot(r.one_low[block_at(b)], r.query_grad[b]) for b in range(blocks)).astype(bf16)
    red.poll()
    pair_product(r.cross_key, r.cross_value)
    red.poll()
    for b in range(blocks):
        r.two_grad[block_at(b)] += dot_t(r.query_grad[b], r.cross_query[...])
    red.poll()
    need(loads.target_all, loads.self_output, loads.self_out, loads.self_inverse, loads.self_key, loads.self_value, loads.self_q,
        loads.self_query, loads.sums)
    def own_target(i):
        b, inner = i // (span // part), i % (span // part)
        return r.target_all[pl.ds(mult((2 * b + core) * span + inner * part, part), part)].astype(f32)
    norm_back(r.two_grad, r.one_hat, r.one_rstd, vec[3], vec[0], own_target, 3)
    for i in range(3):
        r.vec[pl.ds(i, 1)] = jnp.sum(r.acc[3 + i], axis=0, keepdims=True)
        r.vec[pl.ds(3 + i, 1)] = jnp.sum(r.acc[i], axis=0, keepdims=True)
        r.vec[pl.ds(6 + i, 1)] = jnp.sum(r.sums[i], axis=0, keepdims=True)
    r.vec[pl.ds(9, 7)] = jnp.zeros((7, width), f32)
    red.poll()
    r.block[12] = sum(dot(r.self_out[b], r.branch_low[block_at(b)]) for b in range(blocks)).astype(bf16)
    red.poll()
    attention_start(r.self_output, r.self_out, r.self_inverse)
    red.poll()
    keys_again(r.target_all, r.self_key, r.self_value)
    red.poll()
    attention_back(hbm.self_kept, r.self_q, (length // 2, length))
    r.block[13] = t_dot(r.target_all[...], r.key_grad[...]).astype(bf16)
    red.poll()
    r.block[14] = t_dot(r.target_all[...], r.value_grad[...]).astype(bf16)
    red.poll()
    r.block[15] = sum(t_dot(r.target_all[place(2 * b + core)], r.query_grad[b]) for b in range(blocks)).astype(bf16)
    red.poll()
    pair_product(r.self_key, r.self_value)
    for b in range(blocks):
        r.two_grad[block_at(b)] += dot_t(r.query_grad[b], r.self_query[...])
    red.poll()
    red.poll()
    pltpu.make_async_copy(r.output_own, r.output.at[side], out_sem.at[1]).wait()

def backward_call(o, matrices, vectors, heads=8):
    length, width = o.target_all.shape
    tokens, hidden = o.active.shape
    blocks = o.self_kept.shape[0]
    span = tokens // blocks
    any_, vm = pl.BlockSpec(memory_space=pl.ANY), pl.BlockSpec(memory_space=pltpu.VMEM)
    s = jax.ShapeDtypeStruct
    operands = dict(o._asdict(), **dict(zip(MATRICES + VECTORS, matrices + vectors)))
    count = 8 + 2 * hidden // 512
    outs = BackOut(output=s((blocks, span, width), bf16), reduced=s((count, 512, width), bf16), target_grad=s((blocks, span, width), f32),
        memory_grad=s((blocks, span, width), f32), vector_grads=s((16, width), f32))
    full, near, block = ((length, width), bf16), ((blocks, span, width), bf16), ((blocks, width, span), bf16)
    scratch = BackScratch(block=((count, 512, width), bf16), near=((count, 256, width), bf16), landed=((count, 256, width), bf16),
        key_t=((width, length), bf16), value=full, key_grad=full, value_grad=full,
        score_grad=((8, length, span), bf16), kept=((12, length, span), bf16), part=((length // span, span, width), bf16),
        part_core=((2, 2, span, width), bf16), part_side=((2, span, width), bf16),
        query_grad_t=block, query_grad=near, branch_low=((tokens, width), bf16),
        out_grad_t=block, out_grad=near, delta=((blocks, heads, 8, span), f32),
        vec=((16, width), f32), vec_landed=((5, 16, width), f32), acc=((6, 8, width), f32), output_own=((span, width), bf16))
    dma = pltpu.SemaphoreType.DMA
    return BackOut(*pl.pallas_call(
        functools.partial(backward_kernel, heads),
        out_shape=list(outs),
        in_specs=[vm if k in VECTORS else any_ for k in LOADS + UNLOADED],
        out_specs=[any_, any_, vm, vm, vm],
        scratch_shapes=[pltpu.VMEM(operands[k].shape, operands[k].dtype) for k in LOADS] + [pltpu.VMEM(*k) for k in scratch]
            + [dma((len(LOADS),)), dma((12,)), dma((count,)), dma((count, 10)), dma((count,)), dma((7,)), dma((7,)), dma((5,)), dma((5,)), dma((2,))],
        compiler_params=pltpu.CompilerParams(collective_id=1, has_side_effects=True, vmem_limit_bytes=63 << 20),
        name="backward",
    )(*(operands[k] for k in LOADS + UNLOADED)))

FINISH_BLOCK = (15, 13, 14, 12, 11, 9, 10, 8)
VECTOR_PLACE = (0, 3, 6, 1, 2, 4, 5, 7, 8)

def finish_kernel(reduced, vector_grads, output, target_grad, memory_grad, *refs):
    outs, small, handed = refs[3:13], refs[13:22], refs[:3]
    low, vec, stage, *between, load_sem, store_sem, sem = refs[22:]
    slots, count = stage.shape[0], reduced.shape[0]
    wide = outs[8].shape[1] // 512
    places = [outs[9].at[pl.ds(512 * i, 512)] for i in range(wide)] + [outs[8].at[:, pl.ds(512 * i, 512)] for i in range(wide)]
    places += [None] * 8
    for out, block in zip(outs, FINISH_BLOCK):
        places[block] = out
    loads = [pltpu.make_async_copy(reduced.at[i], low.at[i], load_sem.at[i]) for i in range(count)]
    ahead = 4
    for copy in loads[:ahead]:
        copy.start()
    arrive = [pltpu.make_async_copy(a, b, sem.at[i]) for i, (a, b) in enumerate(zip((output, target_grad, memory_grad, vector_grads), (*between, vec)))]
    leave = [pltpu.make_async_copy(a, b, sem.at[4 + i]) for i, (a, b) in enumerate(zip(between, handed))]
    for copy in arrive:
        copy.start()
    copies = [pltpu.make_async_copy(stage.at[i % slots], place, store_sem.at[i % slots]) for i, place in enumerate(places)]
    for i, copy in enumerate(copies):
        if i >= slots:
            copies[i - slots].wait()
        if i + ahead < count:
            loads[i + ahead].start()
        loads[i].wait()
        stage[i % slots] = low[i].astype(f32)
        copy.start()
    for copy in arrive:
        copy.wait()
    for copy in leave:
        copy.start()
    for ref, row in zip(small, VECTOR_PLACE):
        ref[...] = vec[row]
    for copy in copies[-slots:] + leave:
        copy.wait()

def finish_call(back, hidden):
    count, rows, width = back.reduced.shape
    any_, vm = pl.BlockSpec(memory_space=pl.ANY), pl.BlockSpec(memory_space=pltpu.VMEM)
    s = jax.ShapeDtypeStruct
    handed = [back.output, back.target_grad, back.memory_grad]
    shapes = [s(a.shape, a.dtype) for a in handed] + [s((width, width), f32)] * 8 + [s((width, hidden), f32), s((hidden, width), f32)]
    dma = pltpu.SemaphoreType.DMA
    return pl.pallas_call(
        finish_kernel,
        out_shape=shapes + [s((width,), f32)] * 9,
        in_specs=[any_] * 5,
        out_specs=[any_] * 13 + [vm] * 9,
        scratch_shapes=[pltpu.VMEM(back.reduced.shape, bf16), pltpu.VMEM((16, width), f32), pltpu.VMEM((8, rows, width), f32)]
            + [pltpu.VMEM(a.shape, a.dtype) for a in handed] + [dma((count,)), dma((8,)), dma((7,))],
        compiler_params=pltpu.CompilerParams(vmem_limit_bytes=62 << 20),
        name="finish",
    )(back.reduced, back.vector_grads, *handed)


def per_device(*args):
    rows, span, width = args[0].shape
    hidden = args[12].shape[1]
    fits = lax.axis_size("rows") == 8 and lax.axis_size("seq") == 4
    if not fits or (rows, span, width, hidden) != (2, 256, 512, 2048) or args[1].shape != args[0].shape:
        return ring_device(*args)
    matrices, vectors = args[4:14], args[14:23]
    kept = forward_call(args[0], args[1], args[2], args[3], matrices, vectors, args[23], HEADS)
    back = backward_call(kept, matrices, vectors, HEADS)
    return tuple(finish_call(back, hidden))


def solution(mesh):
    placed = (
        P("rows", "seq", None),
        P("rows", "seq", None),
        P("rows", None),
        P("rows", None),
        P(),
        P(),
        P(),
        P(),
        P(),
        P(),
        P(),
        P(),
        P(),
        P(),
        P(),
        P(),
        P(),
        P(),
        P(),
        P(),
        P(),
        P(),
        P(),
        P("rows", "seq", None),
    )
    return jax.shard_map(
        per_device,
        mesh=mesh,
        in_specs=placed,
        out_specs=(
            P("rows", "seq", None),
            P("rows", "seq", None),
            P("rows", "seq", None),
            P(),
            P(),
            P(),
            P(),
            P(),
            P(),
            P(),
            P(),
            P(),
            P(),
            P(),
            P(),
            P(),
            P(),
            P(),
            P(),
            P(),
            P(),
            P(),
        ),
        check_vma=False,
    )
```
